32 devices in a mesh: batch: 8 (over z, core), proto: 4 (over y, x).
Axes of the slice: x: 2, y: 2, z: 4, core: 2. Of those that a mesh axis runs over, the one named last changes fastest.
Arguments:
- slow_embed: bfloat16 [8192, 256], P('batch'), may hold values from -1 to 1
- fast_embed: bfloat16 [8192, 256], P('batch'), may hold values from -1 to 1
- prototypes: float32 [8192, 256], P('proto'), may hold values from -1 to 1
Outputs:
- proto_grad: float32 [8192, 256], P('proto')
- slow_grad: float32 [8192, 256], P('batch')
- fast_grad: float32 [8192, 256], P('batch')
The draws below stay inside these ranges and needn't reach their ends.
All inputs are finite; a program needn't handle non-finite values.
Results may differ from the reference program's by a relative error of at most 0.0005.
The reference program's roundings to bfloat16 on the way count: a program that leaves them out, or rounds other values in their place, can miss the bound.
Values sent between devices are 32-bit elements; how exact they have to be, the bound alone decides.
No kernel may reach another device: no remote copies, remote signals or barrier semaphores. Data moves between devices by JAX's collectives and lax.ppermute only.
A program may use at most 128 MiB of HBM per device.

```python
import jax
import jax.numpy as jnp
from jax import lax

D = 256
PROTO_DEV = 2048
ITERS = 3
CLIPS = 8192
PROTOS = 8192


def row_scales(scale_key, count):
    position = jnp.arange(count, dtype=jnp.float32)[:, None] / count
    jitter = jax.random.uniform(scale_key, (count, 1), jnp.float32, 0.0, jnp.log(4.0))
    return jnp.exp(jnp.log(3.0) * position + jitter)


def view_draw(key, salt):
    common_key = jax.random.fold_in(key, 21)
    own_key = jax.random.fold_in(key, salt)
    first_key, second_key = jax.random.split(own_key, 2)
    scaling = row_scales(second_key, CLIPS)
    shared_part = jnp.clip(jax.random.normal(common_key, (CLIPS, D), jnp.float32), -5.0, 5.0)
    own_part = jnp.clip(jax.random.normal(first_key, (CLIPS, D), jnp.float32), -5.0, 5.0)
    mixed = 0.7 * shared_part + 0.7 * own_part
    return jnp.clip(0.01 * mixed * scaling, -1.0, 1.0).astype(jnp.bfloat16)


def draw_slow_embed(key, part):
    return view_draw(key, 31)


def draw_fast_embed(key, part):
    return view_draw(key, 41)


def draw_prototypes(key, part):
    own_key = jax.random.fold_in(key, 51)
    first_key, second_key = jax.random.split(own_key, 2)
    scaling = row_scales(second_key, PROTOS)
    mixed = jnp.clip(jax.random.normal(first_key, (PROTOS, D), jnp.float32), -5.0, 5.0)
    return jnp.clip(0.01 * mixed * scaling, -1.0, 1.0).astype(jnp.float32)


def setup_inputs(seed: int = 0) -> dict:
    splits = jax.random.split(jax.random.key(seed), 4)
    return {
        "slow_embed": draw_slow_embed(jax.random.fold_in(splits[3], 71), 0),
        "fast_embed": draw_fast_embed(jax.random.fold_in(splits[3], 71), 0),
        "prototypes": draw_prototypes(jax.random.fold_in(splits[3], 71), 0),
    }


CODE_EPS = 0.05
TEMPER = 0.1
NORM_EPS = 1e-06
HIGH = lax.Precision.HIGHEST

def normalize(raw_rows):
    lengths = jnp.sqrt(lax.optimization_barrier(jnp.sum(raw_rows * raw_rows, axis=-1, keepdims=True)) + 1e-12)
    return (raw_rows / lengths, lengths)

def project_back(grad_unit, unit_vec, lengths):
    along = lax.optimization_barrier(jnp.sum(unit_vec * grad_unit, axis=-1, keepdims=True))
    return (grad_unit - unit_vec * along) / lengths

def reference(slow_embed, fast_embed, prototypes):
    raw_views = jnp.stack([slow_embed, fast_embed]).astype(jnp.float32)
    unit_vec, lengths = normalize(raw_views)
    unit_b = lax.optimization_barrier(unit_vec.astype(jnp.bfloat16)).astype(jnp.float32)
    proto_unit, proto_len = normalize(prototypes.astype(jnp.float32))
    proto_b = lax.optimization_barrier(proto_unit.astype(jnp.bfloat16)).astype(jnp.float32)
    blocks = proto_b.reshape(PROTOS // PROTO_DEV, PROTO_DEV, D)

    def score_of(block):
        return jnp.einsum('vbd,kd->vbk', unit_b, block, precision=HIGH)

    def sweep_all(clip_scale, with_denom):

        def advance(running, block):
            clip_total, denominator = running
            score_blk = score_of(block)
            code_table = jnp.exp(score_blk / CODE_EPS)
            col_total = lax.optimization_barrier(jnp.sum(code_table * clip_scale[:, :, None], axis=1))
            proto_scale = 1.0 / (PROTOS * col_total)
            clip_total = clip_total + lax.optimization_barrier(jnp.sum(code_table * proto_scale[:, None, :], axis=2))
            if with_denom:
                denominator = denominator + lax.optimization_barrier(jnp.sum(jnp.exp(score_blk / TEMPER), axis=2))
            return ((clip_total, denominator), proto_scale)
        initial = (jnp.zeros((2, CLIPS), jnp.float32), jnp.zeros((2, CLIPS), jnp.float32))
        (clip_total, denominator), scales = lax.scan(advance, initial, blocks)
        return (clip_total, denominator, scales)
    clip_scale = jnp.ones((2, CLIPS), jnp.float32)
    denominator = jnp.zeros((2, CLIPS), jnp.float32)
    for iteration in range(ITERS):
        clip_total, denom_now, scales = sweep_all(clip_scale, iteration == 0)
        if iteration == 0:
            denominator = denom_now
        clip_scale = 1.0 / (CLIPS * clip_total)

    def grad_step(accum_grad, inputs):
        block, proto_scale = inputs
        score_blk = score_of(block)
        codes = jnp.exp(score_blk / CODE_EPS) * proto_scale[:, None, :] / clip_total[:, :, None]
        probs = jnp.exp(score_blk / TEMPER) / denominator[:, :, None]
        score_grad = jnp.stack([probs[0] - codes[1], probs[1] - codes[0]]) / TEMPER
        grad_b = lax.optimization_barrier(score_grad.astype(jnp.bfloat16)).astype(jnp.float32)
        accum_grad = accum_grad + jnp.einsum('vbk,kd->vbd', grad_b, block, precision=HIGH)
        proto_blk = jnp.einsum('vbk,vbd->kd', grad_b, unit_b, precision=HIGH)
        return (accum_grad, proto_blk)
    grad_unit, proto_blocks = lax.scan(grad_step, jnp.zeros((2, CLIPS, D), jnp.float32), (blocks, scales))
    grad_proto_unit = proto_blocks.reshape(PROTOS, D)
    grad_embed = project_back(grad_unit, unit_vec, lengths)
    grad_proto = project_back(grad_proto_unit, proto_unit, proto_len)
    proto_grad = grad_proto / jnp.sqrt(jnp.mean(grad_proto * grad_proto) + NORM_EPS)
    embed_factor = 1.0 / jnp.sqrt(jnp.mean(grad_embed * grad_embed) + NORM_EPS)
    return (proto_grad, grad_embed[0] * embed_factor, grad_embed[1] * embed_factor)
```

```python
import functools

import jax
import jax.numpy as jnp
from jax import lax
from jax.experimental import pallas as pl
from jax.experimental.pallas import tpu as pltpu
from jax.sharding import PartitionSpec as P

ITERS = 3


CODE_EPS = 0.05
TEMPER = 0.1
NORM_EPS = 1e-06
LANES = 128
MIB = 1024 * 1024


def vmem_spec():
    return pl.BlockSpec(memory_space=pltpu.VMEM)


def params(limit):
    return pltpu.CompilerParams(vmem_limit_bytes=limit * MIB)


def to_columns(line):
    return jnp.broadcast_to(line, (LANES, LANES)).T


def to_line(partial):
    return jnp.sum(partial.T, axis=0, keepdims=True)


def lane_sum(block):
    total = block[:, :LANES]
    for j in range(1, block.shape[1] // LANES):
        total = total + block[:, j * LANES : (j + 1) * LANES]
    return total


def row_fold(block):
    return jnp.sum(block.reshape(block.shape[0] // 8, 8, block.shape[1]), axis=0)


def score_kernel(slow, fast, protos, t_ref, col_ref, den_ref, ub_ref, ubt_ref, cb_ref, den_s):
    clips, feats = slow.shape
    count = protos.shape[0]
    for v, src in enumerate((slow, fast)):
        for first in range(0, clips, 256):
            rows = pl.ds(first, 256)
            x = src[rows, :].astype(jnp.float32)
            length = jnp.sqrt(jnp.sum(x * x, axis=-1, keepdims=True) + 1e-12)
            u = x / length
            ub_ref[v, rows, :] = u.astype(jnp.bfloat16)
            ubt_ref[v, :, rows] = u.T.astype(jnp.bfloat16)

    def proto_rows(i, _):
        rows = pl.ds(pl.multiple_of(i * 256, 256), 256)
        w = protos[rows, :]
        length = jnp.sqrt(jnp.sum(w * w, axis=-1, keepdims=True) + 1e-12)
        cb_ref[rows, :] = (w / length).astype(jnp.bfloat16)
        return 0

    lax.fori_loop(0, count // 256, proto_rows, 0)
    den_s[...] = jnp.zeros_like(den_s)

    def chunk(j, _):
        first = pl.multiple_of(j * 256, 256)
        weights = cb_ref[pl.ds(first, 256), :]
        for v in range(2):
            cols = jnp.zeros((8, 256), jnp.float32)
            for r in range(0, clips, LANES):
                rows = pl.ds(r, LANES)
                s = lax.dot_general(
                    ub_ref[v, rows, :],
                    weights,
                    (((1,), (1,)), ((), ())),
                    preferred_element_type=jnp.float32,
                )
                t = jnp.exp(s * (1.0 / TEMPER))
                t_ref[v, rows, pl.ds(first, 256)] = t
                cols = cols + row_fold(t * t)
                den_s[v, rows, :] += lane_sum(t)
            line = jnp.sum(cols, axis=0, keepdims=True)
            for h in range(2):
                col_ref[pl.ds(v * (count // LANES) + j * 2 + h, 1), :] = line[
                    :, h * LANES : (h + 1) * LANES
                ]
        return 0

    lax.fori_loop(0, count // 256, chunk, 0)
    groups = clips // LANES
    for v in range(2):
        for i in range(groups):
            den_ref[pl.ds(v * groups + i, 1), :] = to_line(den_s[v, i * LANES : (i + 1) * LANES, :])


def scores(slow, fast, protos):
    clips, feats = slow.shape
    count = protos.shape[0]
    return pl.pallas_call(
        score_kernel,
        out_shape=(
            pltpu.VMEM((2, clips, count), jnp.float32),
            jax.ShapeDtypeStruct((2 * count // LANES, LANES), jnp.float32),
            jax.ShapeDtypeStruct((2 * clips // LANES, LANES), jnp.float32),
            jax.ShapeDtypeStruct((2, clips, feats), jnp.bfloat16),
            jax.ShapeDtypeStruct((2, feats, clips), jnp.bfloat16),
            jax.ShapeDtypeStruct((count, feats), jnp.bfloat16),
        ),
        in_specs=[vmem_spec()] * 3,
        out_specs=(vmem_spec(),) * 6,
        scratch_shapes=[pltpu.VMEM((2, clips, LANES), jnp.float32)],
        compiler_params=params(40),
        name="scores",
    )(slow, fast, protos)


def row_kernel(protos_all, extra, parts, *refs):
    t_ref, den_ref = refs[0], refs[1]
    col_parts = refs[2 : 2 + parts]
    row_ref, r_ref = refs[2 + parts :]
    clips, count = t_ref.shape[1:]
    groups, lines = clips // LANES, count // LANES
    total = col_parts[0][...]
    for part in col_parts[1:]:
        total = total + part[...]
    r_ref[...] = 1.0 / (float(protos_all) * total)
    if extra:
        row_ref[2 * groups :, :] = den_ref[...]
    for v in range(2):

        def step(i, _, v=v):
            rows = pl.ds(pl.multiple_of(i * LANES, LANES), LANES)
            acc = jnp.zeros((LANES, LANES), jnp.float32)
            for j in range(lines):
                t = t_ref[v, rows, j * LANES : (j + 1) * LANES]
                acc = acc + t * t * r_ref[v * lines + j : v * lines + j + 1, :]
            row_ref[pl.ds(v * groups + i, 1), :] = to_line(acc)
            return 0

        lax.fori_loop(0, groups, step, 0)


def row_pass(t, den, col_parts, protos_all, extra):
    clips, count = t.shape[1:]
    lines = 2 * clips // LANES
    return pl.pallas_call(
        functools.partial(row_kernel, protos_all, extra, len(col_parts)),
        out_shape=(
            jax.ShapeDtypeStruct((lines * (2 if extra else 1), LANES), jnp.float32),
            jax.ShapeDtypeStruct((2 * count // LANES, LANES), jnp.float32),
        ),
        in_specs=[vmem_spec()] * (2 + len(col_parts)),
        out_specs=(vmem_spec(),) * 2,
        compiler_params=params(16),
        name="row_pass",
    )(pltpu.with_memory_space_constraint(t, pltpu.VMEM), den, *col_parts)


def col_kernel(clips_all, parts, *refs):
    t_ref = refs[0]
    row_parts = refs[1 : 1 + parts]
    col_ref, acc_s, s_s = refs[1 + parts :]
    clips, count = t_ref.shape[1:]
    groups, lines = clips // LANES, count // LANES
    total = row_parts[0][: 2 * groups, :]
    for part in row_parts[1:]:
        total = total + part[: 2 * groups, :]
    s_s[...] = 1.0 / (float(clips_all) * total)
    acc_s[...] = jnp.zeros_like(acc_s)
    for v in range(2):

        def step(i, _, v=v):
            rows = pl.ds(pl.multiple_of(i * LANES, LANES), LANES)
            scale = to_columns(s_s[pl.ds(v * groups + i, 1), :])
            for j in range(lines):
                span = slice(j * LANES, (j + 1) * LANES)
                t = t_ref[v, rows, span]
                acc_s[v, :, span] += row_fold(t * t * scale)
            return 0

        lax.fori_loop(0, groups, step, 0)
        for j in range(lines):
            col_ref[v * lines + j : v * lines + j + 1, :] = jnp.sum(
                acc_s[v, :, j * LANES : (j + 1) * LANES], axis=0, keepdims=True
            )


def col_pass(t, row_parts, clips_all):
    clips, count = t.shape[1:]
    return pl.pallas_call(
        functools.partial(col_kernel, clips_all, len(row_parts)),
        out_shape=jax.ShapeDtypeStruct((2 * count // LANES, LANES), jnp.float32),
        in_specs=[vmem_spec()] * (1 + len(row_parts)),
        out_specs=vmem_spec(),
        scratch_shapes=[
            pltpu.VMEM((2, 8, count), jnp.float32),
            pltpu.VMEM((2 * clips // LANES, LANES), jnp.float32),
        ],
        compiler_params=params(16),
        name="col_pass",
    )(pltpu.with_memory_space_constraint(t, pltpu.VMEM), *row_parts)


def grad_kernel(parts, *refs):
    t_ref, r_ref, ubt_ref, cb_ref = refs[:4]
    row_parts = refs[4 : 4 + parts]
    den_parts = refs[4 + parts : 4 + 2 * parts]
    dc_ref, du_ref, g_s, code_s, prob_s = refs[4 + 2 * parts :]
    clips, count = t_ref.shape[1:]
    groups, lines = clips // LANES, count // LANES
    total = row_parts[0][...]
    for part in row_parts[1:]:
        total = total + part[...]
    code = (1.0 / TEMPER) / total
    total = den_parts[0][2 * groups :, :]
    for part in den_parts[1:]:
        total = total + part[2 * groups :, :]
    prob = (1.0 / TEMPER) / total
    for v in range(2):
        for i in range(groups):
            line = v * groups + i
            rows = slice(i * LANES, (i + 1) * LANES)
            code_s[v, rows, :] = to_columns(code[line : line + 1, :])
            prob_s[v, rows, :] = to_columns(prob[line : line + 1, :])

    def chunk(j, _):
        first = pl.multiple_of(j * 256, 256)
        for h in range(2):
            span = pl.ds(first + h * LANES, LANES)
            scale = [r_ref[pl.ds(v * lines + j * 2 + h, 1), :] for v in range(2)]
            for i in range(groups):
                rows = slice(i * LANES, (i + 1) * LANES)
                t = [t_ref[v, rows, span] for v in range(2)]
                q = [t[v] * t[v] * scale[v] * code_s[v, rows, :] for v in range(2)]
                for v in range(2):
                    g = t[v] * prob_s[v, rows, :] - q[1 - v]
                    g_s[v, rows, span] = g.astype(jnp.bfloat16)
        cols = pl.ds(first, 256)
        dct = jnp.dot(ubt_ref[0], g_s[0, :, cols], preferred_element_type=jnp.float32)
        dct = dct + jnp.dot(ubt_ref[1], g_s[1, :, cols], preferred_element_type=jnp.float32)
        dc_ref[cols, :] = dct.T
        return 0

    lax.fori_loop(0, count // 256, chunk, 0)
    for v in range(2):

        def rows_step(i, _, v=v):
            rows = pl.ds(pl.multiple_of(i * 256, 256), 256)
            du_ref[rows, v * cb_ref.shape[1] : (v + 1) * cb_ref.shape[1]] = jnp.dot(
                g_s[v, rows, :], cb_ref[...], preferred_element_type=jnp.float32
            )
            return 0

        lax.fori_loop(0, clips // 256, rows_step, 0)


def gradients(t, r, ubt, cb, row_parts, den_parts):
    clips, count = t.shape[1:]
    feats = cb.shape[1]
    return pl.pallas_call(
        functools.partial(grad_kernel, len(row_parts)),
        out_shape=(
            jax.ShapeDtypeStruct((count, feats), jnp.float32),
            jax.ShapeDtypeStruct((clips, 2 * feats), jnp.float32),
        ),
        in_specs=[vmem_spec()] * (4 + 2 * len(row_parts)),
        out_specs=(vmem_spec(),) * 2,
        scratch_shapes=[
            pltpu.VMEM((2, clips, count), jnp.bfloat16),
            pltpu.VMEM((2, clips, LANES), jnp.float32),
            pltpu.VMEM((2, clips, LANES), jnp.float32),
        ],
        compiler_params=params(40),
        name="gradients",
    )(
        pltpu.with_memory_space_constraint(t, pltpu.VMEM), r, ubt, cb, *row_parts, *den_parts
    )


def all_parts(own, axis):
    count = lax.axis_size(axis)
    parts = [own]
    for shift in range(1, count):
        parts.append(lax.ppermute(own, axis, [(i, (i + shift) % count) for i in range(count)]))
    return parts


def normalize(raw_rows):
    lengths = jnp.sqrt(jnp.sum(raw_rows * raw_rows, axis=-1, keepdims=True) + 1e-12)
    return (raw_rows / lengths, lengths)


def project_back(grad_unit, unit_vec, lengths):
    along = jnp.sum(unit_vec * grad_unit, axis=-1, keepdims=True)
    return (grad_unit - unit_vec * along) / lengths


def body(slow_embed, fast_embed, prototypes):
    clip_dev, feat_width = slow_embed.shape
    proto_dev = prototypes.shape[0]
    batch_count = lax.axis_size("batch")
    proto_count = lax.axis_size("proto")
    clips_all = clip_dev * batch_count
    protos_all = proto_dev * proto_count
    proto_entries = float(protos_all * feat_width)
    embed_entries = float(2 * clips_all * feat_width)

    t, col, den, unit_b, unit_bt, proto_b = scores(slow_embed, fast_embed, prototypes)
    for iteration in range(ITERS):
        rows, r = row_pass(t, den, all_parts(col, "batch"), protos_all, iteration == 0)
        row_parts = all_parts(rows, "proto")
        if iteration == 0:
            den_parts = row_parts
        if iteration + 1 < ITERS:
            col = col_pass(t, row_parts, clips_all)
    dc, du = gradients(t, r, unit_bt, proto_b, row_parts, den_parts)

    proto_rows = proto_dev // batch_count
    clip_rows = clip_dev // proto_count
    dc_share = lax.psum_scatter(dc, "batch", scatter_dimension=0, tiled=True)
    du_share = lax.psum_scatter(du, "proto", scatter_dimension=0, tiled=True)
    proto_first = lax.axis_index("batch") * proto_rows
    unit_share, len_share = normalize(
        lax.dynamic_slice_in_dim(prototypes, proto_first, proto_rows, 0)
    )
    grad_proto = project_back(dc_share, unit_share, len_share)
    clip_first = lax.axis_index("proto") * clip_rows
    views = [
        lax.dynamic_slice_in_dim(x, clip_first, clip_rows, 0).astype(jnp.float32)
        for x in (slow_embed, fast_embed)
    ]
    grad_embed = []
    for v in range(2):
        unit, length = normalize(views[v])
        grad_embed.append(
            project_back(du_share[:, v * feat_width : (v + 1) * feat_width], unit, length)
        )
    grad_embed = jnp.concatenate(grad_embed, axis=1)
    proto_all = lax.all_gather(grad_proto, "batch", axis=0, tiled=True)
    embed_all = lax.all_gather(grad_embed, "proto", axis=0, tiled=True)
    proto_square = jnp.sum(grad_proto * grad_proto)
    embed_square = jnp.sum(grad_embed * grad_embed)
    totals = lax.psum((proto_square, embed_square), ("batch", "proto"))
    proto_factor = lax.rsqrt(totals[0] / proto_entries + NORM_EPS)
    embed_factor = lax.rsqrt(totals[1] / embed_entries + NORM_EPS)
    return (
        proto_all * proto_factor,
        embed_all[:, :feat_width] * embed_factor,
        embed_all[:, feat_width:] * embed_factor,
    )


def solution(mesh):
    placed = (P("batch", None), P("batch", None), P("proto", None))
    return jax.shard_map(
        body,
        mesh=mesh,
        in_specs=placed,
        out_specs=(P("proto", None), P("batch", None), P("batch", None)),
        check_vma=False,
    )
```

```python
import functools

import jax
import jax.numpy as jnp
from jax import lax
from jax.experimental import pallas as pl
from jax.experimental.pallas import tpu as pltpu
from jax.sharding import PartitionSpec as P

ITERS = 3


CODE_EPS = 0.05
TEMPER = 0.1
NORM_EPS = 1e-06
LANES = 128
MIB = 1024 * 1024


def vmem_spec():
    return pl.BlockSpec(memory_space=pltpu.VMEM)


def params(limit):
    return pltpu.CompilerParams(vmem_limit_bytes=limit * MIB)


def to_columns(line):
    return jnp.broadcast_to(line, (LANES, LANES)).T


def to_line(partial):
    return jnp.sum(partial.T, axis=0, keepdims=True)


def lane_sum(block):
    total = block[:, :LANES]
    for j in range(1, block.shape[1] // LANES):
        total = total + block[:, j * LANES : (j + 1) * LANES]
    return total


def row_fold(block):
    return jnp.sum(block.reshape(block.shape[0] // 8, 8, block.shape[1]), axis=0)


def score_kernel(slow, fast, protos, t_ref, col_ref, den_ref, ub_ref, ubt_ref, cb_ref, den_s):
    clips, feats = slow.shape
    count = protos.shape[0]
    for v, src in enumerate((slow, fast)):
        for first in range(0, clips, 256):
            rows = pl.ds(first, 256)
            x = src[rows, :].astype(jnp.float32)
            length = jnp.sqrt(jnp.sum(x * x, axis=-1, keepdims=True) + 1e-12)
            u = x / length
            ub_ref[v, rows, :] = u.astype(jnp.bfloat16)
            ubt_ref[v, :, rows] = u.T.astype(jnp.bfloat16)

    def proto_rows(i, _):
        rows = pl.ds(pl.multiple_of(i * 256, 256), 256)
        w = protos[rows, :]
        length = jnp.sqrt(jnp.sum(w * w, axis=-1, keepdims=True) + 1e-12)
        cb_ref[rows, :] = (w / length).astype(jnp.bfloat16)
        return 0

    lax.fori_loop(0, count // 256, proto_rows, 0)
    den_s[...] = jnp.zeros_like(den_s)

    def chunk(j, _):
        first = pl.multiple_of(j * 256, 256)
        weights = cb_ref[pl.ds(first, 256), :]
        for v in range(2):
            cols = jnp.zeros((8, 256), jnp.float32)
            for r in range(0, clips, LANES):
                rows = pl.ds(r, LANES)
                s = lax.dot_general(
                    ub_ref[v, rows, :],
                    weights,
                    (((1,), (1,)), ((), ())),
                    preferred_element_type=jnp.float32,
                )
                t = jnp.exp(s * (1.0 / TEMPER))
                t_ref[v, rows, pl.ds(first, 256)] = t
                cols = cols + row_fold(t * t)
                den_s[v, rows, :] += lane_sum(t)
            line = jnp.sum(cols, axis=0, keepdims=True)
            for h in range(2):
                col_ref[pl.ds(v * (count // LANES) + j * 2 + h, 1), :] = line[
                    :, h * LANES : (h + 1) * LANES
                ]
        return 0

    lax.fori_loop(0, count // 256, chunk, 0)
    groups = clips // LANES
    for v in range(2):
        for i in range(groups):
            den_ref[pl.ds(v * groups + i, 1), :] = to_line(den_s[v, i * LANES : (i + 1) * LANES, :])


def scores(slow, fast, protos):
    clips, feats = slow.shape
    count = protos.shape[0]
    return pl.pallas_call(
        score_kernel,
        out_shape=(
            pltpu.VMEM((2, clips, count), jnp.float32),
            jax.ShapeDtypeStruct((2 * count // LANES, LANES), jnp.float32),
            jax.ShapeDtypeStruct((2 * clips // LANES, LANES), jnp.float32),
            jax.ShapeDtypeStruct((2, clips, feats), jnp.bfloat16),
            jax.ShapeDtypeStruct((2, feats, clips), jnp.bfloat16),
            jax.ShapeDtypeStruct((count, feats), jnp.bfloat16),
        ),
        in_specs=[vmem_spec()] * 3,
        out_specs=(vmem_spec(),) * 6,
        scratch_shapes=[pltpu.VMEM((2, clips, LANES), jnp.float32)],
        compiler_params=params(40),
        name="scores",
    )(slow, fast, protos)


def row_kernel(protos_all, extra, parts, *refs):
    t_ref, den_ref = refs[0], refs[1]
    col_parts = refs[2 : 2 + parts]
    row_ref, r_ref = refs[2 + parts :]
    clips, count = t_ref.shape[1:]
    groups, lines = clips // LANES, count // LANES
    total = col_parts[0][...]
    for part in col_parts[1:]:
        total = total + part[...]
    r_ref[...] = 1.0 / (float(protos_all) * total)
    if extra:
        row_ref[2 * groups :, :] = den_ref[...]
    for v in range(2):

        def step(i, _, v=v):
            rows = pl.ds(pl.multiple_of(i * LANES, LANES), LANES)
            acc = jnp.zeros((LANES, LANES), jnp.float32)
            for j in range(lines):
                t = t_ref[v, rows, j * LANES : (j + 1) * LANES]
                acc = acc + t * t * r_ref[v * lines + j : v * lines + j + 1, :]
            row_ref[pl.ds(v * groups + i, 1), :] = to_line(acc)
            return 0

        lax.fori_loop(0, groups, step, 0)


def row_pass(t, den, col_parts, protos_all, extra):
    clips, count = t.shape[1:]
    lines = 2 * clips // LANES
    return pl.pallas_call(
        functools.partial(row_kernel, protos_all, extra, len(col_parts)),
        out_shape=(
            jax.ShapeDtypeStruct((lines * (2 if extra else 1), LANES), jnp.float32),
            jax.ShapeDtypeStruct((2 * count // LANES, LANES), jnp.float32),
        ),
        in_specs=[vmem_spec()] * (2 + len(col_parts)),
        out_specs=(vmem_spec(),) * 2,
        compiler_params=params(16),
        name="row_pass",
    )(pltpu.with_memory_space_constraint(t, pltpu.VMEM), den, *col_parts)


def col_kernel(clips_all, parts, *refs):
    t_ref = refs[0]
    row_parts = refs[1 : 1 + parts]
    col_ref, acc_s, s_s = refs[1 + parts :]
    clips, count = t_ref.shape[1:]
    groups, lines = clips // LANES, count // LANES
    total = row_parts[0][: 2 * groups, :]
    for part in row_parts[1:]:
        total = total + part[: 2 * groups, :]
    s_s[...] = 1.0 / (float(clips_all) * total)
    acc_s[...] = jnp.zeros_like(acc_s)
    for v in range(2):

        def step(i, _, v=v):
            rows = pl.ds(pl.multiple_of(i * LANES, LANES), LANES)
            scale = to_columns(s_s[pl.ds(v * groups + i, 1), :])
            for j in range(lines):
                span = slice(j * LANES, (j + 1) * LANES)
                t = t_ref[v, rows, span]
                acc_s[v, :, span] += row_fold(t * t * scale)
            return 0

        lax.fori_loop(0, groups, step, 0)
        for j in range(lines):
            col_ref[v * lines + j : v * lines + j + 1, :] = jnp.sum(
                acc_s[v, :, j * LANES : (j + 1) * LANES], axis=0, keepdims=True
            )


def col_pass(t, row_parts, clips_all):
    clips, count = t.shape[1:]
    return pl.pallas_call(
        functools.partial(col_kernel, clips_all, len(row_parts)),
        out_shape=jax.ShapeDtypeStruct((2 * count // LANES, LANES), jnp.float32),
        in_specs=[vmem_spec()] * (1 + len(row_parts)),
        out_specs=vmem_spec(),
        scratch_shapes=[
            pltpu.VMEM((2, 8, count), jnp.float32),
            pltpu.VMEM((2 * clips // LANES, LANES), jnp.float32),
        ],
        compiler_params=params(16),
        name="col_pass",
    )(pltpu.with_memory_space_constraint(t, pltpu.VMEM), *row_parts)


def grad_kernel(parts, batch_count, *refs):
    me_ref, t_ref, r_ref, ubt_ref = refs[:4]
    row_parts = refs[4 : 4 + parts]
    den_parts = refs[4 + parts : 4 + 2 * parts]
    send_ref, keep_ref, g_ref, code_s, prob_s = refs[4 + 2 * parts :]
    clips, count = t_ref.shape[1:]
    groups, lines = clips // LANES, count // LANES
    width = count // batch_count
    total = row_parts[0][...]
    for part in row_parts[1:]:
        total = total + part[...]
    code = (1.0 / TEMPER) / total
    total = den_parts[0][2 * groups :, :]
    for part in den_parts[1:]:
        total = total + part[2 * groups :, :]
    prob = (1.0 / TEMPER) / total
    for v in range(2):
        for i in range(groups):
            line = v * groups + i
            rows = slice(i * LANES, (i + 1) * LANES)
            code_s[v, rows, :] = to_columns(code[line : line + 1, :])
            prob_s[v, rows, :] = to_columns(prob[line : line + 1, :])

    def chunk(m, out_ref, slot):
        which = jnp.bitwise_xor(me_ref[0], m)
        first = pl.multiple_of(which * width, width)
        for h in range(width // LANES):
            span = pl.ds(first + h * LANES, LANES)
            line = which * (width // LANES) + h
            scale = [r_ref[pl.ds(v * lines + line, 1), :] for v in range(2)]
            for i in range(groups):
                rows = slice(i * LANES, (i + 1) * LANES)
                t = [t_ref[v, rows, span] for v in range(2)]
                q = [t[v] * t[v] * scale[v] * code_s[v, rows, :] for v in range(2)]
                for v in range(2):
                    g = t[v] * prob_s[v, rows, :] - q[1 - v]
                    g_ref[v, rows, span] = g.astype(jnp.bfloat16)
        cols = pl.ds(first, width)
        dct = jnp.dot(ubt_ref[0], g_ref[0, :, cols], preferred_element_type=jnp.float32)
        dct = dct + jnp.dot(ubt_ref[1], g_ref[1, :, cols], preferred_element_type=jnp.float32)
        out_ref[slot] = dct.T

    def pair(i, _):
        chunk(2 * i + 1, send_ref, i)
        chunk(2 * i, keep_ref, i)
        return 0

    lax.fori_loop(0, batch_count // 2, pair, 0)


def proto_gradients(me, t, r, ubt, row_parts, den_parts, batch_count):
    clips, count = t.shape[1:]
    feats = ubt.shape[1]
    share = jax.ShapeDtypeStruct(
        (batch_count // 2, count // batch_count, feats), jnp.float32
    )
    return pl.pallas_call(
        functools.partial(grad_kernel, len(row_parts), batch_count),
        out_shape=(share, share, pltpu.VMEM((2, clips, count), jnp.bfloat16)),
        in_specs=[pl.BlockSpec(memory_space=pltpu.SMEM)] + [vmem_spec()] * (3 + 2 * len(row_parts)),
        out_specs=(vmem_spec(),) * 3,
        scratch_shapes=[
            pltpu.VMEM((2, clips, LANES), jnp.float32),
            pltpu.VMEM((2, clips, LANES), jnp.float32),
        ],
        compiler_params=params(32),
        cost_estimate=pl.CostEstimate(
            flops=4 * clips * count * feats, bytes_accessed=8 * MIB, transcendentals=0
        ),
        name="proto_gradients",
    )(
        me, pltpu.with_memory_space_constraint(t, pltpu.VMEM), r, ubt, *row_parts, *den_parts
    )


def piece_of(position, order):
    steps = len(order)
    return sum(((position >> (steps - 1 - j)) & 1) << bit for j, bit in enumerate(order))


def embed_grad_kernel(orders, me_ref, g_ref, cb_ref, *outs):
    clips = g_ref.shape[1]
    pieces = 1 << len(orders[0])
    size = clips // pieces
    for v in range(2):
        for place in range(pieces):
            which = jnp.bitwise_xor(me_ref[0], piece_of(place, orders[v]))
            rows = pl.ds(pl.multiple_of(which * size, size), size)
            out_ref = outs[2 * v + (0 if place >= pieces // 2 else 1)]
            out_ref[place % (pieces // 2)] = jnp.dot(
                g_ref[v, rows, :], cb_ref[...], preferred_element_type=jnp.float32
            )


def embed_gradients(me, g, cb, orders):
    clips, count = g.shape[1:]
    feats = cb.shape[1]
    pieces = 1 << len(orders[0])
    share = jax.ShapeDtypeStruct((pieces // 2, clips // pieces, feats), jnp.float32)
    return pl.pallas_call(
        functools.partial(embed_grad_kernel, orders),
        out_shape=(share,) * 4,
        in_specs=[pl.BlockSpec(memory_space=pltpu.SMEM)] + [vmem_spec()] * 2,
        out_specs=(vmem_spec(),) * 4,
        compiler_params=params(24),
        cost_estimate=pl.CostEstimate(
            flops=4 * clips * count * feats, bytes_accessed=8 * MIB, transcendentals=0
        ),
        name="embed_gradients",
    )(me, pltpu.with_memory_space_constraint(g, pltpu.VMEM), cb)


def share_kernel(counts, raw_count, *refs):
    raws = refs[:raw_count]
    terms = refs[raw_count : raw_count + sum(counts)]
    outs = refs[raw_count + sum(counts) :]
    square = jnp.zeros((8, LANES), jnp.float32)
    place = 0
    for n, (raw, count) in enumerate(zip(raws, counts)):
        x = raw[...].astype(jnp.float32)
        length = jnp.sqrt(jnp.sum(x * x, axis=-1, keepdims=True) + 1e-12)
        unit = x / length
        grad = terms[place][...]
        for term in terms[place + 1 : place + count]:
            grad = grad + term[...]
        place += count
        along = jnp.sum(unit * grad, axis=-1, keepdims=True)
        grad = (grad - unit * along) / length
        outs[n][...] = grad
        square = square + row_fold(lane_sum(grad * grad))
    total = jnp.sum(jnp.sum(square, axis=0, keepdims=True), axis=1, keepdims=True)
    outs[-1][...] = jnp.broadcast_to(total, (8, LANES))


def project_shares(raws, groups):
    terms = [term for group in groups for term in group]
    return pl.pallas_call(
        functools.partial(share_kernel, [len(group) for group in groups], len(raws)),
        out_shape=tuple(jax.ShapeDtypeStruct(raw.shape, jnp.float32) for raw in raws)
        + (jax.ShapeDtypeStruct((8, LANES), jnp.float32),),
        in_specs=[vmem_spec()] * (len(raws) + len(terms)),
        out_specs=(vmem_spec(),) * (len(raws) + 1),
        compiler_params=params(8),
        name="project_shares",
    )(*raws, *terms)


def finish_kernel(entries, counts, me_ref, square_ref, *refs):
    ins, outs = refs[: sum(counts)], refs[sum(counts) :]
    place = 0
    for n, count in enumerate(counts):
        mean = square_ref[n, 0:1, 0:1] / entries[n]
        factor = lax.rsqrt(mean + NORM_EPS)
        for m in range(count):
            src = ins[place + m]
            size = src.shape[0]
            which = jnp.bitwise_xor(me_ref[n], m)
            outs[n][pl.ds(pl.multiple_of(which * size, size), size), :] = src[...] * factor
        place += count


def finish(me, squares, groups, entries):
    pieces = [piece for group in groups for piece in group]
    return pl.pallas_call(
        functools.partial(finish_kernel, entries, [len(group) for group in groups]),
        out_shape=tuple(
            jax.ShapeDtypeStruct((len(group) * group[0].shape[0], group[0].shape[1]), jnp.float32)
            for group in groups
        ),
        in_specs=[pl.BlockSpec(memory_space=pltpu.SMEM)] + [vmem_spec()] * (1 + len(pieces)),
        out_specs=(vmem_spec(),) * len(groups),
        compiler_params=params(24),
        name="finish",
    )(me, squares, *pieces)


def all_parts(own, axis):
    count = lax.axis_size(axis)
    parts = [own]
    for shift in range(1, count):
        parts.append(lax.ppermute(own, axis, [(i, (i + shift) % count) for i in range(count)]))
    return parts


def swap(own, axis, bit):
    return lax.ppermute(own, axis, [(i, i ^ (1 << bit)) for i in range(lax.axis_size(axis))])


def bits_of(axis):
    count = lax.axis_size(axis)
    bits = count.bit_length() - 1
    if count != 1 << bits:
        raise ValueError("axis size")
    return bits


def scatter_batch(send, keep):
    bits = bits_of("batch")
    recv = swap(send, "batch", 0)
    pieces = {m: [keep[m], recv[m]] for m in range(1 << (bits - 1))}
    for bit in range(bits - 1):
        for m in sorted((m for m in pieces if m >> bit & 1), reverse=True):
            terms = pieces.pop(m)
            total = terms[0]
            for term in terms[1:]:
                total = total + term
            pieces[m ^ (1 << bit)].append(swap(total, "batch", bit + 1))
    return pieces[0]


def scatter_proto(send, keep, order):
    for bit in order[:-1]:
        recv = swap(send, "proto", bit)
        half = keep.shape[0] // 2
        send = keep[half:] + recv[half:]
        keep = keep[:half] + recv[:half]
    return [keep[0], swap(send, "proto", order[-1])[0]]


def gather_bits(own, axis, order):
    pieces = {0: own}
    for bit in order:
        for m in list(pieces):
            pieces[m | 1 << bit] = swap(pieces[m], axis, bit)
    return [pieces[m] for m in range(len(pieces))]


def body(slow_embed, fast_embed, prototypes):
    clip_dev, feat_width = slow_embed.shape
    proto_dev = prototypes.shape[0]
    batch_count = lax.axis_size("batch")
    proto_count = lax.axis_size("proto")
    clips_all = clip_dev * batch_count
    protos_all = proto_dev * proto_count
    proto_entries = float(protos_all * feat_width)
    embed_entries = float(2 * clips_all * feat_width)
    batch_bits, proto_bits = bits_of("batch"), bits_of("proto")
    me_batch, me_proto = lax.axis_index("batch"), lax.axis_index("proto")
    me = jnp.stack([me_batch, me_proto, me_proto]).astype(jnp.int32)
    me_first = me[:1]
    me_second = me[1:2]

    t, col, den, unit_b, unit_bt, proto_b = scores(slow_embed, fast_embed, prototypes)
    for iteration in range(ITERS):
        rows, r = row_pass(t, den, all_parts(col, "batch"), protos_all, iteration == 0)
        row_parts = all_parts(rows, "proto")
        if iteration == 0:
            den_parts = row_parts
        if iteration + 1 < ITERS:
            col = col_pass(t, row_parts, clips_all)

    orders = (tuple(range(proto_bits)), tuple(reversed(range(proto_bits))))
    send, keep, g = proto_gradients(
        me_first, t, r, unit_bt, row_parts, den_parts, batch_count
    )
    sends = embed_gradients(me_second, g, proto_b, orders)

    proto_rows = proto_dev // batch_count
    clip_rows = clip_dev // proto_count
    raw_protos = lax.dynamic_slice_in_dim(prototypes, me_batch * proto_rows, proto_rows, 0)
    raw_views = [
        lax.dynamic_slice_in_dim(x, me_proto * clip_rows, clip_rows, 0)
        for x in (slow_embed, fast_embed)
    ]
    proto_terms = scatter_batch(send, keep)
    view_terms = [scatter_proto(sends[2 * v], sends[2 * v + 1], orders[v]) for v in range(2)]
    grad_proto, proto_square = project_shares([raw_protos], [proto_terms])
    grad_slow, grad_fast, embed_square = project_shares(raw_views, view_terms)

    proto_pieces = gather_bits(grad_proto, "batch", tuple(reversed(range(batch_bits))))
    slow_pieces = gather_bits(grad_slow, "proto", orders[1])
    fast_pieces = gather_bits(grad_fast, "proto", orders[0])
    squares = jnp.stack([proto_square, embed_square, embed_square])
    for bit in range(proto_bits):
        squares = squares + swap(squares, "proto", bit)
    for bit in range(batch_bits):
        squares = squares + swap(squares, "batch", bit)
    return finish(
        me,
        squares,
        (proto_pieces, slow_pieces, fast_pieces),
        (proto_entries, embed_entries, embed_entries),
    )


def solution(mesh):
    placed = (P("batch", None), P("batch", None), P("proto", None))
    return jax.shard_map(
        body,
        mesh=mesh,
        in_specs=placed,
        out_specs=(P("proto", None), P("batch", None), P("batch", None)),
        check_vma=False,
    )
```

```python
import functools

import jax
import jax.numpy as jnp
from jax import lax
from jax.experimental import pallas as pl
from jax.experimental.pallas import tpu as pltpu
from jax.sharding import PartitionSpec as P

ITERS = 3


CODE_EPS = 0.05
TEMPER = 0.1
NORM_EPS = 1e-06
LANES = 128
MIB = 1024 * 1024


def vmem_spec():
    return pl.BlockSpec(memory_space=pltpu.VMEM)


def params(limit):
    return pltpu.CompilerParams(vmem_limit_bytes=limit * MIB)


def to_columns(line):
    return jnp.broadcast_to(line, (LANES, LANES)).T


def to_line(partial):
    return jnp.sum(partial.T, axis=0, keepdims=True)


def lane_sum(block):
    total = block[:, :LANES]
    for j in range(1, block.shape[1] // LANES):
        total = total + block[:, j * LANES : (j + 1) * LANES]
    return total


def row_fold(block):
    return jnp.sum(block.reshape(block.shape[0] // 8, 8, block.shape[1]), axis=0)


def copies(out_ref, src_ref):
    for i in range(out_ref.shape[0]):
        out_ref[i] = src_ref[...]


def score_kernel(slow, fast, protos, t_ref, out_ref, den_ref, ubt_ref, cb_ref, ub_ref, den_s, col_ref):
    clips, feats = slow.shape
    count = protos.shape[0]
    for v, src in enumerate((slow, fast)):
        for first in range(0, clips, 256):
            rows = pl.ds(first, 256)
            x = src[rows, :].astype(jnp.float32)
            length = jnp.sqrt(jnp.sum(x * x, axis=-1, keepdims=True) + 1e-12)
            u = x / length
            ub_ref[v, rows, :] = u.astype(jnp.bfloat16)
            ubt_ref[v, :, rows] = u.T.astype(jnp.bfloat16)

    def proto_rows(i, _):
        rows = pl.ds(pl.multiple_of(i * 256, 256), 256)
        w = protos[rows, :]
        length = jnp.sqrt(jnp.sum(w * w, axis=-1, keepdims=True) + 1e-12)
        cb_ref[rows, :] = (w / length).astype(jnp.bfloat16)
        return 0

    lax.fori_loop(0, count // 256, proto_rows, 0)
    den_s[...] = jnp.zeros_like(den_s)

    def chunk(j, _):
        first = pl.multiple_of(j * 256, 256)
        weights = cb_ref[pl.ds(first, 256), :]
        for v in range(2):
            cols = jnp.zeros((8, 256), jnp.float32)
            for r in range(0, clips, LANES):
                rows = pl.ds(r, LANES)
                s = lax.dot_general(
                    ub_ref[v, rows, :],
                    weights,
                    (((1,), (1,)), ((), ())),
                    preferred_element_type=jnp.float32,
                )
                t = jnp.exp(s * (1.0 / TEMPER))
                t_ref[v, rows, pl.ds(first, 256)] = t
                cols = cols + row_fold(t * t)
                den_s[v, rows, :] += lane_sum(t)
            line = jnp.sum(cols, axis=0, keepdims=True)
            for h in range(2):
                col_ref[pl.ds(v * (count // LANES) + j * 2 + h, 1), :] = line[
                    :, h * LANES : (h + 1) * LANES
                ]
        return 0

    lax.fori_loop(0, count // 256, chunk, 0)
    groups = clips // LANES
    for v in range(2):
        for i in range(groups):
            den_ref[pl.ds(v * groups + i, 1), :] = to_line(den_s[v, i * LANES : (i + 1) * LANES, :])
    copies(out_ref, col_ref)


def scores(slow, fast, protos, peers):
    clips, feats = slow.shape
    count = protos.shape[0]
    return pl.pallas_call(
        score_kernel,
        out_shape=(
            pltpu.VMEM((2, clips, count), jnp.float32),
            jax.ShapeDtypeStruct((peers, 2 * count // LANES, LANES), jnp.float32),
            jax.ShapeDtypeStruct((2 * clips // LANES, LANES), jnp.float32),
            jax.ShapeDtypeStruct((2, feats, clips), jnp.bfloat16),
            jax.ShapeDtypeStruct((count, feats), jnp.bfloat16),
        ),
        in_specs=[vmem_spec()] * 3,
        out_specs=(vmem_spec(),) * 5,
        scratch_shapes=[
            pltpu.VMEM((2, clips, feats), jnp.bfloat16),
            pltpu.VMEM((2, clips, LANES), jnp.float32),
            pltpu.VMEM((2 * count // LANES, LANES), jnp.float32),
        ],
        compiler_params=params(14),
        name="scores",
    )(slow, fast, protos)


def stack_sum(ref, first=0, size=None):
    size = ref.shape[1] if size is None else size
    total = ref[0, first : first + size, :]
    for i in range(1, ref.shape[0]):
        total = total + ref[i, first : first + size, :]
    return total


def row_kernel(protos_all, extra, t_ref, den_ref, col_ref, out_ref, r_ref, row_ref):
    clips, count = t_ref.shape[1:]
    groups, lines = clips // LANES, count // LANES
    r_ref[...] = 1.0 / (float(protos_all) * stack_sum(col_ref))
    if extra:
        row_ref[2 * groups :, :] = den_ref[...]
    for v in range(2):

        def step(i, _, v=v):
            rows = pl.ds(pl.multiple_of(i * LANES, LANES), LANES)
            acc = jnp.zeros((LANES, LANES), jnp.float32)
            for j in range(lines):
                t = t_ref[v, rows, j * LANES : (j + 1) * LANES]
                acc = acc + t * t * r_ref[v * lines + j : v * lines + j + 1, :]
            row_ref[pl.ds(v * groups + i, 1), :] = to_line(acc)
            return 0

        lax.fori_loop(0, groups, step, 0)
    copies(out_ref, row_ref)


def row_pass(t, den, col_parts, protos_all, extra, peers):
    clips, count = t.shape[1:]
    lines = 2 * clips // LANES * (2 if extra else 1)
    return pl.pallas_call(
        functools.partial(row_kernel, protos_all, extra),
        out_shape=(
            jax.ShapeDtypeStruct((peers, lines, LANES), jnp.float32),
            jax.ShapeDtypeStruct((2 * count // LANES, LANES), jnp.float32),
        ),
        in_specs=[vmem_spec()] * 3,
        out_specs=(vmem_spec(),) * 2,
        scratch_shapes=[pltpu.VMEM((lines, LANES), jnp.float32)],
        compiler_params=params(8),
        name="row_pass",
    )(pltpu.with_memory_space_constraint(t, pltpu.VMEM), den, col_parts)


def col_kernel(clips_all, t_ref, row_ref, out_ref, acc_s, s_s, col_ref):
    clips, count = t_ref.shape[1:]
    groups, lines = clips // LANES, count // LANES
    s_s[...] = 1.0 / (float(clips_all) * stack_sum(row_ref, 0, 2 * groups))
    acc_s[...] = jnp.zeros_like(acc_s)
    for v in range(2):

        def step(i, _, v=v):
            rows = pl.ds(pl.multiple_of(i * LANES, LANES), LANES)
            scale = to_columns(s_s[pl.ds(v * groups + i, 1), :])
            for j in range(lines):
                span = slice(j * LANES, (j + 1) * LANES)
                t = t_ref[v, rows, span]
                acc_s[v, :, span] += row_fold(t * t * scale)
            return 0

        lax.fori_loop(0, groups, step, 0)
        for j in range(lines):
            col_ref[v * lines + j : v * lines + j + 1, :] = jnp.sum(
                acc_s[v, :, j * LANES : (j + 1) * LANES], axis=0, keepdims=True
            )
    copies(out_ref, col_ref)


def col_pass(t, row_parts, clips_all, peers):
    clips, count = t.shape[1:]
    return pl.pallas_call(
        functools.partial(col_kernel, clips_all),
        out_shape=jax.ShapeDtypeStruct((peers, 2 * count // LANES, LANES), jnp.float32),
        in_specs=[vmem_spec()] * 2,
        out_specs=vmem_spec(),
        scratch_shapes=[
            pltpu.VMEM((2, 8, count), jnp.float32),
            pltpu.VMEM((2 * clips // LANES, LANES), jnp.float32),
            pltpu.VMEM((2 * count // LANES, LANES), jnp.float32),
        ],
        compiler_params=params(8),
        name="col_pass",
    )(pltpu.with_memory_space_constraint(t, pltpu.VMEM), row_parts)


def grad_kernel(batch_count, me_ref, t_ref, r_ref, ubt_ref, row_ref, den_ref, *outs):
    send_ref, keep_ref, g_ref, code_s, prob_s = outs
    clips, count = t_ref.shape[1:]
    groups, lines = clips // LANES, count // LANES
    width = count // batch_count
    code = (1.0 / TEMPER) / stack_sum(row_ref, 0, 2 * groups)
    prob = (1.0 / TEMPER) / stack_sum(den_ref, 2 * groups, 2 * groups)
    for v in range(2):
        for i in range(groups):
            line = v * groups + i
            rows = slice(i * LANES, (i + 1) * LANES)
            code_s[v, rows, :] = to_columns(code[line : line + 1, :])
            prob_s[v, rows, :] = to_columns(prob[line : line + 1, :])

    def chunk(m, out_ref, slot):
        which = jnp.bitwise_xor(me_ref[0], m)
        first = pl.multiple_of(which * width, width)
        for h in range(width // LANES):
            span = pl.ds(first + h * LANES, LANES)
            line = which * (width // LANES) + h
            scale = [r_ref[pl.ds(v * lines + line, 1), :] for v in range(2)]
            for i in range(groups):
                rows = slice(i * LANES, (i + 1) * LANES)
                t = [t_ref[v, rows, span] for v in range(2)]
                q = [t[v] * t[v] * scale[v] * code_s[v, rows, :] for v in range(2)]
                for v in range(2):
                    g = t[v] * prob_s[v, rows, :] - q[1 - v]
                    g_ref[v, rows, span] = g.astype(jnp.bfloat16)
        cols = pl.ds(first, width)
        dct = jnp.dot(ubt_ref[0], g_ref[0, :, cols], preferred_element_type=jnp.float32)
        dct = dct + jnp.dot(ubt_ref[1], g_ref[1, :, cols], preferred_element_type=jnp.float32)
        out_ref[slot] = dct.T

    def pair(i, _):
        chunk(2 * i + 1, send_ref, i)
        chunk(2 * i, keep_ref, i)
        return 0

    lax.fori_loop(0, batch_count // 2, pair, 0)


def proto_gradients(me, t, r, ubt, row_parts, den_parts, batch_count):
    clips, count = t.shape[1:]
    feats = ubt.shape[1]
    share = jax.ShapeDtypeStruct(
        (batch_count // 2, count // batch_count, feats), jnp.float32
    )
    return pl.pallas_call(
        functools.partial(grad_kernel, batch_count),
        out_shape=(share, share, pltpu.VMEM((2, clips, count), jnp.bfloat16)),
        in_specs=[pl.BlockSpec(memory_space=pltpu.SMEM)] + [vmem_spec()] * 5,
        out_specs=(vmem_spec(),) * 3,
        scratch_shapes=[
            pltpu.VMEM((2, clips, LANES), jnp.float32),
            pltpu.VMEM((2, clips, LANES), jnp.float32),
        ],
        compiler_params=params(14),
        cost_estimate=pl.CostEstimate(
            flops=4 * clips * count * feats, bytes_accessed=8 * MIB, transcendentals=0
        ),
        name="proto_gradients",
    )(
        me, pltpu.with_memory_space_constraint(t, pltpu.VMEM), r, ubt, row_parts, den_parts
    )


def piece_of(position, order):
    steps = len(order)
    return sum(((position >> (steps - 1 - j)) & 1) << bit for j, bit in enumerate(order))


def embed_grad_kernel(orders, me_ref, g_ref, cb_ref, *outs):
    clips = g_ref.shape[1]
    pieces = 1 << len(orders[0])
    size = clips // pieces
    for v in range(2):
        for place in range(pieces):
            which = jnp.bitwise_xor(me_ref[0], piece_of(place, orders[v]))
            rows = pl.ds(pl.multiple_of(which * size, size), size)
            out_ref = outs[2 * v + (0 if place >= pieces // 2 else 1)]
            out_ref[place % (pieces // 2)] = jnp.dot(
                g_ref[v, rows, :], cb_ref[...], preferred_element_type=jnp.float32
            )


def embed_gradients(me, g, cb, orders):
    clips, count = g.shape[1:]
    feats = cb.shape[1]
    pieces = 1 << len(orders[0])
    share = jax.ShapeDtypeStruct((pieces // 2, clips // pieces, feats), jnp.float32)
    return pl.pallas_call(
        functools.partial(embed_grad_kernel, orders),
        out_shape=(share,) * 4,
        in_specs=[pl.BlockSpec(memory_space=pltpu.SMEM)] + [vmem_spec()] * 2,
        out_specs=(vmem_spec(),) * 4,
        compiler_params=params(10),
        cost_estimate=pl.CostEstimate(
            flops=4 * clips * count * feats, bytes_accessed=8 * MIB, transcendentals=0
        ),
        name="embed_gradients",
    )(me, pltpu.with_memory_space_constraint(g, pltpu.VMEM), cb)


def share_kernel(counts, raw_count, *refs):
    raws = refs[:raw_count]
    terms = refs[raw_count : raw_count + sum(counts)]
    outs = refs[raw_count + sum(counts) :]
    square = jnp.zeros((8, LANES), jnp.float32)
    place = 0
    for n, (raw, count) in enumerate(zip(raws, counts)):
        x = raw[...].astype(jnp.float32)
        length = jnp.sqrt(jnp.sum(x * x, axis=-1, keepdims=True) + 1e-12)
        unit = x / length
        grad = terms[place][...]
        for term in terms[place + 1 : place + count]:
            grad = grad + term[...]
        place += count
        along = jnp.sum(unit * grad, axis=-1, keepdims=True)
        grad = (grad - unit * along) / length
        outs[n][...] = grad
        square = square + row_fold(lane_sum(grad * grad))
    total = jnp.sum(jnp.sum(square, axis=0, keepdims=True), axis=1, keepdims=True)
    outs[-1][...] = jnp.broadcast_to(total, (8, LANES))


def project_shares(raws, groups):
    terms = [term for group in groups for term in group]
    return pl.pallas_call(
        functools.partial(share_kernel, [len(group) for group in groups], len(raws)),
        out_shape=tuple(jax.ShapeDtypeStruct(raw.shape, jnp.float32) for raw in raws)
        + (jax.ShapeDtypeStruct((8, LANES), jnp.float32),),
        in_specs=[vmem_spec()] * (len(raws) + len(terms)),
        out_specs=(vmem_spec(),) * (len(raws) + 1),
        compiler_params=params(8),
        name="project_shares",
    )(*raws, *terms)


def finish_kernel(entries, counts, me_ref, square_ref, *refs):
    ins, outs = refs[: sum(counts)], refs[sum(counts) :]
    place = 0
    for n, count in enumerate(counts):
        mean = square_ref[n, 0:1, 0:1] / entries[n]
        factor = lax.rsqrt(mean + NORM_EPS)
        for m in range(count):
            src = ins[place + m]
            size = src.shape[0]
            which = jnp.bitwise_xor(me_ref[n], m)
            outs[n][pl.ds(pl.multiple_of(which * size, size), size), :] = src[...] * factor
        place += count


def finish(me, squares, groups, entries):
    pieces = [piece for group in groups for piece in group]
    return pl.pallas_call(
        functools.partial(finish_kernel, entries, [len(group) for group in groups]),
        out_shape=tuple(
            jax.ShapeDtypeStruct((len(group) * group[0].shape[0], group[0].shape[1]), jnp.float32)
            for group in groups
        ),
        in_specs=[pl.BlockSpec(memory_space=pltpu.SMEM)] + [vmem_spec()] * (1 + len(pieces)),
        out_specs=(vmem_spec(),) * len(groups),
        compiler_params=params(24),
        name="finish",
    )(me, squares, *pieces)


def exchange(copied, axis):
    return lax.all_to_all(copied, axis, split_axis=0, concat_axis=0, tiled=True)


def swap(own, axis, bit):
    return lax.ppermute(own, axis, [(i, i ^ (1 << bit)) for i in range(lax.axis_size(axis))])


def bits_of(axis):
    count = lax.axis_size(axis)
    bits = count.bit_length() - 1
    if count != 1 << bits:
        raise ValueError("axis size")
    return bits


def scatter_batch(send, keep):
    bits = bits_of("batch")
    recv = swap(send, "batch", 0)
    pieces = {m: [keep[m], recv[m]] for m in range(1 << (bits - 1))}
    for bit in range(bits - 1):
        for m in sorted((m for m in pieces if m >> bit & 1), reverse=True):
            terms = pieces.pop(m)
            total = terms[0]
            for term in terms[1:]:
                total = total + term
            pieces[m ^ (1 << bit)].append(swap(total, "batch", bit + 1))
    return pieces[0]


def scatter_proto(send, keep, order):
    for bit in order[:-1]:
        recv = swap(send, "proto", bit)
        half = keep.shape[0] // 2
        send = keep[half:] + recv[half:]
        keep = keep[:half] + recv[:half]
    return [keep[0], swap(send, "proto", order[-1])[0]]


def gather_bits(own, axis, order):
    pieces = {0: own}
    for bit in order:
        for m in list(pieces):
            pieces[m | 1 << bit] = swap(pieces[m], axis, bit)
    return [pieces[m] for m in range(len(pieces))]


def body(slow_embed, fast_embed, prototypes):
    clip_dev, feat_width = slow_embed.shape
    proto_dev = prototypes.shape[0]
    batch_count = lax.axis_size("batch")
    proto_count = lax.axis_size("proto")
    clips_all = clip_dev * batch_count
    protos_all = proto_dev * proto_count
    proto_entries = float(protos_all * feat_width)
    embed_entries = float(2 * clips_all * feat_width)
    batch_bits, proto_bits = bits_of("batch"), bits_of("proto")
    me_batch, me_proto = lax.axis_index("batch"), lax.axis_index("proto")
    me = jnp.stack([me_batch, me_proto, me_proto]).astype(jnp.int32)
    me_first = me[:1]
    me_second = me[1:2]

    t, col, den, unit_bt, proto_b = scores(slow_embed, fast_embed, prototypes, batch_count)
    for iteration in range(ITERS):
        rows, r = row_pass(
            t, den, exchange(col, "batch"), protos_all, iteration == 0, proto_count
        )
        row_parts = exchange(rows, "proto")
        if iteration == 0:
            den_parts = row_parts
        if iteration + 1 < ITERS:
            col = col_pass(t, row_parts, clips_all, batch_count)

    orders = (tuple(range(proto_bits)), tuple(reversed(range(proto_bits))))
    send, keep, g = proto_gradients(
        me_first, t, r, unit_bt, row_parts, den_parts, batch_count
    )
    sends = embed_gradients(me_second, g, proto_b, orders)

    proto_rows = proto_dev // batch_count
    clip_rows = clip_dev // proto_count
    raw_protos = lax.dynamic_slice_in_dim(prototypes, me_batch * proto_rows, proto_rows, 0)
    raw_views = [
        lax.dynamic_slice_in_dim(x, me_proto * clip_rows, clip_rows, 0)
        for x in (slow_embed, fast_embed)
    ]
    proto_terms = scatter_batch(send, keep)
    view_terms = [scatter_proto(sends[2 * v], sends[2 * v + 1], orders[v]) for v in range(2)]
    grad_proto, proto_square = project_shares([raw_protos], [proto_terms])
    grad_slow, grad_fast, embed_square = project_shares(raw_views, view_terms)

    proto_pieces = gather_bits(grad_proto, "batch", tuple(reversed(range(batch_bits))))
    slow_pieces = gather_bits(grad_slow, "proto", orders[1])
    fast_pieces = gather_bits(grad_fast, "proto", orders[0])
    squares = jnp.stack([proto_square, embed_square, embed_square])
    for bit in range(proto_bits):
        squares = squares + swap(squares, "proto", bit)
    for bit in range(batch_bits):
        squares = squares + swap(squares, "batch", bit)
    return finish(
        me,
        squares,
        (proto_pieces, slow_pieces, fast_pieces),
        (proto_entries, embed_entries, embed_entries),
    )


def solution(mesh):
    placed = (P("batch", None), P("batch", None), P("proto", None))
    return jax.shard_map(
        body,
        mesh=mesh,
        in_specs=placed,
        out_specs=(P("proto", None), P("batch", None), P("batch", None)),
        check_vma=False,
    )
```

```python
import functools

import jax
import jax.numpy as jnp
from jax import lax
from jax.experimental import pallas as pl
from jax.experimental.pallas import tpu as pltpu
from jax.sharding import PartitionSpec as P

ITERS = 3


CODE_EPS = 0.05
TEMPER = 0.1
NORM_EPS = 1e-06
LANES = 128
MIB = 1024 * 1024


def vmem_spec():
    return pl.BlockSpec(memory_space=pltpu.VMEM)


def params(limit):
    return pltpu.CompilerParams(vmem_limit_bytes=limit * MIB)


def to_columns(line):
    return jnp.broadcast_to(line, (LANES, LANES)).T


def to_line(partial):
    return jnp.sum(partial.T, axis=0, keepdims=True)


def lane_sum(block):
    total = block[:, :LANES]
    for j in range(1, block.shape[1] // LANES):
        total = total + block[:, j * LANES : (j + 1) * LANES]
    return total


def row_fold(block):
    return jnp.sum(block.reshape(block.shape[0] // 8, 8, block.shape[1]), axis=0)


def sum_of(refs, first=0, size=None):
    size = refs[0].shape[0] if size is None else size
    total = refs[0][first : first + size, :]
    for ref in refs[1:]:
        total = total + ref[first : first + size, :]
    return total


LOG2E = 1.4426950408889634


def score_kernel(slow, fast, protos, t_ref, col_ref, den_ref, ubt_ref, cb_ref, raw_s, w_s, ub_s, den_s, sems):
    clips, feats = slow.shape
    count = protos.shape[0]
    loads = []
    for v, src in enumerate((slow, fast)):
        loads.append(pltpu.make_async_copy(src, raw_s.at[v], sems.at[v]))
    loads.append(pltpu.make_async_copy(protos, w_s, sems.at[2]))
    for load in loads:
        load.start()
    for v in range(2):
        loads[v].wait()
        for first in range(0, clips, 256):
            rows = pl.ds(first, 256)
            x = raw_s[v, rows, :].astype(jnp.float32)
            length = jnp.sqrt(jnp.sum(x * x, axis=-1, keepdims=True) + 1e-12)
            u = x / length
            ub_s[v, rows, :] = u.astype(jnp.bfloat16)
            ubt_ref[:, v * clips + first : v * clips + first + 256] = u.T.astype(jnp.bfloat16)
    den_s[...] = jnp.zeros_like(den_s)
    loads[2].wait()

    def chunk(j, _):
        first = pl.multiple_of(j * 256, 256)
        w = w_s[pl.ds(first, 256), :]
        length = jnp.sqrt(jnp.sum(w * w, axis=-1, keepdims=True) + 1e-12)
        c = w / length
        cb_ref[pl.ds(first, 256), :] = c.astype(jnp.bfloat16)
        weights = c.T.astype(jnp.bfloat16)
        for v in range(2):
            cols = jnp.zeros((8, 256), jnp.float32)
            for r in range(0, clips, 512):
                s = jnp.dot(
                    ub_s[v, r : r + 512, :], weights, preferred_element_type=jnp.float32
                )
                for q in range(0, 512, 64):
                    rows = pl.ds(r + q, 64)
                    t = jnp.exp2(s[q : q + 64] * (LOG2E / TEMPER))
                    t_ref[v, rows, pl.ds(first, 256)] = t
                    cols = cols + row_fold(t * t)
                    den_s[v, rows, :] += lane_sum(t)
            line = jnp.sum(cols, axis=0, keepdims=True)
            for h in range(2):
                col_ref[pl.ds(v * (count // LANES) + j * 2 + h, 1), :] = line[
                    :, h * LANES : (h + 1) * LANES
                ]
        return 0

    lax.fori_loop(0, count // 256, chunk, 0)
    groups = clips // LANES
    for v in range(2):
        for i in range(groups):
            den_ref[pl.ds(v * groups + i, 1), :] = to_line(den_s[v, i * LANES : (i + 1) * LANES, :])


def scores(slow, fast, protos):
    clips, feats = slow.shape
    count = protos.shape[0]
    return pl.pallas_call(
        score_kernel,
        out_shape=(
            pltpu.VMEM((2, clips, count), jnp.float32),
            jax.ShapeDtypeStruct((2 * count // LANES, LANES), jnp.float32),
            jax.ShapeDtypeStruct((2 * clips // LANES, LANES), jnp.float32),
            jax.ShapeDtypeStruct((feats, 2 * clips), jnp.bfloat16),
            jax.ShapeDtypeStruct((count, feats), jnp.bfloat16),
        ),
        in_specs=[pl.BlockSpec(memory_space=pl.ANY)] * 3,
        out_specs=(vmem_spec(),) * 5,
        scratch_shapes=[
            pltpu.VMEM((2, clips, feats), jnp.bfloat16),
            pltpu.VMEM((count, feats), jnp.float32),
            pltpu.VMEM((2, clips, feats), jnp.bfloat16),
            pltpu.VMEM((2, clips, LANES), jnp.float32),
            pltpu.SemaphoreType.DMA((3,)),
        ],
        compiler_params=params(20),
        name="scores",
    )(slow, fast, protos)


def row_kernel(protos_all, extra, t_ref, den_ref, *refs):
    col_parts, (row_ref, r_ref) = refs[:-2], refs[-2:]
    clips, count = t_ref.shape[1:]
    groups, lines = clips // LANES, count // LANES
    r_ref[...] = 1.0 / (float(protos_all) * sum_of(col_parts))
    if extra:
        row_ref[2 * groups :, :] = den_ref[...]
    for v in range(2):

        def step(i, _, v=v):
            rows = pl.ds(pl.multiple_of(i * LANES, LANES), LANES)
            acc = jnp.zeros((LANES, LANES), jnp.float32)
            for j in range(lines):
                t = t_ref[v, rows, j * LANES : (j + 1) * LANES]
                acc = acc + t * t * r_ref[v * lines + j : v * lines + j + 1, :]
            row_ref[pl.ds(v * groups + i, 1), :] = to_line(acc)
            return 0

        lax.fori_loop(0, groups, step, 0)


def row_pass(t, den, col_parts, protos_all, extra):
    clips, count = t.shape[1:]
    lines = 2 * clips // LANES * (2 if extra else 1)
    return pl.pallas_call(
        functools.partial(row_kernel, protos_all, extra),
        out_shape=(
            jax.ShapeDtypeStruct((lines, LANES), jnp.float32),
            jax.ShapeDtypeStruct((2 * count // LANES, LANES), jnp.float32),
        ),
        in_specs=[vmem_spec()] * (2 + len(col_parts)),
        out_specs=(vmem_spec(),) * 2,
        compiler_params=params(8),
        name="row_pass",
    )(pltpu.with_memory_space_constraint(t, pltpu.VMEM), den, *col_parts)


def col_kernel(clips_all, t_ref, *refs):
    row_parts, (col_ref, acc_s, s_s) = refs[:-3], refs[-3:]
    clips, count = t_ref.shape[1:]
    groups, lines = clips // LANES, count // LANES
    s_s[...] = 1.0 / (float(clips_all) * sum_of(row_parts, 0, 2 * groups))
    acc_s[...] = jnp.zeros_like(acc_s)
    for v in range(2):

        def step(i, _, v=v):
            rows = pl.ds(pl.multiple_of(i * LANES, LANES), LANES)
            scale = to_columns(s_s[pl.ds(v * groups + i, 1), :])
            for j in range(lines):
                span = slice(j * LANES, (j + 1) * LANES)
                t = t_ref[v, rows, span]
                acc_s[v, :, span] += row_fold(t * t * scale)
            return 0

        lax.fori_loop(0, groups, step, 0)
        for j in range(lines):
            col_ref[v * lines + j : v * lines + j + 1, :] = jnp.sum(
                acc_s[v, :, j * LANES : (j + 1) * LANES], axis=0, keepdims=True
            )


def col_pass(t, row_parts, clips_all):
    clips, count = t.shape[1:]
    return pl.pallas_call(
        functools.partial(col_kernel, clips_all),
        out_shape=jax.ShapeDtypeStruct((2 * count // LANES, LANES), jnp.float32),
        in_specs=[vmem_spec()] * (1 + len(row_parts)),
        out_specs=vmem_spec(),
        scratch_shapes=[
            pltpu.VMEM((2, 8, count), jnp.float32),
            pltpu.VMEM((2 * clips // LANES, LANES), jnp.float32),
        ],
        compiler_params=params(8),
        name="col_pass",
    )(pltpu.with_memory_space_constraint(t, pltpu.VMEM), *row_parts)


def piece_of(position, order):
    steps = len(order)
    return sum(((position >> (steps - 1 - j)) & 1) << bit for j, bit in enumerate(order))


def place_of(piece, order):
    steps = len(order)
    return sum(((piece >> bit) & 1) << (steps - 1 - j) for j, bit in enumerate(order))


def grad_kernel(batch_orders, proto_orders, parts, me_ref, t_ref, r_ref, ubt_ref, cb_ref, *refs):
    row_parts, den_parts = refs[:parts], refs[parts : 2 * parts]
    send_ref, keep_ref = refs[2 * parts : 2 * parts + 2]
    du_refs = refs[2 * parts + 2 : 2 * parts + 6]
    g_s, odd_s, even_s, code_s, prob_s = refs[2 * parts + 6 :]
    clips, count = t_ref.shape[1:]
    groups, lines = clips // LANES, count // LANES
    pieces = 1 << len(batch_orders[0])
    width = count // (2 * pieces)
    half = width // 2
    code = (1.0 / TEMPER) / sum_of(row_parts, 0, 2 * groups)
    prob = (1.0 / TEMPER) / sum_of(den_parts, 2 * groups, 2 * groups)
    for v in range(2):
        for i in range(groups):
            line = v * groups + i
            rows = slice(i * LANES, (i + 1) * LANES)
            code_s[v, rows, :] = to_columns(code[line : line + 1, :])
            prob_s[v, rows, :] = to_columns(prob[line : line + 1, :])

    def score_grads(m, chunk_s):
        which = jnp.bitwise_xor(me_ref[0], m)
        first = pl.multiple_of(which * width, width)
        for i in range(0, clips, 32):
            rows = slice(i, i + 32)
            codes = [code_s[v, rows, :] for v in range(2)]
            probs = [prob_s[v, rows, :] for v in range(2)]
            for h in range(width // LANES):
                span = pl.ds(first + h * LANES, LANES)
                line = which * (width // LANES) + h
                t = [t_ref[v, rows, span] for v in range(2)]
                q = [
                    t[v] * t[v] * r_ref[pl.ds(v * lines + line, 1), :] * codes[v]
                    for v in range(2)
                ]
                for v in range(2):
                    g = (t[v] * probs[v] - q[1 - v]).astype(jnp.bfloat16)
                    g_s[v, rows, span] = g
                    chunk_s[v * clips + i : v * clips + i + 32, h * LANES : (h + 1) * LANES] = g

    def proto_grads(i, chunk_s, out_ref):
        dct = jnp.dot(ubt_ref[...], chunk_s[...], preferred_element_type=jnp.float32)
        dc = dct.T
        for h in range(2):
            place = place_of(i, batch_orders[h])
            out_ref[h, place] = dc[h * half : (h + 1) * half]

    even_s[...] = jnp.zeros_like(even_s)

    def pair(i, _):
        score_grads(2 * i + 1, odd_s)
        proto_grads(jnp.maximum(i - 1, 0), even_s, keep_ref)
        score_grads(2 * i, even_s)
        proto_grads(i, odd_s, send_ref)
        return 0

    lax.fori_loop(0, pieces, pair, 0)
    proto_grads(pieces - 1, even_s, keep_ref)

    peers = 1 << len(proto_orders[0])
    size = clips // peers
    for v in range(2):
        for place in range(peers):
            which = jnp.bitwise_xor(me_ref[1], piece_of(place, proto_orders[v]))
            rows = pl.ds(pl.multiple_of(which * size, size), size)
            out_ref = du_refs[2 * v + (0 if place >= peers // 2 else 1)]
            out_ref[place % (peers // 2)] = jnp.dot(
                g_s[v, rows, :], cb_ref[...], preferred_element_type=jnp.float32
            )


def gradients(me, t, r, ubt, cb, row_parts, den_parts, batch_orders, proto_orders):
    clips, count = t.shape[1:]
    feats = cb.shape[1]
    pieces, peers = 1 << len(batch_orders[0]), 1 << len(proto_orders[0])
    width = count // (2 * pieces)
    proto_share = jax.ShapeDtypeStruct((2, pieces, width // 2, feats), jnp.float32)
    embed_share = jax.ShapeDtypeStruct((peers // 2, clips // peers, feats), jnp.float32)
    return pl.pallas_call(
        functools.partial(grad_kernel, batch_orders, proto_orders, len(row_parts)),
        out_shape=(proto_share,) * 2 + (embed_share,) * 4,
        in_specs=[pl.BlockSpec(memory_space=pltpu.SMEM)] + [vmem_spec()] * (4 + 2 * len(row_parts)),
        out_specs=(vmem_spec(),) * 6,
        scratch_shapes=[
            pltpu.VMEM((2, clips, count), jnp.bfloat16),
            pltpu.VMEM((2 * clips, width), jnp.bfloat16),
            pltpu.VMEM((2 * clips, width), jnp.bfloat16),
            pltpu.VMEM((2, clips, LANES), jnp.float32),
            pltpu.VMEM((2, clips, LANES), jnp.float32),
        ],
        compiler_params=params(28),
        name="gradients",
    )(
        me,
        pltpu.with_memory_space_constraint(t, pltpu.VMEM),
        r,
        ubt,
        cb,
        *row_parts,
        *den_parts,
    )


def split_add_kernel(plan, inputs, *refs):
    ins, outs = refs[:inputs], refs[inputs:]
    for n, (keep_place, recv_place, part) in enumerate(plan):
        keep, recv = ins[keep_place], ins[recv_place]
        if part is not None:
            keep, recv = keep.at[part], recv.at[part]
        send_out, keep_out = outs[2 * n : 2 * n + 2]
        half = keep_out.shape[0]
        keep_out[...] = keep[:half] + recv[:half]
        send_out[...] = keep[half:] + recv[half:]


def split_add(arrays, plan):
    halves = []
    for place, _, part in plan:
        shape = arrays[place].shape if part is None else arrays[place].shape[1:]
        halves += [jax.ShapeDtypeStruct((shape[0] // 2,) + shape[1:], jnp.float32)] * 2
    outs = pl.pallas_call(
        functools.partial(split_add_kernel, plan, len(arrays)),
        out_shape=tuple(halves),
        in_specs=[vmem_spec()] * len(arrays),
        out_specs=(vmem_spec(),) * len(halves),
        compiler_params=params(12),
        name="split_add",
    )(*arrays)
    return [(outs[2 * n], outs[2 * n + 1]) for n in range(len(plan))]


def share_kernel(proto_raw, slow_raw, fast_raw, *refs):
    terms, (proto_out, embed_out, square_out) = refs[:-3], refs[-3:]
    half = proto_raw.shape[0] // 2
    jobs = [(proto_raw, slice(h * half, (h + 1) * half), None) for h in range(2)]
    jobs += [(raw, slice(None), v) for v, raw in enumerate((slow_raw, fast_raw))]
    squares = [jnp.zeros((8, LANES), jnp.float32)] * 2
    for n, (raw, rows, view) in enumerate(jobs):
        x = raw[rows, :].astype(jnp.float32)
        length = jnp.sqrt(jnp.sum(x * x, axis=-1, keepdims=True) + 1e-12)
        unit = x / length
        grad = terms[2 * n][0] + terms[2 * n + 1][0]
        along = jnp.sum(unit * grad, axis=-1, keepdims=True)
        grad = (grad - unit * along) / length
        if view is None:
            proto_out[rows, :] = grad
        else:
            embed_out[view] = grad
        kind = 0 if view is None else 1
        squares[kind] = squares[kind] + row_fold(lane_sum(grad * grad))
    for kind in range(2):
        total = jnp.sum(jnp.sum(squares[kind], axis=0, keepdims=True), axis=1, keepdims=True)
        square_out[kind] = jnp.broadcast_to(total, (8, LANES))


def project_shares(raws, terms):
    rows, feats = raws[1].shape
    return pl.pallas_call(
        share_kernel,
        out_shape=(
            jax.ShapeDtypeStruct(raws[0].shape, jnp.float32),
            jax.ShapeDtypeStruct((2, rows, feats), jnp.float32),
            jax.ShapeDtypeStruct((2, 8, LANES), jnp.float32),
        ),
        in_specs=[vmem_spec()] * (len(raws) + len(terms)),
        out_specs=(vmem_spec(),) * 3,
        compiler_params=params(10),
        name="project_shares",
    )(*raws, *terms)


def finish_kernel(entries, plan, inputs, me_ref, square_ref, *refs):
    ins, outs = refs[:inputs], refs[inputs:]
    for n, pieces in enumerate(plan):
        kind = min(n, 1)
        mean = square_ref[kind, 0:1, 0:1] / entries[kind]
        factor = lax.rsqrt(mean + NORM_EPS)
        for m, (place, view) in enumerate(pieces):
            src = ins[place][...] if view is None else ins[place][view]
            size = src.shape[0]
            which = jnp.bitwise_xor(me_ref[kind], m)
            outs[n][pl.ds(pl.multiple_of(which * size, size), size), :] = src * factor


def finish(me, squares, groups, entries):
    arrays, plan, outs = [], [], []
    for group in groups:
        pieces = []
        for array, view in group:
            place = next((i for i, other in enumerate(arrays) if other is array), None)
            if place is None:
                place = len(arrays)
                arrays.append(array)
            pieces.append((place, view))
        plan.append(pieces)
        rows, feats = group[0][0].shape[-2:]
        outs.append(jax.ShapeDtypeStruct((len(group) * rows, feats), jnp.float32))
    return pl.pallas_call(
        functools.partial(finish_kernel, entries, plan, len(arrays)),
        out_shape=tuple(outs),
        in_specs=[pl.BlockSpec(memory_space=pltpu.SMEM)] + [vmem_spec()] * (1 + len(arrays)),
        out_specs=(vmem_spec(),) * len(groups),
        compiler_params=params(16),
        name="finish",
    )(me, squares, *arrays)


def swap(own, axis, mask):
    return lax.ppermute(own, axis, [(i, i ^ mask) for i in range(lax.axis_size(axis))])


def bits_of(axis):
    count = lax.axis_size(axis)
    bits = count.bit_length() - 1
    if count != 1 << bits:
        raise ValueError("axis size")
    return bits


def proto_parts(own):
    return [own] + [swap(own, "proto", m) for m in range(1, lax.axis_size("proto"))]


def batch_parts(own):
    pair = own + swap(own, "batch", 1)
    return [pair] + [swap(pair, "batch", 2 * m) for m in range(1, lax.axis_size("batch") // 2)]


def scatter_sums(groups):
    stage, terms = 0, [None] * len(groups)
    state = list(groups)
    while any(term is None for term in terms):
        live = [n for n in range(len(state)) if terms[n] is None]
        recvs = {}
        for n in live:
            axis, order, send, keep = state[n]
            recvs[n] = swap(send, axis, 1 << order[stage])
        going = []
        for n in live:
            axis, order, send, keep = state[n]
            if stage + 1 == len(order):
                terms[n] = (keep, recvs[n])
            else:
                going.append(n)
        if going:
            arrays = [x for n in going for x in (state[n][3], recvs[n])]
            split = split_add(arrays, [(2 * i, 2 * i + 1, None) for i in range(len(going))])
            for n, (send, keep) in zip(going, split):
                state[n] = (state[n][0], state[n][1], send, keep)
        stage += 1
    return [x for term in terms for x in term]


def gather_batch(own):
    bits = list(reversed(range(lax.axis_size("batch").bit_length() - 1)))
    pieces = {0: own}
    first = {bit: swap(own, "batch", 1 << bit) for bit in bits}
    for bit in bits:
        for m in list(pieces):
            pieces[m | 1 << bit] = first[bit] if m == 0 else swap(pieces[m], "batch", 1 << bit)
    return [(pieces[m], None) for m in range(len(pieces))]


def gather_views(own, orders):
    first = {bit: swap(own, "proto", 1 << bit) for bit in sorted(orders[0])}
    groups = []
    for v, order in enumerate(orders):
        pieces = {0: (own, v)}
        for bit in order:
            for m in list(pieces):
                if m == 0:
                    pieces[1 << bit] = (first[bit], v)
                else:
                    array, view = pieces[m]
                    piece = array if view is None else array[view]
                    pieces[m | 1 << bit] = (swap(piece, "proto", 1 << bit), None)
        groups.append([pieces[m] for m in range(len(pieces))])
    return groups


def body(slow_embed, fast_embed, prototypes):
    clip_dev, feat_width = slow_embed.shape
    proto_dev = prototypes.shape[0]
    batch_count = lax.axis_size("batch")
    proto_count = lax.axis_size("proto")
    clips_all = clip_dev * batch_count
    protos_all = proto_dev * proto_count
    proto_entries = float(protos_all * feat_width)
    embed_entries = float(2 * clips_all * feat_width)
    batch_bits, proto_bits = bits_of("batch"), bits_of("proto")
    me_batch, me_proto = lax.axis_index("batch"), lax.axis_index("proto")
    me = jnp.stack([me_batch, me_proto]).astype(jnp.int32)

    t, col, den, unit_bt, proto_b = scores(slow_embed, fast_embed, prototypes)
    for iteration in range(ITERS):
        rows, r = row_pass(t, den, batch_parts(col), protos_all, iteration == 0)
        row_parts = proto_parts(rows)
        if iteration == 0:
            den_parts = row_parts
        if iteration + 1 < ITERS:
            col = col_pass(t, row_parts, clips_all)

    near = tuple(range(batch_bits - 1))
    batch_orders = (near, tuple(reversed(near)))
    proto_orders = (tuple(range(proto_bits)), tuple(reversed(range(proto_bits))))
    send, keep, *shares = gradients(
        me, t, r, unit_bt, proto_b, row_parts, den_parts, batch_orders, proto_orders
    )

    proto_rows = proto_dev // batch_count
    clip_rows = clip_dev // proto_count
    raws = [lax.dynamic_slice_in_dim(prototypes, me_batch * proto_rows, proto_rows, 0)]
    for x in (slow_embed, fast_embed):
        raws.append(lax.dynamic_slice_in_dim(x, me_proto * clip_rows, clip_rows, 0))
    recv = swap(send, "batch", 1)
    halves = split_add([keep, recv], [(0, 1, h) for h in range(2)])
    groups = []
    for h in range(2):
        order = tuple(bit + 1 for bit in batch_orders[h])
        groups.append(("batch", order) + tuple(halves[h]))
    for v in range(2):
        groups.append(("proto", proto_orders[v], shares[2 * v], shares[2 * v + 1]))
    grad_proto, grad_embed, squares = project_shares(raws, scatter_sums(groups))

    proto_pieces = gather_batch(grad_proto)
    view_pieces = gather_views(grad_embed, (proto_orders[1], proto_orders[0]))
    for bit in range(proto_bits):
        squares = squares + swap(squares, "proto", 1 << bit)
    for bit in range(batch_bits):
        squares = squares + swap(squares, "batch", 1 << bit)
    return finish(me, squares, [proto_pieces] + view_pieces, (proto_entries, embed_entries))


def solution(mesh):
    placed = (P("batch", None), P("batch", None), P("proto", None))
    return jax.shard_map(
        body,
        mesh=mesh,
        in_specs=placed,
        out_specs=(P("proto", None), P("batch", None), P("batch", None)),
        check_vma=False,
    )
```

```python
import functools

import jax
import jax.numpy as jnp
from jax import lax
from jax.experimental import pallas as pl
from jax.experimental.pallas import tpu as pltpu
from jax.sharding import PartitionSpec as P

ITERS = 3


CODE_EPS = 0.05
TEMPER = 0.1
NORM_EPS = 1e-06
LANES = 128
MIB = 1024 * 1024


def vmem_spec():
    return pl.BlockSpec(memory_space=pltpu.VMEM)


def params(limit):
    return pltpu.CompilerParams(vmem_limit_bytes=limit * MIB)


def to_columns(line):
    return jnp.broadcast_to(line, (LANES, LANES)).T


def to_line(partial):
    return jnp.sum(partial.T, axis=0, keepdims=True)


def lane_sum(block):
    total = block[:, :LANES]
    for j in range(1, block.shape[1] // LANES):
        total = total + block[:, j * LANES : (j + 1) * LANES]
    return total


def row_fold(block):
    return jnp.sum(block.reshape(block.shape[0] // 8, 8, block.shape[1]), axis=0)


def sum_of(refs, first=0, size=None):
    size = refs[0].shape[0] if size is None else size
    total = refs[0][first : first + size, :]
    for ref in refs[1:]:
        total = total + ref[first : first + size, :]
    return total


LOG2E = 1.4426950408889634


def score_kernel(slow, fast, protos, t_ref, col_ref, den_ref, ubt_ref, cb_ref, raw_s, w_s, ub_s, den_s, sems):
    clips, feats = slow.shape
    count = protos.shape[0]
    loads = []
    for v, src in enumerate((slow, fast)):
        loads.append(pltpu.make_async_copy(src, raw_s.at[v], sems.at[v]))
    loads.append(pltpu.make_async_copy(protos, w_s, sems.at[2]))
    for load in loads:
        load.start()
    for v in range(2):
        loads[v].wait()
        for first in range(0, clips, 256):
            rows = pl.ds(first, 256)
            x = raw_s[v, rows, :].astype(jnp.float32)
            length = jnp.sqrt(jnp.sum(x * x, axis=-1, keepdims=True) + 1e-12)
            u = x / length
            ub_s[v, rows, :] = u.astype(jnp.bfloat16)
            ubt_ref[:, v * clips + first : v * clips + first + 256] = u.T.astype(jnp.bfloat16)
    den_s[...] = jnp.zeros_like(den_s)
    loads[2].wait()

    def chunk(j, _):
        first = pl.multiple_of(j * 256, 256)
        w = w_s[pl.ds(first, 256), :]
        length = jnp.sqrt(jnp.sum(w * w, axis=-1, keepdims=True) + 1e-12)
        c = w / length
        cb_ref[pl.ds(first, 256), :] = c.astype(jnp.bfloat16)
        weights = c.T.astype(jnp.bfloat16)
        for v in range(2):
            cols = jnp.zeros((8, 256), jnp.float32)
            for r in range(0, clips, 512):
                s = jnp.dot(
                    ub_s[v, r : r + 512, :], weights, preferred_element_type=jnp.float32
                )
                for q in range(0, 512, 64):
                    rows = pl.ds(r + q, 64)
                    t = jnp.exp2(s[q : q + 64] * (LOG2E / TEMPER))
                    t_ref[v, rows, pl.ds(first, 256)] = t
                    cols = cols + row_fold(t * t)
                    den_s[v, rows, :] += lane_sum(t)
            line = jnp.sum(cols, axis=0, keepdims=True)
            for h in range(2):
                col_ref[pl.ds(v * (count // LANES) + j * 2 + h, 1), :] = line[
                    :, h * LANES : (h + 1) * LANES
                ]
        return 0

    lax.fori_loop(0, count // 256, chunk, 0)
    groups = clips // LANES
    for v in range(2):
        for i in range(groups):
            den_ref[pl.ds(v * groups + i, 1), :] = to_line(den_s[v, i * LANES : (i + 1) * LANES, :])


def scores(slow, fast, protos):
    clips, feats = slow.shape
    count = protos.shape[0]
    return pl.pallas_call(
        score_kernel,
        out_shape=(
            pltpu.VMEM((2, clips, count), jnp.float32),
            jax.ShapeDtypeStruct((2 * count // LANES, LANES), jnp.float32),
            jax.ShapeDtypeStruct((2 * clips // LANES, LANES), jnp.float32),
            jax.ShapeDtypeStruct((feats, 2 * clips), jnp.bfloat16),
            jax.ShapeDtypeStruct((count, feats), jnp.bfloat16),
        ),
        in_specs=[pl.BlockSpec(memory_space=pltpu.HBM)] * 3,
        out_specs=(vmem_spec(),) * 5,
        scratch_shapes=[
            pltpu.VMEM((2, clips, feats), jnp.bfloat16),
            pltpu.VMEM((count, feats), jnp.float32),
            pltpu.VMEM((2, clips, feats), jnp.bfloat16),
            pltpu.VMEM((2, clips, LANES), jnp.float32),
            pltpu.SemaphoreType.DMA((3,)),
        ],
        compiler_params=params(24),
        name="scores",
    )(slow, fast, protos)


def row_kernel(protos_all, extra, t_ref, den_ref, *refs):
    col_parts, (row_ref, r_ref) = refs[:-2], refs[-2:]
    clips, count = t_ref.shape[1:]
    groups, lines = clips // LANES, count // LANES
    r_ref[...] = 1.0 / (float(protos_all) * sum_of(col_parts))
    if extra:
        row_ref[2 * groups :, :] = den_ref[...]
    for v in range(2):

        def step(i, _, v=v):
            rows = pl.ds(pl.multiple_of(i * LANES, LANES), LANES)
            acc = jnp.zeros((LANES, LANES), jnp.float32)
            for j in range(lines):
                t = t_ref[v, rows, j * LANES : (j + 1) * LANES]
                acc = acc + t * t * r_ref[v * lines + j : v * lines + j + 1, :]
            row_ref[pl.ds(v * groups + i, 1), :] = to_line(acc)
            return 0

        lax.fori_loop(0, groups, step, 0)


def row_pass(t, den, col_parts, protos_all, extra):
    clips, count = t.shape[1:]
    lines = 2 * clips // LANES * (2 if extra else 1)
    return pl.pallas_call(
        functools.partial(row_kernel, protos_all, extra),
        out_shape=(
            jax.ShapeDtypeStruct((lines, LANES), jnp.float32),
            jax.ShapeDtypeStruct((2 * count // LANES, LANES), jnp.float32),
        ),
        in_specs=[vmem_spec()] * (2 + len(col_parts)),
        out_specs=(vmem_spec(),) * 2,
        compiler_params=params(8),
        name="row_pass",
    )(pltpu.with_memory_space_constraint(t, pltpu.VMEM), den, *col_parts)


def col_kernel(clips_all, t_ref, *refs):
    row_parts, (col_ref, acc_s, s_s) = refs[:-3], refs[-3:]
    clips, count = t_ref.shape[1:]
    groups, lines = clips // LANES, count // LANES
    s_s[...] = 1.0 / (float(clips_all) * sum_of(row_parts, 0, 2 * groups))
    acc_s[...] = jnp.zeros_like(acc_s)
    for v in range(2):

        def step(i, _, v=v):
            rows = pl.ds(pl.multiple_of(i * LANES, LANES), LANES)
            scale = to_columns(s_s[pl.ds(v * groups + i, 1), :])
            for j in range(lines):
                span = slice(j * LANES, (j + 1) * LANES)
                t = t_ref[v, rows, span]
                acc_s[v, :, span] += row_fold(t * t * scale)
            return 0

        lax.fori_loop(0, groups, step, 0)
        for j in range(lines):
            col_ref[v * lines + j : v * lines + j + 1, :] = jnp.sum(
                acc_s[v, :, j * LANES : (j + 1) * LANES], axis=0, keepdims=True
            )


def col_pass(t, row_parts, clips_all):
    clips, count = t.shape[1:]
    return pl.pallas_call(
        functools.partial(col_kernel, clips_all),
        out_shape=jax.ShapeDtypeStruct((2 * count // LANES, LANES), jnp.float32),
        in_specs=[vmem_spec()] * (1 + len(row_parts)),
        out_specs=vmem_spec(),
        scratch_shapes=[
            pltpu.VMEM((2, 8, count), jnp.float32),
            pltpu.VMEM((2 * clips // LANES, LANES), jnp.float32),
        ],
        compiler_params=params(8),
        name="col_pass",
    )(pltpu.with_memory_space_constraint(t, pltpu.VMEM), *row_parts)


def piece_of(position, order):
    steps = len(order)
    return sum(((position >> (steps - 1 - j)) & 1) << bit for j, bit in enumerate(order))


def place_of(piece, order):
    steps = len(order)
    return sum(((piece >> bit) & 1) << (steps - 1 - j) for j, bit in enumerate(order))


def grad_kernel(batch_orders, proto_orders, parts, t_ref, r_ref, ubt_ref, cb_ref, *refs):
    row_parts, den_parts = refs[:parts], refs[parts : 2 * parts]
    send_ref, keep_ref = refs[2 * parts : 2 * parts + 2]
    du_refs = refs[2 * parts + 2 : 2 * parts + 6]
    g_s, odd_s, even_s, code_s, prob_s = refs[2 * parts + 6 :]
    clips, count = t_ref.shape[1:]
    groups, lines = clips // LANES, count // LANES
    pieces = 1 << len(batch_orders[0])
    width = count // (2 * pieces)
    half = width // 2
    code = (1.0 / TEMPER) / sum_of(row_parts, 0, 2 * groups)
    prob = (1.0 / TEMPER) / sum_of(den_parts, 2 * groups, 2 * groups)
    for v in range(2):
        for i in range(groups):
            line = v * groups + i
            rows = slice(i * LANES, (i + 1) * LANES)
            code_s[v, rows, :] = to_columns(code[line : line + 1, :])
            prob_s[v, rows, :] = to_columns(prob[line : line + 1, :])

    def score_grads(m, chunk_s):
        which = jnp.bitwise_xor(lax.axis_index("batch"), m)
        first = pl.multiple_of(which * width, width)
        for i in range(0, clips, 32):
            rows = slice(i, i + 32)
            codes = [code_s[v, rows, :] for v in range(2)]
            probs = [prob_s[v, rows, :] for v in range(2)]
            for h in range(width // LANES):
                span = pl.ds(first + h * LANES, LANES)
                line = which * (width // LANES) + h
                t = [t_ref[v, rows, span] for v in range(2)]
                q = [
                    t[v] * t[v] * r_ref[pl.ds(v * lines + line, 1), :] * codes[v]
                    for v in range(2)
                ]
                for v in range(2):
                    g = (t[v] * probs[v] - q[1 - v]).astype(jnp.bfloat16)
                    g_s[v, rows, span] = g
                    chunk_s[v * clips + i : v * clips + i + 32, h * LANES : (h + 1) * LANES] = g

    def proto_grads(i, chunk_s, out_ref):
        dct = jnp.dot(ubt_ref[...], chunk_s[...], preferred_element_type=jnp.float32)
        dc = dct.T
        for h in range(2):
            place = place_of(i, batch_orders[h])
            out_ref[h, place] = dc[h * half : (h + 1) * half]

    even_s[...] = jnp.zeros_like(even_s)

    def pair(i, _):
        score_grads(2 * i + 1, odd_s)
        proto_grads(jnp.maximum(i - 1, 0), even_s, keep_ref)
        score_grads(2 * i, even_s)
        proto_grads(i, odd_s, send_ref)
        return 0

    lax.fori_loop(0, pieces, pair, 0)
    proto_grads(pieces - 1, even_s, keep_ref)

    peers = 1 << len(proto_orders[0])
    size = clips // peers
    for v in range(2):
        for place in range(peers):
            which = jnp.bitwise_xor(lax.axis_index("proto"), piece_of(place, proto_orders[v]))
            rows = pl.ds(pl.multiple_of(which * size, size), size)
            out_ref = du_refs[2 * v + (0 if place >= peers // 2 else 1)]
            out_ref[place % (peers // 2)] = jnp.dot(
                g_s[v, rows, :], cb_ref[...], preferred_element_type=jnp.float32
            )


def gradients(t, r, ubt, cb, row_parts, den_parts, batch_orders, proto_orders):
    clips, count = t.shape[1:]
    feats = cb.shape[1]
    pieces, peers = 1 << len(batch_orders[0]), 1 << len(proto_orders[0])
    width = count // (2 * pieces)
    proto_share = jax.ShapeDtypeStruct((2, pieces, width // 2, feats), jnp.float32)
    embed_share = jax.ShapeDtypeStruct((peers // 2, clips // peers, feats), jnp.float32)
    return pl.pallas_call(
        functools.partial(grad_kernel, batch_orders, proto_orders, len(row_parts)),
        out_shape=(proto_share,) * 2 + (embed_share,) * 4,
        in_specs=[vmem_spec()] * (4 + 2 * len(row_parts)),
        out_specs=(vmem_spec(),) * 6,
        scratch_shapes=[
            pltpu.VMEM((2, clips, count), jnp.bfloat16),
            pltpu.VMEM((2 * clips, width), jnp.bfloat16),
            pltpu.VMEM((2 * clips, width), jnp.bfloat16),
            pltpu.VMEM((2, clips, LANES), jnp.float32),
            pltpu.VMEM((2, clips, LANES), jnp.float32),
        ],
        compiler_params=params(24),
        name="gradients",
    )(
        pltpu.with_memory_space_constraint(t, pltpu.VMEM),
        r,
        ubt,
        cb,
        *row_parts,
        *den_parts,
    )


def split_add_kernel(plan, inputs, *refs):
    ins, outs = refs[:inputs], refs[inputs:]
    for n, (keep_place, recv_place, part) in enumerate(plan):
        keep, recv = ins[keep_place], ins[recv_place]
        if part is not None:
            keep, recv = keep.at[part], recv.at[part]
        send_out, keep_out = outs[2 * n : 2 * n + 2]
        half = keep_out.shape[0]
        keep_out[...] = keep[:half] + recv[:half]
        send_out[...] = keep[half:] + recv[half:]


def split_add(arrays, plan):
    halves = []
    for place, _, part in plan:
        shape = arrays[place].shape if part is None else arrays[place].shape[1:]
        halves += [jax.ShapeDtypeStruct((shape[0] // 2,) + shape[1:], jnp.float32)] * 2
    outs = pl.pallas_call(
        functools.partial(split_add_kernel, plan, len(arrays)),
        out_shape=tuple(halves),
        in_specs=[vmem_spec()] * len(arrays),
        out_specs=(vmem_spec(),) * len(halves),
        compiler_params=params(12),
        name="split_add",
    )(*arrays)
    return [(outs[2 * n], outs[2 * n + 1]) for n in range(len(plan))]


def project(raw, terms):
    x = raw.astype(jnp.float32)
    length = jnp.sqrt(jnp.sum(x * x, axis=-1, keepdims=True) + 1e-12)
    unit = x / length
    grad = terms[0][0] + terms[1][0]
    along = jnp.sum(unit * grad, axis=-1, keepdims=True)
    return (grad - unit * along) / length


def share_kernel(proto_raw, slow_raw, fast_raw, *refs):
    terms, (proto_out, square_out) = refs[:-2], refs[-2:]
    half = proto_raw.shape[0] // 2
    squares = [jnp.zeros((8, LANES), jnp.float32)] * 2
    for h in range(2):
        rows = slice(h * half, (h + 1) * half)
        grad = project(proto_raw[rows, :], terms[2 * h : 2 * h + 2])
        proto_out[rows, :] = grad
        squares[0] = squares[0] + row_fold(lane_sum(grad * grad))
    for v, raw in enumerate((slow_raw, fast_raw)):
        grad = project(raw[...], terms[4 + 2 * v : 6 + 2 * v])
        squares[1] = squares[1] + row_fold(lane_sum(grad * grad))
    for kind in range(2):
        total = jnp.sum(jnp.sum(squares[kind], axis=0, keepdims=True), axis=1, keepdims=True)
        square_out[kind] = jnp.broadcast_to(total, (8, LANES))


def project_protos(raws, terms):
    return pl.pallas_call(
        share_kernel,
        out_shape=(
            jax.ShapeDtypeStruct(raws[0].shape, jnp.float32),
            jax.ShapeDtypeStruct((2, 8, LANES), jnp.float32),
        ),
        in_specs=[vmem_spec()] * (len(raws) + len(terms)),
        out_specs=(vmem_spec(),) * 2,
        compiler_params=params(10),
        name="project_protos",
    )(*raws, *terms)


def embed_kernel(square_ref, other_ref, slow_raw, fast_raw, *refs):
    terms, (embed_out, square_out) = refs[:-2], refs[-2:]
    square_out[...] = square_ref[...] + other_ref[...]
    for v, raw in enumerate((slow_raw, fast_raw)):
        embed_out[v] = project(raw[...], terms[2 * v : 2 * v + 2])


def project_embeds(square, other, raws, terms):
    rows, feats = raws[0].shape
    return pl.pallas_call(
        embed_kernel,
        out_shape=(
            jax.ShapeDtypeStruct((2, rows, feats), jnp.float32),
            jax.ShapeDtypeStruct(square.shape, jnp.float32),
        ),
        in_specs=[vmem_spec()] * (2 + len(raws) + len(terms)),
        out_specs=(vmem_spec(),) * 2,
        compiler_params=params(10),
        name="project_embeds",
    )(square, other, *raws, *terms)


def add_kernel(x_ref, y_ref, *refs):
    refs[-1][...] = x_ref[...] + y_ref[...]


def add_after(x, y, arrived):
    return pl.pallas_call(
        add_kernel,
        out_shape=jax.ShapeDtypeStruct(x.shape, x.dtype),
        in_specs=[vmem_spec()] * 2 + [pl.BlockSpec(memory_space=pl.ANY)] * len(arrived),
        out_specs=vmem_spec(),
        compiler_params=params(4),
        name="add_after",
    )(x, y, *arrived)


def finish_kernel(axis, kind, entries, plan, inputs, square_ref, other_ref, *refs):
    ins, outs = refs[:inputs], refs[inputs:]
    square = square_ref[kind, 0:1, 0:1] + other_ref[kind, 0:1, 0:1]
    factor = lax.rsqrt(square / entries + NORM_EPS)
    for n, pieces in enumerate(plan):
        for m, (place, view) in enumerate(pieces):
            src = ins[place][...] if view is None else ins[place][view]
            size = src.shape[0]
            which = jnp.bitwise_xor(lax.axis_index(axis), m)
            outs[n][pl.ds(pl.multiple_of(which * size, size), size), :] = src * factor


def finish(axis, kind, entries, square, other, groups):
    arrays, plan, outs = [], [], []
    for group in groups:
        pieces = []
        for array, view in group:
            place = next((i for i, known in enumerate(arrays) if known is array), None)
            if place is None:
                place = len(arrays)
                arrays.append(array)
            pieces.append((place, view))
        plan.append(pieces)
        rows, feats = group[0][0].shape[-2:]
        outs.append(jax.ShapeDtypeStruct((len(group) * rows, feats), jnp.float32))
    return pl.pallas_call(
        functools.partial(finish_kernel, axis, kind, entries, plan, len(arrays)),
        out_shape=tuple(outs),
        in_specs=[vmem_spec()] * (2 + len(arrays)),
        out_specs=(vmem_spec(),) * len(groups),
        compiler_params=params(12),
        name="finish",
    )(square, other, *arrays)


def swap(own, axis, mask):
    return lax.ppermute(own, axis, [(i, i ^ mask) for i in range(lax.axis_size(axis))])


def bits_of(axis):
    count = lax.axis_size(axis)
    bits = count.bit_length() - 1
    if count != 1 << bits:
        raise ValueError("axis size")
    return bits


def proto_parts(own):
    return [own] + [swap(own, "proto", m) for m in range(1, lax.axis_size("proto"))]


def batch_parts(own):
    pair = own + swap(own, "batch", 1)
    return [pair] + [swap(pair, "batch", 2 * m) for m in range(1, lax.axis_size("batch") // 2)]


def scatter_sums(groups):
    stage, terms = 0, [None] * len(groups)
    state = list(groups)
    while any(term is None for term in terms):
        live = [n for n in range(len(state)) if terms[n] is None]
        recvs = {}
        for n in live:
            axis, order, send, keep = state[n]
            recvs[n] = swap(send, axis, 1 << order[stage])
        going = []
        for n in live:
            axis, order, send, keep = state[n]
            if stage + 1 == len(order):
                terms[n] = (keep, recvs[n])
            else:
                going.append(n)
        if going:
            arrays = [x for n in going for x in (state[n][3], recvs[n])]
            split = split_add(arrays, [(2 * i, 2 * i + 1, None) for i in range(len(going))])
            for n, (send, keep) in zip(going, split):
                state[n] = (state[n][0], state[n][1], send, keep)
        stage += 1
    return [x for term in terms for x in term]


def gather_batch(own):
    bits = list(reversed(range(lax.axis_size("batch").bit_length() - 1)))
    pieces = {0: own}
    first = {bit: swap(own, "batch", 1 << bit) for bit in bits}
    for bit in bits:
        for m in list(pieces):
            pieces[m | 1 << bit] = first[bit] if m == 0 else swap(pieces[m], "batch", 1 << bit)
    return [(pieces[m], None) for m in range(len(pieces))]


def gather_views(own, orders):
    first = {bit: swap(own, "proto", 1 << bit) for bit in sorted(orders[0])}
    groups = []
    for v, order in enumerate(orders):
        pieces = {0: (own, v)}
        for bit in order:
            for m in list(pieces):
                if m == 0:
                    pieces[1 << bit] = (first[bit], v)
                else:
                    array, view = pieces[m]
                    piece = array if view is None else array[view]
                    pieces[m | 1 << bit] = (swap(piece, "proto", 1 << bit), None)
        groups.append([pieces[m] for m in range(len(pieces))])
    return groups


def body(slow_embed, fast_embed, prototypes):
    clip_dev, feat_width = slow_embed.shape
    proto_dev = prototypes.shape[0]
    batch_count = lax.axis_size("batch")
    proto_count = lax.axis_size("proto")
    clips_all = clip_dev * batch_count
    protos_all = proto_dev * proto_count
    proto_entries = float(protos_all * feat_width)
    embed_entries = float(2 * clips_all * feat_width)
    batch_bits, proto_bits = bits_of("batch"), bits_of("proto")
    me_batch, me_proto = lax.axis_index("batch"), lax.axis_index("proto")

    t, col, den, unit_bt, proto_b = scores(slow_embed, fast_embed, prototypes)
    for iteration in range(ITERS):
        rows, r = row_pass(t, den, batch_parts(col), protos_all, iteration == 0)
        row_parts = proto_parts(rows)
        if iteration == 0:
            den_parts = row_parts
        if iteration + 1 < ITERS:
            col = col_pass(t, row_parts, clips_all)

    near = tuple(range(batch_bits - 1))
    batch_orders = (near, tuple(reversed(near)))
    proto_orders = (tuple(range(proto_bits)), tuple(reversed(range(proto_bits))))
    send, keep, *shares = gradients(
        t, r, unit_bt, proto_b, row_parts, den_parts, batch_orders, proto_orders
    )

    proto_rows = proto_dev // batch_count
    clip_rows = clip_dev // proto_count
    raws = [lax.dynamic_slice_in_dim(prototypes, me_batch * proto_rows, proto_rows, 0)]
    for x in (slow_embed, fast_embed):
        raws.append(lax.dynamic_slice_in_dim(x, me_proto * clip_rows, clip_rows, 0))
    recv = swap(send, "batch", 1)
    halves = split_add([keep, recv], [(0, 1, h) for h in range(2)])
    groups = []
    for h in range(2):
        order = tuple(bit + 1 for bit in batch_orders[h])
        groups.append(("batch", order) + tuple(halves[h]))
    for v in range(2):
        groups.append(("proto", proto_orders[v], shares[2 * v], shares[2 * v + 1]))
    terms = scatter_sums(groups)
    grad_proto, square = project_protos(raws, terms)
    proto_pieces = gather_batch(grad_proto)
    for bit in range(proto_bits - 1):
        square = square + swap(square, "proto", 1 << bit)
    other = swap(square, "proto", 1 << (proto_bits - 1))
    grad_embed, square = project_embeds(square, other, raws[1:], terms[4:])
    view_pieces = gather_views(grad_embed, (proto_orders[1], proto_orders[0]))
    arrived = [proto_pieces[1 << bit][0] for bit in range(1, batch_bits)]
    square = add_after(square, swap(square, "batch", 1), arrived)
    for bit in range(1, batch_bits - 1):
        square = square + swap(square, "batch", 1 << bit)
    other = swap(square, "batch", 1 << (batch_bits - 1))
    (proto_grad,) = finish("batch", 0, proto_entries, square, other, [proto_pieces])
    slow_grad, fast_grad = finish("proto", 1, embed_entries, square, other, view_pieces)
    return proto_grad, slow_grad, fast_grad


def solution(mesh):
    placed = (P("batch", None), P("batch", None), P("proto", None))
    return jax.shard_map(
        body,
        mesh=mesh,
        in_specs=placed,
        out_specs=(P("proto", None), P("batch", None), P("batch", None)),
        check_vma=False,
    )
```

```python
import functools

import jax
import jax.numpy as jnp
from jax import lax
from jax.experimental import pallas as pl
from jax.experimental.pallas import tpu as pltpu
from jax.sharding import PartitionSpec as P

ITERS = 3


CODE_EPS = 0.05
TEMPER = 0.1
NORM_EPS = 1e-06
LANES = 128
MIB = 1024 * 1024


def vmem_spec():
    return pl.BlockSpec(memory_space=pltpu.VMEM)


def params(limit):
    return pltpu.CompilerParams(vmem_limit_bytes=limit * MIB)


def to_columns(line):
    return jnp.broadcast_to(line, (LANES, LANES)).T


def to_line(partial):
    return jnp.sum(partial.T, axis=0, keepdims=True)


def lane_sum(block):
    total = block[:, :LANES]
    for j in range(1, block.shape[1] // LANES):
        total = total + block[:, j * LANES : (j + 1) * LANES]
    return total


def row_fold(block):
    return jnp.sum(block.reshape(block.shape[0] // 8, 8, block.shape[1]), axis=0)


def sum_of(refs, first=0, size=None):
    size = refs[0].shape[0] if size is None else size
    total = refs[0][first : first + size, :]
    for ref in refs[1:]:
        total = total + ref[first : first + size, :]
    return total


LOG2E = 1.4426950408889634


def score_kernel(slow, fast, protos, t_ref, col_ref, den_ref, ubt_ref, cb_ref, raw_s, w_s, ub_s, den_s, sems):
    clips, feats = slow.shape
    count = protos.shape[0]
    loads = []
    for v, src in enumerate((slow, fast)):
        loads.append(pltpu.make_async_copy(src, raw_s.at[v], sems.at[v]))
    loads.append(pltpu.make_async_copy(protos, w_s, sems.at[2]))
    for load in loads:
        load.start()
    for v in range(2):
        loads[v].wait()
        for first in range(0, clips, 256):
            rows = pl.ds(first, 256)
            x = raw_s[v, rows, :].astype(jnp.float32)
            length = jnp.sqrt(jnp.sum(x * x, axis=-1, keepdims=True) + 1e-12)
            u = x / length
            ub_s[v, rows, :] = u.astype(jnp.bfloat16)
            ubt_ref[:, v * clips + first : v * clips + first + 256] = u.T.astype(jnp.bfloat16)
    den_s[...] = jnp.zeros_like(den_s)
    loads[2].wait()

    def chunk(j, _):
        first = pl.multiple_of(j * 256, 256)
        w = w_s[pl.ds(first, 256), :]
        length = jnp.sqrt(jnp.sum(w * w, axis=-1, keepdims=True) + 1e-12)
        c = w / length
        cb_ref[pl.ds(first, 256), :] = c.astype(jnp.bfloat16)
        weights = c.T.astype(jnp.bfloat16)
        for v in range(2):
            cols = jnp.zeros((8, 256), jnp.float32)
            for r in range(0, clips, 512):
                s = jnp.dot(
                    ub_s[v, r : r + 512, :], weights, preferred_element_type=jnp.float32
                )
                for q in range(0, 512, 64):
                    rows = pl.ds(r + q, 64)
                    t = jnp.exp2(s[q : q + 64] * (LOG2E / TEMPER))
                    t_ref[v, rows, pl.ds(first, 256)] = t
                    cols = cols + row_fold(t * t)
                    den_s[v, rows, :] += lane_sum(t)
            line = jnp.sum(cols, axis=0, keepdims=True)
            for h in range(2):
                col_ref[pl.ds(v * (count // LANES) + j * 2 + h, 1), :] = line[
                    :, h * LANES : (h + 1) * LANES
                ]
        return 0

    lax.fori_loop(0, count // 256, chunk, 0)
    groups = clips // LANES
    for v in range(2):
        for i in range(groups):
            den_ref[pl.ds(v * groups + i, 1), :] = to_line(den_s[v, i * LANES : (i + 1) * LANES, :])


def scores(slow, fast, protos):
    clips, feats = slow.shape
    count = protos.shape[0]
    return pl.pallas_call(
        score_kernel,
        out_shape=(
            pltpu.VMEM((2, clips, count), jnp.float32),
            jax.ShapeDtypeStruct((2 * count // LANES, LANES), jnp.float32),
            jax.ShapeDtypeStruct((2 * clips // LANES, LANES), jnp.float32),
            jax.ShapeDtypeStruct((feats, 2 * clips), jnp.bfloat16),
            jax.ShapeDtypeStruct((count, feats), jnp.bfloat16),
        ),
        in_specs=[pl.BlockSpec(memory_space=pltpu.HBM)] * 3,
        out_specs=(vmem_spec(),) * 5,
        scratch_shapes=[
            pltpu.VMEM((2, clips, feats), jnp.bfloat16),
            pltpu.VMEM((count, feats), jnp.float32),
            pltpu.VMEM((2, clips, feats), jnp.bfloat16),
            pltpu.VMEM((2, clips, LANES), jnp.float32),
            pltpu.SemaphoreType.DMA((3,)),
        ],
        compiler_params=params(24),
        name="scores",
    )(*[pltpu.with_memory_space_constraint(x, pltpu.HBM) for x in (slow, fast, protos)])


def row_kernel(protos_all, extra, t_ref, den_ref, *refs):
    col_parts, (row_ref, r_ref, acc_s) = refs[:-3], refs[-3:]
    clips, count = t_ref.shape[1:]
    groups, lines = clips // LANES, count // LANES
    r_ref[...] = 1.0 / (float(protos_all) * sum_of(col_parts))
    if extra:
        row_ref[2 * groups :, :] = den_ref[...]
    for v in range(2):

        def step(i, _, v=v):
            rows = pl.ds(pl.multiple_of(i * LANES, LANES), LANES)
            acc = jnp.zeros((LANES, LANES), jnp.float32)
            for j in range(lines):
                t = t_ref[v, rows, j * LANES : (j + 1) * LANES]
                acc = acc + t * t * r_ref[v * lines + j : v * lines + j + 1, :]
            acc_s[pl.ds(pl.multiple_of((v * groups + i) * LANES, LANES), LANES), :] = acc
            return 0

        lax.fori_loop(0, groups, step, 0)
    for line in range(2 * groups):
        row_ref[line : line + 1, :] = to_line(acc_s[line * LANES : (line + 1) * LANES, :])


def row_pass(t, den, col_parts, protos_all, extra):
    clips, count = t.shape[1:]
    lines = 2 * clips // LANES * (2 if extra else 1)
    return pl.pallas_call(
        functools.partial(row_kernel, protos_all, extra),
        out_shape=(
            jax.ShapeDtypeStruct((lines, LANES), jnp.float32),
            jax.ShapeDtypeStruct((2 * count // LANES, LANES), jnp.float32),
        ),
        in_specs=[vmem_spec()] * (2 + len(col_parts)),
        out_specs=(vmem_spec(),) * 2,
        scratch_shapes=[pltpu.VMEM((2 * clips, LANES), jnp.float32)],
        compiler_params=params(8),
        name="row_pass",
    )(pltpu.with_memory_space_constraint(t, pltpu.VMEM), den, *col_parts)


def col_kernel(clips_all, t_ref, *refs):
    row_parts, (col_ref, acc_s, s_s) = refs[:-3], refs[-3:]
    clips, count = t_ref.shape[1:]
    groups, lines = clips // LANES, count // LANES
    s_s[...] = 1.0 / (float(clips_all) * sum_of(row_parts, 0, 2 * groups))
    acc_s[...] = jnp.zeros_like(acc_s)
    for v in range(2):

        def step(i, _, v=v):
            rows = pl.ds(pl.multiple_of(i * LANES, LANES), LANES)
            scale = to_columns(s_s[pl.ds(v * groups + i, 1), :])
            for j in range(lines):
                span = slice(j * LANES, (j + 1) * LANES)
                t = t_ref[v, rows, span]
                acc_s[v, :, span] += row_fold(t * t * scale)
            return 0

        lax.fori_loop(0, groups, step, 0)
        for j in range(lines):
            col_ref[v * lines + j : v * lines + j + 1, :] = jnp.sum(
                acc_s[v, :, j * LANES : (j + 1) * LANES], axis=0, keepdims=True
            )


def col_pass(t, row_parts, clips_all):
    clips, count = t.shape[1:]
    return pl.pallas_call(
        functools.partial(col_kernel, clips_all),
        out_shape=jax.ShapeDtypeStruct((2 * count // LANES, LANES), jnp.float32),
        in_specs=[vmem_spec()] * (1 + len(row_parts)),
        out_specs=vmem_spec(),
        scratch_shapes=[
            pltpu.VMEM((2, 8, count), jnp.float32),
            pltpu.VMEM((2 * clips // LANES, LANES), jnp.float32),
        ],
        compiler_params=params(8),
        name="col_pass",
    )(pltpu.with_memory_space_constraint(t, pltpu.VMEM), *row_parts)


def piece_of(position, order):
    steps = len(order)
    return sum(((position >> (steps - 1 - j)) & 1) << bit for j, bit in enumerate(order))


def place_of(piece, order):
    steps = len(order)
    return sum(((piece >> bit) & 1) << (steps - 1 - j) for j, bit in enumerate(order))


def grad_kernel(batch_orders, proto_orders, parts, t_ref, r_ref, ubt_ref, cb_ref, *refs):
    row_parts, den_parts = refs[:parts], refs[parts : 2 * parts]
    send_ref, keep_ref = refs[2 * parts : 2 * parts + 2]
    du_refs = refs[2 * parts + 2 : 2 * parts + 6]
    g_s, odd_s, even_s, code_s, prob_s = refs[2 * parts + 6 :]
    clips, count = t_ref.shape[1:]
    groups, lines = clips // LANES, count // LANES
    pieces = 1 << len(batch_orders[0])
    width = count // (2 * pieces)
    half = width // 2
    code = (1.0 / TEMPER) / sum_of(row_parts, 0, 2 * groups)
    prob = (1.0 / TEMPER) / sum_of(den_parts, 2 * groups, 2 * groups)
    for v in range(2):
        for i in range(groups):
            line = v * groups + i
            rows = slice(i * LANES, (i + 1) * LANES)
            code_s[v, rows, :] = to_columns(code[line : line + 1, :])
            prob_s[v, rows, :] = to_columns(prob[line : line + 1, :])

    def score_grads(m, chunk_s):
        which = jnp.bitwise_xor(lax.axis_index("batch"), m)
        first = pl.multiple_of(which * width, width)
        for i in range(0, clips, 32):
            rows = slice(i, i + 32)
            codes = [code_s[v, rows, :] for v in range(2)]
            probs = [prob_s[v, rows, :] for v in range(2)]
            for h in range(width // LANES):
                span = pl.ds(first + h * LANES, LANES)
                line = which * (width // LANES) + h
                t = [t_ref[v, rows, span] for v in range(2)]
                q = [
                    t[v] * t[v] * r_ref[pl.ds(v * lines + line, 1), :] * codes[v]
                    for v in range(2)
                ]
                for v in range(2):
                    g = (t[v] * probs[v] - q[1 - v]).astype(jnp.bfloat16)
                    g_s[v, rows, span] = g
                    chunk_s[v * clips + i : v * clips + i + 32, h * LANES : (h + 1) * LANES] = g

    def proto_grads(i, chunk_s, out_ref):
        dct = jnp.dot(ubt_ref[...], chunk_s[...], preferred_element_type=jnp.float32)
        dc = dct.T
        for h in range(2):
            place = place_of(i, batch_orders[h])
            out_ref[h, place] = dc[h * half : (h + 1) * half]

    even_s[...] = jnp.zeros_like(even_s)

    def pair(i, _):
        score_grads(2 * i + 1, odd_s)
        proto_grads(jnp.maximum(i - 1, 0), even_s, keep_ref)
        score_grads(2 * i, even_s)
        proto_grads(i, odd_s, send_ref)
        return 0

    lax.fori_loop(0, pieces, pair, 0)
    proto_grads(pieces - 1, even_s, keep_ref)

    peers = 1 << len(proto_orders[0])
    size = clips // peers
    for v in range(2):
        for place in range(peers):
            which = jnp.bitwise_xor(lax.axis_index("proto"), piece_of(place, proto_orders[v]))
            rows = pl.ds(pl.multiple_of(which * size, size), size)
            out_ref = du_refs[2 * v + (0 if place >= peers // 2 else 1)]
            out_ref[place % (peers // 2)] = jnp.dot(
                g_s[v, rows, :], cb_ref[...], preferred_element_type=jnp.float32
            )


def gradients(t, r, ubt, cb, row_parts, den_parts, batch_orders, proto_orders):
    clips, count = t.shape[1:]
    feats = cb.shape[1]
    pieces, peers = 1 << len(batch_orders[0]), 1 << len(proto_orders[0])
    width = count // (2 * pieces)
    proto_share = jax.ShapeDtypeStruct((2, pieces, width // 2, feats), jnp.float32)
    embed_share = jax.ShapeDtypeStruct((peers // 2, clips // peers, feats), jnp.float32)
    return pl.pallas_call(
        functools.partial(grad_kernel, batch_orders, proto_orders, len(row_parts)),
        out_shape=(proto_share,) * 2 + (embed_share,) * 4,
        in_specs=[vmem_spec()] * (4 + 2 * len(row_parts)),
        out_specs=(vmem_spec(),) * 6,
        scratch_shapes=[
            pltpu.VMEM((2, clips, count), jnp.bfloat16),
            pltpu.VMEM((2 * clips, width), jnp.bfloat16),
            pltpu.VMEM((2 * clips, width), jnp.bfloat16),
            pltpu.VMEM((2, clips, LANES), jnp.float32),
            pltpu.VMEM((2, clips, LANES), jnp.float32),
        ],
        compiler_params=params(24),
        name="gradients",
    )(
        pltpu.with_memory_space_constraint(t, pltpu.VMEM),
        r,
        ubt,
        cb,
        *row_parts,
        *den_parts,
    )


def split_add_kernel(plan, inputs, *refs):
    ins, outs = refs[:inputs], refs[inputs:]
    for n, (keep_place, recv_place, part) in enumerate(plan):
        keep, recv = ins[keep_place], ins[recv_place]
        if part is not None:
            keep, recv = keep.at[part], recv.at[part]
        send_out, keep_out = outs[2 * n : 2 * n + 2]
        half = keep_out.shape[0]
        keep_out[...] = keep[:half] + recv[:half]
        send_out[...] = keep[half:] + recv[half:]


def split_add(arrays, plan):
    halves = []
    for place, _, part in plan:
        shape = arrays[place].shape if part is None else arrays[place].shape[1:]
        halves += [jax.ShapeDtypeStruct((shape[0] // 2,) + shape[1:], jnp.float32)] * 2
    outs = pl.pallas_call(
        functools.partial(split_add_kernel, plan, len(arrays)),
        out_shape=tuple(halves),
        in_specs=[vmem_spec()] * len(arrays),
        out_specs=(vmem_spec(),) * len(halves),
        compiler_params=params(12),
        name="split_add",
    )(*arrays)
    return [(outs[2 * n], outs[2 * n + 1]) for n in range(len(plan))]


def project(raw, terms):
    x = raw.astype(jnp.float32)
    length = jnp.sqrt(jnp.sum(x * x, axis=-1, keepdims=True) + 1e-12)
    unit = x / length
    grad = terms[0][0] + terms[1][0]
    along = jnp.sum(unit * grad, axis=-1, keepdims=True)
    return (grad - unit * along) / length


EXTRA = 8


def share_kernel(proto_raw, slow_raw, fast_raw, *refs):
    terms, (proto_out, embed_out, square_out) = refs[:-3], refs[-3:]
    half = proto_raw.shape[0] // 2
    squares = [jnp.zeros((8, LANES), jnp.float32)] * 2
    for h in range(2):
        rows = slice(h * half, (h + 1) * half)
        grad = project(proto_raw[rows, :], terms[2 * h : 2 * h + 2])
        proto_out[rows, :] = grad
        squares[0] = squares[0] + row_fold(lane_sum(grad * grad))
    for v, raw in enumerate((slow_raw, fast_raw)):
        grad = project(raw[...], terms[4 + 2 * v : 6 + 2 * v])
        embed_out[v] = grad
        squares[1] = squares[1] + row_fold(lane_sum(grad * grad))
    for kind in range(2):
        total = jnp.sum(jnp.sum(squares[kind], axis=0, keepdims=True), axis=1, keepdims=True)
        square_out[kind] = jnp.broadcast_to(total, (8, LANES))


def project_shares(raws, terms):
    rows, feats = raws[1].shape
    return pl.pallas_call(
        share_kernel,
        out_shape=(
            jax.ShapeDtypeStruct(raws[0].shape, jnp.float32),
            jax.ShapeDtypeStruct((2, rows, feats), jnp.float32),
            jax.ShapeDtypeStruct((2, 8, LANES), jnp.float32),
        ),
        in_specs=[vmem_spec()] * (len(raws) + len(terms)),
        out_specs=(vmem_spec(),) * 3,
        compiler_params=params(10),
        name="project_shares",
    )(*raws, *terms)


def tree_sum(terms):
    while len(terms) > 1:
        terms = [terms[i] + terms[i + 1] for i in range(0, len(terms), 2)]
    return terms[0]


def pack_kernel(proto_ref, embed_ref, *refs):
    squares, (proto_out, embed_out) = refs[:-2], refs[-2:]
    rows = proto_ref.shape[0]
    total = tree_sum([square[...] for square in squares])
    proto_out[:rows, :] = proto_ref[...]
    for kind in range(2):
        proto_out[rows:, kind * LANES : (kind + 1) * LANES] = total[kind]
    embed_out[...] = embed_ref[...]


def pack_shares(grad_proto, grad_embed, squares):
    rows, feats = grad_proto.shape
    return pl.pallas_call(
        pack_kernel,
        out_shape=(
            jax.ShapeDtypeStruct((rows + EXTRA, feats), jnp.float32),
            jax.ShapeDtypeStruct(grad_embed.shape, jnp.float32),
        ),
        in_specs=[vmem_spec()] * (2 + len(squares)),
        out_specs=(vmem_spec(),) * 2,
        compiler_params=params(10),
        name="pack_shares",
    )(grad_proto, grad_embed, *squares)


def total_square(refs, kind):
    lanes = slice(kind * LANES, (kind + 1) * LANES)
    return tree_sum([ref[ref.shape[0] - EXTRA :, lanes] for ref in refs])[0:1, 0:1]


def finish_protos_kernel(entries, *refs):
    pieces, out_ref = refs[:-1], refs[-1]
    factor = lax.rsqrt(total_square(pieces, 0) / entries + NORM_EPS)
    size = pieces[0].shape[0] - EXTRA
    for m, piece in enumerate(pieces):
        which = jnp.bitwise_xor(lax.axis_index("batch"), m)
        out_ref[pl.ds(pl.multiple_of(which * size, size), size), :] = piece[:size, :] * factor


def finish_protos(entries, pieces):
    rows, feats = pieces[0].shape
    return pl.pallas_call(
        functools.partial(finish_protos_kernel, entries),
        out_shape=jax.ShapeDtypeStruct((len(pieces) * (rows - EXTRA), feats), jnp.float32),
        in_specs=[vmem_spec()] * len(pieces),
        out_specs=vmem_spec(),
        compiler_params=params(12),
        name="finish_protos",
    )(*pieces)


def finish_embeds_kernel(entries, plan, count, *refs):
    pieces, ins, outs = refs[:count], refs[count:-2], refs[-2:]
    factor = lax.rsqrt(total_square(pieces, 1) / entries + NORM_EPS)
    for v, places in enumerate(plan):
        for m, (place, view) in enumerate(places):
            src = ins[place][...] if view is None else ins[place][view]
            size = src.shape[0]
            which = jnp.bitwise_xor(lax.axis_index("proto"), m)
            outs[v][pl.ds(pl.multiple_of(which * size, size), size), :] = src * factor


def finish_embeds(entries, pieces, groups):
    arrays, plan, outs = [], [], []
    for group in groups:
        places = []
        for array, view in group:
            place = next((i for i, known in enumerate(arrays) if known is array), None)
            if place is None:
                place = len(arrays)
                arrays.append(array)
            places.append((place, view))
        plan.append(places)
        rows, feats = group[0][0].shape[-2:]
        outs.append(jax.ShapeDtypeStruct((len(group) * rows, feats), jnp.float32))
    return pl.pallas_call(
        functools.partial(finish_embeds_kernel, entries, plan, len(pieces)),
        out_shape=tuple(outs),
        in_specs=[vmem_spec()] * (len(pieces) + len(arrays)),
        out_specs=(vmem_spec(),) * len(groups),
        compiler_params=params(12),
        name="finish_embeds",
    )(*pieces, *arrays)


def swap(own, axis, mask):
    return lax.ppermute(own, axis, [(i, i ^ mask) for i in range(lax.axis_size(axis))])


def bits_of(axis):
    count = lax.axis_size(axis)
    bits = count.bit_length() - 1
    if count != 1 << bits:
        raise ValueError("axis size")
    return bits


def proto_parts(own):
    return [own] + [swap(own, "proto", m) for m in range(1, lax.axis_size("proto"))]


def batch_parts(own):
    pair = own + swap(own, "batch", 1)
    return [pair] + [swap(pair, "batch", 2 * m) for m in range(1, lax.axis_size("batch") // 2)]


def scatter_sums(groups):
    stage, terms = 0, [None] * len(groups)
    state = list(groups)
    while any(term is None for term in terms):
        live = [n for n in range(len(state)) if terms[n] is None]
        recvs = {}
        for n in live:
            axis, order, send, keep = state[n]
            recvs[n] = swap(send, axis, 1 << order[stage])
        going = []
        for n in live:
            axis, order, send, keep = state[n]
            if stage + 1 == len(order):
                terms[n] = (keep, recvs[n])
            else:
                going.append(n)
        if going:
            arrays = [x for n in going for x in (state[n][3], recvs[n])]
            split = split_add(arrays, [(2 * i, 2 * i + 1, None) for i in range(len(going))])
            for n, (send, keep) in zip(going, split):
                state[n] = (state[n][0], state[n][1], send, keep)
        stage += 1
    return [x for term in terms for x in term]


def gather_batch(own):
    bits = list(reversed(range(lax.axis_size("batch").bit_length() - 1)))
    pieces = {0: own}
    first = {bit: swap(own, "batch", 1 << bit) for bit in bits}
    for bit in bits:
        for m in list(pieces):
            pieces[m | 1 << bit] = first[bit] if m == 0 else swap(pieces[m], "batch", 1 << bit)
    return [pieces[m] for m in range(len(pieces))]


def gather_views(own, orders):
    first = {bit: swap(own, "proto", 1 << bit) for bit in sorted(orders[0])}
    groups = []
    for v, order in enumerate(orders):
        pieces = {0: (own, v)}
        for bit in order:
            for m in list(pieces):
                if m == 0:
                    pieces[1 << bit] = (first[bit], v)
                else:
                    array, view = pieces[m]
                    piece = array if view is None else array[view]
                    pieces[m | 1 << bit] = (swap(piece, "proto", 1 << bit), None)
        groups.append([pieces[m] for m in range(len(pieces))])
    return groups


def body(slow_embed, fast_embed, prototypes):
    clip_dev, feat_width = slow_embed.shape
    proto_dev = prototypes.shape[0]
    batch_count = lax.axis_size("batch")
    proto_count = lax.axis_size("proto")
    clips_all = clip_dev * batch_count
    protos_all = proto_dev * proto_count
    proto_entries = float(protos_all * feat_width)
    embed_entries = float(2 * clips_all * feat_width)
    batch_bits, proto_bits = bits_of("batch"), bits_of("proto")
    me_batch, me_proto = lax.axis_index("batch"), lax.axis_index("proto")

    t, col, den, unit_bt, proto_b = scores(slow_embed, fast_embed, prototypes)
    for iteration in range(ITERS):
        rows, r = row_pass(t, den, batch_parts(col), protos_all, iteration == 0)
        row_parts = proto_parts(rows)
        if iteration == 0:
            den_parts = row_parts
        if iteration + 1 < ITERS:
            col = col_pass(t, row_parts, clips_all)

    near = tuple(range(batch_bits - 1))
    batch_orders = (near, tuple(reversed(near)))
    proto_orders = (tuple(range(proto_bits)), tuple(reversed(range(proto_bits))))
    send, keep, *shares = gradients(
        t, r, unit_bt, proto_b, row_parts, den_parts, batch_orders, proto_orders
    )

    proto_rows = proto_dev // batch_count
    clip_rows = clip_dev // proto_count
    raws = [lax.dynamic_slice_in_dim(prototypes, me_batch * proto_rows, proto_rows, 0)]
    for x in (slow_embed, fast_embed):
        raws.append(lax.dynamic_slice_in_dim(x, me_proto * clip_rows, clip_rows, 0))
    recv = swap(send, "batch", 1)
    halves = split_add([keep, recv], [(0, 1, h) for h in range(2)])
    groups = []
    for h in range(2):
        order = tuple(bit + 1 for bit in batch_orders[h])
        groups.append(("batch", order) + tuple(halves[h]))
    for v in range(2):
        groups.append(("proto", proto_orders[v], shares[2 * v], shares[2 * v + 1]))
    terms = scatter_sums(groups)
    grad_proto, grad_embed, square = project_shares(raws, terms)
    packed, grad_embed = pack_shares(grad_proto, grad_embed, proto_parts(square))
    proto_pieces = gather_batch(packed)
    view_pieces = gather_views(grad_embed, (proto_orders[1], proto_orders[0]))
    proto_grad = finish_protos(proto_entries, proto_pieces)
    slow_grad, fast_grad = finish_embeds(embed_entries, proto_pieces, view_pieces)
    return proto_grad, slow_grad, fast_grad


def solution(mesh):
    placed = (P("batch", None), P("batch", None), P("proto", None))
    return jax.shard_map(
        body,
        mesh=mesh,
        in_specs=placed,
        out_specs=(P("proto", None), P("batch", None), P("batch", None)),
        check_vma=False,
    )
```

```python
import functools

import jax
import jax.numpy as jnp
from jax import lax
from jax.experimental import pallas as pl
from jax.experimental.pallas import tpu as pltpu
from jax.sharding import PartitionSpec as P

ITERS = 3


CODE_EPS = 0.05
TEMPER = 0.1
NORM_EPS = 1e-06
LANES = 128
MIB = 1024 * 1024


def vmem_spec():
    return pl.BlockSpec(memory_space=pltpu.VMEM)


def params(limit):
    return pltpu.CompilerParams(vmem_limit_bytes=limit * MIB)


def to_columns(line):
    return jnp.broadcast_to(line, (LANES, LANES)).T


def to_line(partial):
    return jnp.sum(partial.T, axis=0, keepdims=True)


def lane_sum(block):
    total = block[:, :LANES]
    for j in range(1, block.shape[1] // LANES):
        total = total + block[:, j * LANES : (j + 1) * LANES]
    return total


def row_fold(block):
    return jnp.sum(block.reshape(block.shape[0] // 8, 8, block.shape[1]), axis=0)


def sum_of(refs, first=0, size=None):
    size = refs[0].shape[0] if size is None else size
    total = refs[0][first : first + size, :]
    for ref in refs[1:]:
        total = total + ref[first : first + size, :]
    return total


LOG2E = 1.4426950408889634


def score_kernel(slow, fast, protos, t_ref, col_ref, den_ref, ubt_ref, cb_ref, raw_s, w_s, ub_s, den_s, sems):
    clips, feats = slow.shape
    count = protos.shape[0]
    loads = []
    for v, src in enumerate((slow, fast)):
        loads.append(pltpu.make_async_copy(src, raw_s.at[v], sems.at[v]))
    loads.append(pltpu.make_async_copy(protos, w_s, sems.at[2]))
    for load in loads:
        load.start()
    for v in range(2):
        loads[v].wait()
        for first in range(0, clips, 256):
            rows = pl.ds(first, 256)
            x = raw_s[v, rows, :].astype(jnp.float32)
            length = jnp.sqrt(jnp.sum(x * x, axis=-1, keepdims=True) + 1e-12)
            u = x / length
            ub_s[v, rows, :] = u.astype(jnp.bfloat16)
            ubt_ref[:, v * clips + first : v * clips + first + 256] = u.T.astype(jnp.bfloat16)
    den_s[...] = jnp.zeros_like(den_s)
    loads[2].wait()

    def chunk(j, _):
        first = pl.multiple_of(j * 256, 256)
        w = w_s[pl.ds(first, 256), :]
        length = jnp.sqrt(jnp.sum(w * w, axis=-1, keepdims=True) + 1e-12)
        c = w / length
        cb_ref[pl.ds(first, 256), :] = c.astype(jnp.bfloat16)
        weights = c.T.astype(jnp.bfloat16)
        for v in range(2):
            cols = jnp.zeros((8, 256), jnp.float32)
            for r in range(0, clips, 512):
                s = jnp.dot(
                    ub_s[v, r : r + 512, :], weights, preferred_element_type=jnp.float32
                )
                for q in range(0, 512, 64):
                    rows = pl.ds(r + q, 64)
                    t = jnp.exp2(s[q : q + 64] * (LOG2E / TEMPER))
                    t_ref[v, rows, pl.ds(first, 256)] = t
                    cols = cols + row_fold(t * t)
                    den_s[v, rows, :] += lane_sum(t)
            line = jnp.sum(cols, axis=0, keepdims=True)
            for h in range(2):
                col_ref[pl.ds(v * (count // LANES) + j * 2 + h, 1), :] = line[
                    :, h * LANES : (h + 1) * LANES
                ]
        return 0

    lax.fori_loop(0, count // 256, chunk, 0)
    groups = clips // LANES
    for v in range(2):
        for i in range(groups):
            den_ref[pl.ds(v * groups + i, 1), :] = to_line(den_s[v, i * LANES : (i + 1) * LANES, :])


def scores(slow, fast, protos):
    clips, feats = slow.shape
    count = protos.shape[0]
    return pl.pallas_call(
        score_kernel,
        out_shape=(
            pltpu.VMEM((2, clips, count), jnp.float32),
            jax.ShapeDtypeStruct((2 * count // LANES, LANES), jnp.float32),
            jax.ShapeDtypeStruct((2 * clips // LANES, LANES), jnp.float32),
            jax.ShapeDtypeStruct((feats, 2 * clips), jnp.bfloat16),
            jax.ShapeDtypeStruct((count, feats), jnp.bfloat16),
        ),
        in_specs=[pl.BlockSpec(memory_space=pltpu.HBM)] * 3,
        out_specs=(vmem_spec(),) * 5,
        scratch_shapes=[
            pltpu.VMEM((2, clips, feats), jnp.bfloat16),
            pltpu.VMEM((count, feats), jnp.float32),
            pltpu.VMEM((2, clips, feats), jnp.bfloat16),
            pltpu.VMEM((2, clips, LANES), jnp.float32),
            pltpu.SemaphoreType.DMA((3,)),
        ],
        compiler_params=params(24),
        name="scores",
    )(*[pltpu.with_memory_space_constraint(x, pltpu.HBM) for x in (slow, fast, protos)])


def row_kernel(protos_all, extra, t_ref, den_ref, *refs):
    col_parts, (row_ref, r_ref, acc_s) = refs[:-3], refs[-3:]
    clips, count = t_ref.shape[1:]
    groups, lines = clips // LANES, count // LANES
    r_ref[...] = 1.0 / (float(protos_all) * sum_of(col_parts))
    if extra:
        row_ref[2 * groups :, :] = den_ref[...]
    for v in range(2):

        def step(i, _, v=v):
            rows = pl.ds(pl.multiple_of(i * LANES, LANES), LANES)
            acc = jnp.zeros((LANES, LANES), jnp.float32)
            for j in range(lines):
                t = t_ref[v, rows, j * LANES : (j + 1) * LANES]
                acc = acc + t * t * r_ref[v * lines + j : v * lines + j + 1, :]
            acc_s[pl.ds(pl.multiple_of((v * groups + i) * LANES, LANES), LANES), :] = acc
            return 0

        lax.fori_loop(0, groups, step, 0)
    for line in range(2 * groups):
        row_ref[line : line + 1, :] = to_line(acc_s[line * LANES : (line + 1) * LANES, :])


def row_pass(t, den, col_parts, protos_all, extra):
    clips, count = t.shape[1:]
    lines = 2 * clips // LANES * (2 if extra else 1)
    return pl.pallas_call(
        functools.partial(row_kernel, protos_all, extra),
        out_shape=(
            jax.ShapeDtypeStruct((lines, LANES), jnp.float32),
            jax.ShapeDtypeStruct((2 * count // LANES, LANES), jnp.float32),
        ),
        in_specs=[vmem_spec()] * (2 + len(col_parts)),
        out_specs=(vmem_spec(),) * 2,
        scratch_shapes=[pltpu.VMEM((2 * clips, LANES), jnp.float32)],
        compiler_params=params(8),
        name="row_pass",
    )(pltpu.with_memory_space_constraint(t, pltpu.VMEM), den, *col_parts)


def col_kernel(clips_all, t_ref, *refs):
    row_parts, (col_ref, acc_s, s_s) = refs[:-3], refs[-3:]
    clips, count = t_ref.shape[1:]
    groups, lines = clips // LANES, count // LANES
    s_s[...] = 1.0 / (float(clips_all) * sum_of(row_parts, 0, 2 * groups))
    acc_s[...] = jnp.zeros_like(acc_s)
    for v in range(2):

        def step(i, _, v=v):
            rows = pl.ds(pl.multiple_of(i * LANES, LANES), LANES)
            scale = to_columns(s_s[pl.ds(v * groups + i, 1), :])
            for j in range(lines):
                span = slice(j * LANES, (j + 1) * LANES)
                t = t_ref[v, rows, span]
                acc_s[v, :, span] += row_fold(t * t * scale)
            return 0

        lax.fori_loop(0, groups, step, 0)
        for j in range(lines):
            col_ref[v * lines + j : v * lines + j + 1, :] = jnp.sum(
                acc_s[v, :, j * LANES : (j + 1) * LANES], axis=0, keepdims=True
            )


def col_pass(t, row_parts, clips_all):
    clips, count = t.shape[1:]
    return pl.pallas_call(
        functools.partial(col_kernel, clips_all),
        out_shape=jax.ShapeDtypeStruct((2 * count // LANES, LANES), jnp.float32),
        in_specs=[vmem_spec()] * (1 + len(row_parts)),
        out_specs=vmem_spec(),
        scratch_shapes=[
            pltpu.VMEM((2, 8, count), jnp.float32),
            pltpu.VMEM((2 * clips // LANES, LANES), jnp.float32),
        ],
        compiler_params=params(8),
        name="col_pass",
    )(pltpu.with_memory_space_constraint(t, pltpu.VMEM), *row_parts)


def piece_of(position, order):
    steps = len(order)
    return sum(((position >> (steps - 1 - j)) & 1) << bit for j, bit in enumerate(order))


def place_of(piece, order):
    steps = len(order)
    return sum(((piece >> bit) & 1) << (steps - 1 - j) for j, bit in enumerate(order))


def chunk_span(m, width):
    which = jnp.bitwise_xor(lax.axis_index("batch"), m)
    return which, pl.multiple_of(which * width, width)


def proto_grads(ubt, chunk, orders, i, out_ref):
    dc = jnp.dot(ubt, chunk, preferred_element_type=jnp.float32).T
    half = dc.shape[0] // 2
    for h in range(2):
        out_ref[h, place_of(i, orders[h])] = dc[h * half : (h + 1) * half]


def send_kernel(orders, parts, t_ref, r_ref, ubt_ref, *refs):
    row_parts, den_parts = refs[:parts], refs[parts : 2 * parts]
    send_ref, g_ref, chunk_s, code_s, prob_s = refs[2 * parts :]
    clips, count = t_ref.shape[1:]
    groups, lines = clips // LANES, count // LANES
    pieces = 1 << len(orders[0])
    width = count // (2 * pieces)
    code = (1.0 / TEMPER) / sum_of(row_parts, 0, 2 * groups)
    prob = (1.0 / TEMPER) / sum_of(den_parts, 2 * groups, 2 * groups)
    for v in range(2):
        for i in range(groups):
            line = v * groups + i
            rows = slice(i * LANES, (i + 1) * LANES)
            code_s[v, rows, :] = to_columns(code[line : line + 1, :])
            prob_s[v, rows, :] = to_columns(prob[line : line + 1, :])

    def score_grads(m, keep_chunk):
        which, first = chunk_span(m, width)
        for i in range(0, clips, 32):
            rows = slice(i, i + 32)
            codes = [code_s[v, rows, :] for v in range(2)]
            probs = [prob_s[v, rows, :] for v in range(2)]
            for h in range(width // LANES):
                span = pl.ds(first + h * LANES, LANES)
                line = which * (width // LANES) + h
                t = [t_ref[v, rows, span] for v in range(2)]
                q = [
                    t[v] * t[v] * r_ref[pl.ds(v * lines + line, 1), :] * codes[v]
                    for v in range(2)
                ]
                for v in range(2):
                    g = (t[v] * probs[v] - q[1 - v]).astype(jnp.bfloat16)
                    own = slice(v * clips + i, v * clips + i + 32)
                    g_ref[own, span] = g
                    if keep_chunk:
                        chunk_s[own, h * LANES : (h + 1) * LANES] = g

    def pair(i, _):
        score_grads(2 * i + 1, True)
        score_grads(2 * i, False)
        proto_grads(ubt_ref[...], chunk_s[...], orders, i, send_ref)
        return 0

    lax.fori_loop(0, pieces, pair, 0)


def send_gradients(t, r, ubt, row_parts, den_parts, orders):
    clips, count = t.shape[1:]
    feats = ubt.shape[0]
    pieces = 1 << len(orders[0])
    width = count // (2 * pieces)
    return pl.pallas_call(
        functools.partial(send_kernel, orders, len(row_parts)),
        out_shape=(
            jax.ShapeDtypeStruct((2, pieces, width // 2, feats), jnp.float32),
            pltpu.VMEM((2 * clips, count), jnp.bfloat16),
        ),
        in_specs=[vmem_spec()] * (3 + 2 * len(row_parts)),
        out_specs=(vmem_spec(),) * 2,
        scratch_shapes=[
            pltpu.VMEM((2 * clips, width), jnp.bfloat16),
            pltpu.VMEM((2, clips, LANES), jnp.float32),
            pltpu.VMEM((2, clips, LANES), jnp.float32),
        ],
        compiler_params=params(14),
        cost_estimate=pl.CostEstimate(
            flops=2 * clips * count * feats, bytes_accessed=20 * MIB, transcendentals=0
        ),
        name="send_gradients",
    )(pltpu.with_memory_space_constraint(t, pltpu.VMEM), r, ubt, *row_parts, *den_parts)


def embed_grad_kernel(orders, g_ref, cb_ref, *outs):
    clips = g_ref.shape[0] // 2
    peers = 1 << len(orders[0])
    size = clips // peers
    for v in range(2):
        for place in range(peers):
            which = jnp.bitwise_xor(lax.axis_index("proto"), piece_of(place, orders[v]))
            rows = pl.ds(pl.multiple_of(v * clips + which * size, size), size)
            out_ref = outs[2 * v + (0 if place >= peers // 2 else 1)]
            out_ref[place % (peers // 2)] = jnp.dot(
                g_ref[rows, :], cb_ref[...], preferred_element_type=jnp.float32
            )


def embed_gradients(g, cb, orders):
    clips, count = g.shape[0] // 2, g.shape[1]
    feats = cb.shape[1]
    peers = 1 << len(orders[0])
    share = jax.ShapeDtypeStruct((peers // 2, clips // peers, feats), jnp.float32)
    return pl.pallas_call(
        functools.partial(embed_grad_kernel, orders),
        out_shape=(share,) * 4,
        in_specs=[vmem_spec()] * 2,
        out_specs=(vmem_spec(),) * 4,
        compiler_params=params(14),
        cost_estimate=pl.CostEstimate(
            flops=4 * clips * count * feats, bytes_accessed=11 * MIB, transcendentals=0
        ),
        name="embed_gradients",
    )(pltpu.with_memory_space_constraint(g, pltpu.VMEM), cb)


def keep_kernel(orders, g_ref, ubt_ref, after_ref, keep_ref):
    pieces = 1 << len(orders[0])
    width = g_ref.shape[1] // (2 * pieces)

    def step(i, _):
        _, first = chunk_span(2 * i, width)
        proto_grads(ubt_ref[...], g_ref[:, pl.ds(first, width)], orders, i, keep_ref)
        return 0

    lax.fori_loop(0, pieces, step, 0)


def keep_gradients(g, ubt, after, orders):
    count = g.shape[1]
    feats, clips = ubt.shape
    pieces = 1 << len(orders[0])
    return pl.pallas_call(
        functools.partial(keep_kernel, orders),
        out_shape=jax.ShapeDtypeStruct((2, pieces, count // (4 * pieces), feats), jnp.float32),
        in_specs=[vmem_spec()] * 2 + [pl.BlockSpec(memory_space=pl.ANY)],
        out_specs=vmem_spec(),
        compiler_params=params(14),
        cost_estimate=pl.CostEstimate(
            flops=clips * count * feats, bytes_accessed=6 * MIB, transcendentals=0
        ),
        name="keep_gradients",
    )(pltpu.with_memory_space_constraint(g, pltpu.VMEM), ubt, after)


def split_add_kernel(plan, inputs, *refs):
    ins, outs = refs[:inputs], refs[inputs:]
    for n, (keep_place, recv_place, part) in enumerate(plan):
        keep, recv = ins[keep_place], ins[recv_place]
        if part is not None:
            keep, recv = keep.at[part], recv.at[part]
        send_out, keep_out = outs[2 * n : 2 * n + 2]
        half = keep_out.shape[0]
        keep_out[...] = keep[:half] + recv[:half]
        send_out[...] = keep[half:] + recv[half:]


def split_add(arrays, plan):
    halves = []
    for place, _, part in plan:
        shape = arrays[place].shape if part is None else arrays[place].shape[1:]
        halves += [jax.ShapeDtypeStruct((shape[0] // 2,) + shape[1:], jnp.float32)] * 2
    outs = pl.pallas_call(
        functools.partial(split_add_kernel, plan, len(arrays)),
        out_shape=tuple(halves),
        in_specs=[vmem_spec()] * len(arrays),
        out_specs=(vmem_spec(),) * len(halves),
        compiler_params=params(12),
        name="split_add",
    )(*arrays)
    return [(outs[2 * n], outs[2 * n + 1]) for n in range(len(plan))]


def project(raw, terms):
    x = raw.astype(jnp.float32)
    length = jnp.sqrt(jnp.sum(x * x, axis=-1, keepdims=True) + 1e-12)
    unit = x / length
    grad = terms[0][0] + terms[1][0]
    along = jnp.sum(unit * grad, axis=-1, keepdims=True)
    return (grad - unit * along) / length


EXTRA = 8


def share_kernel(proto_raw, slow_raw, fast_raw, *refs):
    terms, (proto_out, embed_out) = refs[:-2], refs[-2:]
    count = proto_raw.shape[0]
    half = count // 2
    squares = [jnp.zeros((8, LANES), jnp.float32)] * 2
    for h in range(2):
        rows = slice(h * half, (h + 1) * half)
        grad = project(proto_raw[rows, :], terms[2 * h : 2 * h + 2])
        proto_out[rows, :] = grad
        squares[0] = squares[0] + row_fold(lane_sum(grad * grad))
    for v, raw in enumerate((slow_raw, fast_raw)):
        grad = project(raw[...], terms[4 + 2 * v : 6 + 2 * v])
        embed_out[v] = grad
        squares[1] = squares[1] + row_fold(lane_sum(grad * grad))
    for kind in range(2):
        total = jnp.sum(jnp.sum(squares[kind], axis=0, keepdims=True), axis=1, keepdims=True)
        proto_out[count:, kind * LANES : (kind + 1) * LANES] = jnp.broadcast_to(total, (EXTRA, LANES))


def project_shares(raws, terms):
    rows, feats = raws[1].shape
    count = raws[0].shape[0]
    return pl.pallas_call(
        share_kernel,
        out_shape=(
            jax.ShapeDtypeStruct((count + EXTRA, feats), jnp.float32),
            jax.ShapeDtypeStruct((2, rows, feats), jnp.float32),
        ),
        in_specs=[vmem_spec()] * (len(raws) + len(terms)),
        out_specs=(vmem_spec(),) * 2,
        compiler_params=params(10),
        name="project_shares",
    )(*raws, *terms)


def tree_sum(terms):
    while len(terms) > 1:
        terms = [terms[i] + terms[i + 1] for i in range(0, len(terms), 2)]
    return terms[0]


def squares_kernel(*refs):
    pieces, out_ref = refs[:-1], refs[-1]
    total = tree_sum([piece[piece.shape[0] - EXTRA :, :] for piece in pieces])
    for kind in range(2):
        out_ref[kind] = total[:, kind * LANES : (kind + 1) * LANES]


def sum_squares(pieces):
    return pl.pallas_call(
        squares_kernel,
        out_shape=jax.ShapeDtypeStruct((2, 8, LANES), jnp.float32),
        in_specs=[vmem_spec()] * len(pieces),
        out_specs=vmem_spec(),
        compiler_params=params(8),
        name="sum_squares",
    )(*pieces)


def finish_kernel(entries, plan, counts, *refs):
    squares, protos = refs[: counts[0]], refs[counts[0] : counts[0] + counts[1]]
    ins, outs = refs[counts[0] + counts[1] : -7], refs[-7:-4]
    proto_s, slow_s, fast_s, sems = refs[-4:]
    total = tree_sum([square[...] for square in squares])
    factors = [lax.rsqrt(total[k, 0:1, 0:1] / entries[k] + NORM_EPS) for k in range(2)]
    size = protos[0].shape[0] - EXTRA
    copies = []
    for m, piece in enumerate(protos):
        which = jnp.bitwise_xor(lax.axis_index("batch"), m)
        rows = pl.ds(pl.multiple_of(which * size, size), size)
        proto_s[m] = piece[:size, :] * factors[0]
        copies.append(pltpu.make_async_copy(proto_s.at[m], outs[0].at[rows], sems.at[m]))
        copies[-1].start()
    for v, (places, scaled) in enumerate(zip(plan, (slow_s, fast_s))):
        for m, (place, view) in enumerate(places):
            src = ins[place][...] if view is None else ins[place][view]
            size = src.shape[0]
            which = jnp.bitwise_xor(lax.axis_index("proto"), m)
            rows = pl.ds(pl.multiple_of(which * size, size), size)
            scaled[m] = src * factors[1]
            sem = sems.at[counts[1] + v * len(places) + m]
            copies.append(pltpu.make_async_copy(scaled.at[m], outs[1 + v].at[rows], sem))
            copies[-1].start()
    for copy in copies:
        copy.wait()


def finish(entries, squares, protos, groups):
    arrays, plan = [], []
    rows, feats = protos[0].shape
    scratch = [pltpu.VMEM((len(protos), rows - EXTRA, feats), jnp.float32)]
    outs = [jax.ShapeDtypeStruct((len(protos) * (rows - EXTRA), feats), jnp.float32)]
    for group in groups:
        places = []
        for array, view in group:
            place = next((i for i, known in enumerate(arrays) if known is array), None)
            if place is None:
                place = len(arrays)
                arrays.append(array)
            places.append((place, view))
        plan.append(places)
        rows, feats = group[0][0].shape[-2:]
        scratch.append(pltpu.VMEM((len(group), rows, feats), jnp.float32))
        outs.append(jax.ShapeDtypeStruct((len(group) * rows, feats), jnp.float32))
    count = len(protos) + sum(len(places) for places in plan)
    return pl.pallas_call(
        functools.partial(finish_kernel, entries, plan, (len(squares), len(protos))),
        out_shape=tuple(outs),
        in_specs=[vmem_spec()] * (len(squares) + len(protos) + len(arrays)),
        out_specs=(pl.BlockSpec(memory_space=pltpu.HBM),) * len(outs),
        scratch_shapes=scratch + [pltpu.SemaphoreType.DMA((count,))],
        compiler_params=params(12),
        name="finish",
    )(*squares, *protos, *arrays)


def swap(own, axis, mask):
    return lax.ppermute(own, axis, [(i, i ^ mask) for i in range(lax.axis_size(axis))])


def bits_of(axis):
    count = lax.axis_size(axis)
    bits = count.bit_length() - 1
    if count != 1 << bits:
        raise ValueError("axis size")
    return bits


def proto_parts(own):
    return [own] + [swap(own, "proto", m) for m in range(1, lax.axis_size("proto"))]


def batch_parts(own):
    pair = own + swap(own, "batch", 1)
    return [pair] + [swap(pair, "batch", 2 * m) for m in range(1, lax.axis_size("batch") // 2)]


def scatter_sums(groups):
    stage, terms = 0, [None] * len(groups)
    state = list(groups)
    while any(term is None for term in terms):
        live = [n for n in range(len(state)) if terms[n] is None]
        recvs = {}
        for n in live:
            axis, order, send, keep = state[n]
            recvs[n] = swap(send, axis, 1 << order[stage])
        going = []
        for n in live:
            axis, order, send, keep = state[n]
            if stage + 1 == len(order):
                terms[n] = (keep, recvs[n])
            else:
                going.append(n)
        if going:
            arrays = [x for n in going for x in (state[n][3], recvs[n])]
            split = split_add(arrays, [(2 * i, 2 * i + 1, None) for i in range(len(going))])
            for n, (send, keep) in zip(going, split):
                state[n] = (state[n][0], state[n][1], send, keep)
        stage += 1
    return [x for term in terms for x in term]


def gather_batch(own):
    bits = list(reversed(range(lax.axis_size("batch").bit_length() - 1)))
    pieces = {0: own}
    first = {bit: swap(own, "batch", 1 << bit) for bit in bits}
    for bit in bits:
        for m in list(pieces):
            pieces[m | 1 << bit] = first[bit] if m == 0 else swap(pieces[m], "batch", 1 << bit)
    return [pieces[m] for m in range(len(pieces))]


def gather_views(own, orders):
    first = {bit: swap(own, "proto", 1 << bit) for bit in sorted(orders[0])}
    groups = []
    for v, order in enumerate(orders):
        pieces = {0: (own, v)}
        for bit in order:
            for m in list(pieces):
                if m == 0:
                    pieces[1 << bit] = (first[bit], v)
                else:
                    array, view = pieces[m]
                    piece = array if view is None else array[view]
                    pieces[m | 1 << bit] = (swap(piece, "proto", 1 << bit), None)
        groups.append([pieces[m] for m in range(len(pieces))])
    return groups


def body(slow_embed, fast_embed, prototypes):
    clip_dev, feat_width = slow_embed.shape
    proto_dev = prototypes.shape[0]
    batch_count = lax.axis_size("batch")
    proto_count = lax.axis_size("proto")
    clips_all = clip_dev * batch_count
    protos_all = proto_dev * proto_count
    proto_entries = float(protos_all * feat_width)
    embed_entries = float(2 * clips_all * feat_width)
    batch_bits, proto_bits = bits_of("batch"), bits_of("proto")
    me_batch, me_proto = lax.axis_index("batch"), lax.axis_index("proto")

    t, col, den, unit_bt, proto_b = scores(slow_embed, fast_embed, prototypes)
    for iteration in range(ITERS):
        rows, r = row_pass(t, den, batch_parts(col), protos_all, iteration == 0)
        row_parts = proto_parts(rows)
        if iteration == 0:
            den_parts = row_parts
        if iteration + 1 < ITERS:
            col = col_pass(t, row_parts, clips_all)

    near = tuple(range(batch_bits - 1))
    batch_orders = (near, tuple(reversed(near)))
    proto_orders = (tuple(range(proto_bits)), tuple(reversed(range(proto_bits))))
    send, g = send_gradients(t, r, unit_bt, row_parts, den_parts, batch_orders)
    shares = embed_gradients(g, proto_b, proto_orders)
    keep = keep_gradients(g, unit_bt, shares[0], batch_orders)

    proto_rows = proto_dev // batch_count
    clip_rows = clip_dev // proto_count
    raws = [lax.dynamic_slice_in_dim(prototypes, me_batch * proto_rows, proto_rows, 0)]
    for x in (slow_embed, fast_embed):
        raws.append(lax.dynamic_slice_in_dim(x, me_proto * clip_rows, clip_rows, 0))
    recv = swap(send, "batch", 1)
    halves = split_add([keep, recv], [(0, 1, h) for h in range(2)])
    groups = []
    for h in range(2):
        order = tuple(bit + 1 for bit in batch_orders[h])
        groups.append(("batch", order) + tuple(halves[h]))
    for v in range(2):
        groups.append(("proto", proto_orders[v], shares[2 * v], shares[2 * v + 1]))
    terms = scatter_sums(groups)
    grad_proto, grad_embed = project_shares(raws, terms)
    proto_pieces = gather_batch(grad_proto)
    view_pieces = gather_views(grad_embed, (proto_orders[1], proto_orders[0]))
    squares = proto_parts(sum_squares(proto_pieces))
    return finish((proto_entries, embed_entries), squares, proto_pieces, view_pieces)


def solution(mesh):
    placed = (P("batch", None), P("batch", None), P("proto", None))
    return jax.shard_map(
        body,
        mesh=mesh,
        in_specs=placed,
        out_specs=(P("proto", None), P("batch", None), P("batch", None)),
        check_vma=False,
    )
```

```python
import functools

import jax
import jax.numpy as jnp
from jax import lax
from jax.experimental import pallas as pl
from jax.experimental.pallas import tpu as pltpu
from jax.sharding import PartitionSpec as P

ITERS = 3


CODE_EPS = 0.05
TEMPER = 0.1
NORM_EPS = 1e-06
LANES = 128
MIB = 1024 * 1024


def vmem_spec():
    return pl.BlockSpec(memory_space=pltpu.VMEM)


def params(limit):
    return pltpu.CompilerParams(vmem_limit_bytes=limit * MIB)


def to_columns(line):
    return jnp.broadcast_to(line, (LANES, LANES)).T


def to_line(partial):
    return jnp.sum(partial.T, axis=0, keepdims=True)


def lane_sum(block):
    total = block[:, :LANES]
    for j in range(1, block.shape[1] // LANES):
        total = total + block[:, j * LANES : (j + 1) * LANES]
    return total


def row_fold(block):
    return jnp.sum(block.reshape(block.shape[0] // 8, 8, block.shape[1]), axis=0)


def sum_of(refs, first=0, size=None):
    size = refs[0].shape[0] if size is None else size
    total = refs[0][first : first + size, :]
    for ref in refs[1:]:
        total = total + ref[first : first + size, :]
    return total


LOG2E = 1.4426950408889634


def score_kernel(slow, fast, protos, t_ref, col_ref, den_ref, ubt_ref, cb_ref, raw_s, w_s, ub_s, den_s, sems):
    clips, feats = slow.shape
    count = protos.shape[0]
    loads = []
    for v, src in enumerate((slow, fast)):
        loads.append(pltpu.make_async_copy(src, raw_s.at[v], sems.at[v]))
    loads.append(pltpu.make_async_copy(protos, w_s, sems.at[2]))
    for load in loads:
        load.start()
    for v in range(2):
        loads[v].wait()
        for first in range(0, clips, 256):
            rows = pl.ds(first, 256)
            x = raw_s[v, rows, :].astype(jnp.float32)
            length = jnp.sqrt(jnp.sum(x * x, axis=-1, keepdims=True) + 1e-12)
            u = x / length
            ub_s[v, rows, :] = u.astype(jnp.bfloat16)
            ubt_ref[:, v * clips + first : v * clips + first + 256] = u.T.astype(jnp.bfloat16)
    den_s[...] = jnp.zeros_like(den_s)
    loads[2].wait()

    def chunk(j, _):
        first = pl.multiple_of(j * 256, 256)
        w = w_s[pl.ds(first, 256), :]
        length = jnp.sqrt(jnp.sum(w * w, axis=-1, keepdims=True) + 1e-12)
        c = w / length
        cb_ref[pl.ds(first, 256), :] = c.astype(jnp.bfloat16)
        weights = c.T.astype(jnp.bfloat16)
        for v in range(2):
            cols = jnp.zeros((8, 256), jnp.float32)
            for r in range(0, clips, 512):
                s = jnp.dot(
                    ub_s[v, r : r + 512, :], weights, preferred_element_type=jnp.float32
                )
                for q in range(0, 512, 64):
                    rows = pl.ds(r + q, 64)
                    t = jnp.exp2(s[q : q + 64] * (LOG2E / TEMPER))
                    t_ref[v, rows, pl.ds(first, 256)] = t
                    cols = cols + row_fold(t * t)
                    den_s[v, rows, :] += lane_sum(t)
            line = jnp.sum(cols, axis=0, keepdims=True)
            for h in range(2):
                col_ref[pl.ds(v * (count // LANES) + j * 2 + h, 1), :] = line[
                    :, h * LANES : (h + 1) * LANES
                ]
        return 0

    lax.fori_loop(0, count // 256, chunk, 0)
    groups = clips // LANES
    for v in range(2):
        for i in range(groups):
            den_ref[pl.ds(v * groups + i, 1), :] = to_line(den_s[v, i * LANES : (i + 1) * LANES, :])


def scores(slow, fast, protos):
    clips, feats = slow.shape
    count = protos.shape[0]
    return pl.pallas_call(
        score_kernel,
        out_shape=(
            pltpu.VMEM((2, clips, count), jnp.float32),
            jax.ShapeDtypeStruct((2 * count // LANES, LANES), jnp.float32),
            jax.ShapeDtypeStruct((2 * clips // LANES, LANES), jnp.float32),
            jax.ShapeDtypeStruct((feats, 2 * clips), jnp.bfloat16),
            jax.ShapeDtypeStruct((count, feats), jnp.bfloat16),
        ),
        in_specs=[pl.BlockSpec(memory_space=pltpu.HBM)] * 3,
        out_specs=(vmem_spec(),) * 5,
        scratch_shapes=[
            pltpu.VMEM((2, clips, feats), jnp.bfloat16),
            pltpu.VMEM((count, feats), jnp.float32),
            pltpu.VMEM((2, clips, feats), jnp.bfloat16),
            pltpu.VMEM((2, clips, LANES), jnp.float32),
            pltpu.SemaphoreType.DMA((3,)),
        ],
        compiler_params=params(24),
        name="scores",
    )(*[pltpu.with_memory_space_constraint(x, pltpu.HBM) for x in (slow, fast, protos)])


def row_kernel(protos_all, extra, t_ref, den_ref, *refs):
    col_parts, (row_ref, r_ref, acc_s) = refs[:-3], refs[-3:]
    clips, count = t_ref.shape[1:]
    groups, lines = clips // LANES, count // LANES
    r_ref[...] = 1.0 / (float(protos_all) * sum_of(col_parts))
    if extra:
        row_ref[2 * groups :, :] = den_ref[...]
    for v in range(2):

        def step(i, _, v=v):
            rows = pl.ds(pl.multiple_of(i * LANES, LANES), LANES)
            acc = jnp.zeros((LANES, LANES), jnp.float32)
            for j in range(lines):
                t = t_ref[v, rows, j * LANES : (j + 1) * LANES]
                acc = acc + t * t * r_ref[v * lines + j : v * lines + j + 1, :]
            acc_s[pl.ds(pl.multiple_of((v * groups + i) * LANES, LANES), LANES), :] = acc
            return 0

        lax.fori_loop(0, groups, step, 0)
    for line in range(2 * groups):
        row_ref[line : line + 1, :] = to_line(acc_s[line * LANES : (line + 1) * LANES, :])


def row_pass(t, den, col_parts, protos_all, extra):
    clips, count = t.shape[1:]
    lines = 2 * clips // LANES * (2 if extra else 1)
    return pl.pallas_call(
        functools.partial(row_kernel, protos_all, extra),
        out_shape=(
            jax.ShapeDtypeStruct((lines, LANES), jnp.float32),
            jax.ShapeDtypeStruct((2 * count // LANES, LANES), jnp.float32),
        ),
        in_specs=[vmem_spec()] * (2 + len(col_parts)),
        out_specs=(vmem_spec(),) * 2,
        scratch_shapes=[pltpu.VMEM((2 * clips, LANES), jnp.float32)],
        compiler_params=params(8),
        name="row_pass",
    )(pltpu.with_memory_space_constraint(t, pltpu.VMEM), den, *col_parts)


def col_kernel(clips_all, t_ref, *refs):
    row_parts, (col_ref, acc_s, s_s) = refs[:-3], refs[-3:]
    clips, count = t_ref.shape[1:]
    groups, lines = clips // LANES, count // LANES
    s_s[...] = 1.0 / (float(clips_all) * sum_of(row_parts, 0, 2 * groups))
    acc_s[...] = jnp.zeros_like(acc_s)
    for v in range(2):

        def step(i, _, v=v):
            rows = pl.ds(pl.multiple_of(i * LANES, LANES), LANES)
            scale = to_columns(s_s[pl.ds(v * groups + i, 1), :])
            for j in range(lines):
                span = slice(j * LANES, (j + 1) * LANES)
                t = t_ref[v, rows, span]
                acc_s[v, :, span] += row_fold(t * t * scale)
            return 0

        lax.fori_loop(0, groups, step, 0)
        for j in range(lines):
            col_ref[v * lines + j : v * lines + j + 1, :] = jnp.sum(
                acc_s[v, :, j * LANES : (j + 1) * LANES], axis=0, keepdims=True
            )


def col_pass(t, row_parts, clips_all):
    clips, count = t.shape[1:]
    return pl.pallas_call(
        functools.partial(col_kernel, clips_all),
        out_shape=jax.ShapeDtypeStruct((2 * count // LANES, LANES), jnp.float32),
        in_specs=[vmem_spec()] * (1 + len(row_parts)),
        out_specs=vmem_spec(),
        scratch_shapes=[
            pltpu.VMEM((2, 8, count), jnp.float32),
            pltpu.VMEM((2 * clips // LANES, LANES), jnp.float32),
        ],
        compiler_params=params(8),
        name="col_pass",
    )(pltpu.with_memory_space_constraint(t, pltpu.VMEM), *row_parts)


def piece_of(position, order):
    steps = len(order)
    return sum(((position >> (steps - 1 - j)) & 1) << bit for j, bit in enumerate(order))


def place_of(piece, order):
    steps = len(order)
    return sum(((piece >> bit) & 1) << (steps - 1 - j) for j, bit in enumerate(order))


def chunk_span(m, width):
    which = jnp.bitwise_xor(lax.axis_index("batch"), m)
    return which, pl.multiple_of(which * width, width)


def proto_grads(ubt, chunk, orders, i, out_ref):
    dct = jnp.dot(ubt, chunk, preferred_element_type=jnp.float32)
    half = dct.shape[0] // 2
    for h in range(2):
        out_ref[h, place_of(i, orders[h])] = dct[h * half : (h + 1) * half]


def send_kernel(orders, parts, t_ref, r_ref, ubt_ref, *refs):
    row_parts, den_parts = refs[:parts], refs[parts : 2 * parts]
    send_ref, g_ref, chunk_s, code_s, prob_s = refs[2 * parts :]
    clips, count = t_ref.shape[1:]
    groups, lines = clips // LANES, count // LANES
    pieces = 1 << len(orders[0])
    width = count // (2 * pieces)
    code = (1.0 / TEMPER) / sum_of(row_parts, 0, 2 * groups)
    prob = (1.0 / TEMPER) / sum_of(den_parts, 2 * groups, 2 * groups)
    for v in range(2):
        for i in range(groups):
            line = v * groups + i
            rows = slice(i * LANES, (i + 1) * LANES)
            code_s[v, rows, :] = to_columns(code[line : line + 1, :])
            prob_s[v, rows, :] = to_columns(prob[line : line + 1, :])

    def score_grads(m, keep_chunk):
        which, first = chunk_span(m, width)
        for i in range(0, clips, 32):
            rows = slice(i, i + 32)
            codes = [code_s[v, rows, :] for v in range(2)]
            probs = [prob_s[v, rows, :] for v in range(2)]
            for h in range(width // LANES):
                span = pl.ds(first + h * LANES, LANES)
                line = which * (width // LANES) + h
                t = [t_ref[v, rows, span] for v in range(2)]
                q = [
                    t[v] * t[v] * r_ref[pl.ds(v * lines + line, 1), :] * codes[v]
                    for v in range(2)
                ]
                for v in range(2):
                    g = (t[v] * probs[v] - q[1 - v]).astype(jnp.bfloat16)
                    own = slice(v * clips + i, v * clips + i + 32)
                    g_ref[own, span] = g
                    if keep_chunk:
                        chunk_s[own, h * LANES : (h + 1) * LANES] = g

    def pair(i, _):
        score_grads(2 * i + 1, True)
        score_grads(2 * i, False)
        proto_grads(ubt_ref[...], chunk_s[...], orders, i, send_ref)
        return 0

    lax.fori_loop(0, pieces, pair, 0)


def send_gradients(t, r, ubt, row_parts, den_parts, orders):
    clips, count = t.shape[1:]
    feats = ubt.shape[0]
    pieces = 1 << len(orders[0])
    width = count // (2 * pieces)
    return pl.pallas_call(
        functools.partial(send_kernel, orders, len(row_parts)),
        out_shape=(
            jax.ShapeDtypeStruct((2, pieces, feats // 2, width), jnp.float32),
            pltpu.VMEM((2 * clips, count), jnp.bfloat16),
        ),
        in_specs=[vmem_spec()] * (3 + 2 * len(row_parts)),
        out_specs=(vmem_spec(),) * 2,
        scratch_shapes=[
            pltpu.VMEM((2 * clips, width), jnp.bfloat16),
            pltpu.VMEM((2, clips, LANES), jnp.float32),
            pltpu.VMEM((2, clips, LANES), jnp.float32),
        ],
        compiler_params=params(14),
        cost_estimate=pl.CostEstimate(
            flops=2 * clips * count * feats, bytes_accessed=20 * MIB, transcendentals=0
        ),
        name="send_gradients",
    )(pltpu.with_memory_space_constraint(t, pltpu.VMEM), r, ubt, *row_parts, *den_parts)


def embed_grad_kernel(orders, g_ref, cb_ref, *outs):
    clips = g_ref.shape[0] // 2
    peers = 1 << len(orders[0])
    size = clips // peers
    for v in range(2):
        for place in range(peers):
            which = jnp.bitwise_xor(lax.axis_index("proto"), piece_of(place, orders[v]))
            rows = pl.ds(pl.multiple_of(v * clips + which * size, size), size)
            out_ref = outs[2 * v + (0 if place >= peers // 2 else 1)]
            out_ref[place % (peers // 2)] = jnp.dot(
                g_ref[rows, :], cb_ref[...], preferred_element_type=jnp.float32
            )


def embed_gradients(g, cb, orders):
    clips, count = g.shape[0] // 2, g.shape[1]
    feats = cb.shape[1]
    peers = 1 << len(orders[0])
    share = jax.ShapeDtypeStruct((peers // 2, clips // peers, feats), jnp.float32)
    return pl.pallas_call(
        functools.partial(embed_grad_kernel, orders),
        out_shape=(share,) * 4,
        in_specs=[vmem_spec()] * 2,
        out_specs=(vmem_spec(),) * 4,
        compiler_params=params(14),
        cost_estimate=pl.CostEstimate(
            flops=4 * clips * count * feats, bytes_accessed=11 * MIB, transcendentals=0
        ),
        name="embed_gradients",
    )(pltpu.with_memory_space_constraint(g, pltpu.VMEM), cb)


def keep_kernel(orders, g_ref, ubt_ref, after_ref, keep_ref):
    pieces = 1 << len(orders[0])
    width = g_ref.shape[1] // (2 * pieces)

    def step(i, _):
        _, first = chunk_span(2 * i, width)
        proto_grads(ubt_ref[...], g_ref[:, pl.ds(first, width)], orders, i, keep_ref)
        return 0

    lax.fori_loop(0, pieces, step, 0)


def keep_gradients(g, ubt, after, orders):
    count = g.shape[1]
    feats, clips = ubt.shape
    pieces = 1 << len(orders[0])
    return pl.pallas_call(
        functools.partial(keep_kernel, orders),
        out_shape=jax.ShapeDtypeStruct((2, pieces, feats // 2, count // (2 * pieces)), jnp.float32),
        in_specs=[vmem_spec()] * 2 + [pl.BlockSpec(memory_space=pl.ANY)],
        out_specs=vmem_spec(),
        compiler_params=params(14),
        cost_estimate=pl.CostEstimate(
            flops=clips * count * feats, bytes_accessed=6 * MIB, transcendentals=0
        ),
        name="keep_gradients",
    )(pltpu.with_memory_space_constraint(g, pltpu.VMEM), ubt, after)


def split_add_kernel(plan, inputs, *refs):
    ins, outs = refs[:inputs], refs[inputs:]
    for n, (keep_place, recv_place, part) in enumerate(plan):
        keep, recv = ins[keep_place], ins[recv_place]
        if part is not None:
            keep, recv = keep.at[part], recv.at[part]
        send_out, keep_out = outs[2 * n : 2 * n + 2]
        half = keep_out.shape[0]
        keep_out[...] = keep[:half] + recv[:half]
        send_out[...] = keep[half:] + recv[half:]


def split_add(arrays, plan):
    halves = []
    for place, _, part in plan:
        shape = arrays[place].shape if part is None else arrays[place].shape[1:]
        halves += [jax.ShapeDtypeStruct((shape[0] // 2,) + shape[1:], jnp.float32)] * 2
    outs = pl.pallas_call(
        functools.partial(split_add_kernel, plan, len(arrays)),
        out_shape=tuple(halves),
        in_specs=[vmem_spec()] * len(arrays),
        out_specs=(vmem_spec(),) * len(halves),
        compiler_params=params(12),
        name="split_add",
    )(*arrays)
    return [(outs[2 * n], outs[2 * n + 1]) for n in range(len(plan))]


def project(raw, grad):
    x = raw.astype(jnp.float32)
    length = jnp.sqrt(jnp.sum(x * x, axis=-1, keepdims=True) + 1e-12)
    unit = x / length
    along = jnp.sum(unit * grad, axis=-1, keepdims=True)
    return (grad - unit * along) / length


EXTRA = 8


def share_kernel(proto_raw, slow_raw, fast_raw, *refs):
    terms, (proto_out, embed_out) = refs[:-2], refs[-2:]
    count = proto_raw.shape[0]
    squares = [jnp.zeros((8, LANES), jnp.float32)] * 2
    halves = [terms[2 * h][0] + terms[2 * h + 1][0] for h in range(2)]
    grad = project(proto_raw[...], jnp.concatenate(halves, axis=0).T)
    proto_out[:count, :] = grad
    squares[0] = row_fold(lane_sum(grad * grad))
    for v, raw in enumerate((slow_raw, fast_raw)):
        grad = project(raw[...], terms[4 + 2 * v][0] + terms[5 + 2 * v][0])
        embed_out[v] = grad
        squares[1] = squares[1] + row_fold(lane_sum(grad * grad))
    for kind in range(2):
        total = jnp.sum(jnp.sum(squares[kind], axis=0, keepdims=True), axis=1, keepdims=True)
        proto_out[count:, kind * LANES : (kind + 1) * LANES] = jnp.broadcast_to(total, (EXTRA, LANES))


def project_shares(raws, terms):
    rows, feats = raws[1].shape
    count = raws[0].shape[0]
    return pl.pallas_call(
        share_kernel,
        out_shape=(
            jax.ShapeDtypeStruct((count + EXTRA, feats), jnp.float32),
            jax.ShapeDtypeStruct((2, rows, feats), jnp.float32),
        ),
        in_specs=[vmem_spec()] * (len(raws) + len(terms)),
        out_specs=(vmem_spec(),) * 2,
        compiler_params=params(10),
        name="project_shares",
    )(*raws, *terms)


def tree_sum(terms):
    while len(terms) > 1:
        terms = [terms[i] + terms[i + 1] for i in range(0, len(terms), 2)]
    return terms[0]


def distinct(groups):
    arrays, plan = [], []
    for group in groups:
        places = []
        for array, part in group:
            place = next((i for i, known in enumerate(arrays) if known is array), None)
            if place is None:
                place = len(arrays)
                arrays.append(array)
            places.append((place, part))
        plan.append(places)
    return arrays, plan


def piece_ref(ins, place, part):
    return ins[place] if part is None else ins[place].at[part]


def squares_kernel(plan, rows, *refs):
    ins, out_ref = refs[:-1], refs[-1]
    total = tree_sum([piece_ref(ins, *piece)[rows:, :] for piece in plan])
    for kind in range(2):
        out_ref[kind] = total[:, kind * LANES : (kind + 1) * LANES]


def sum_squares(pieces, rows):
    arrays, plan = distinct([pieces])
    return pl.pallas_call(
        functools.partial(squares_kernel, plan[0], rows),
        out_shape=jax.ShapeDtypeStruct((2, 8, LANES), jnp.float32),
        in_specs=[vmem_spec()] * len(arrays),
        out_specs=vmem_spec(),
        compiler_params=params(8),
        cost_estimate=pl.CostEstimate(flops=8, bytes_accessed=8, transcendentals=0),
        name="sum_squares",
    )(*arrays)


def finish_kernel(entries, plan, count, *refs):
    squares, ins, outs = refs[:count], refs[count:-7], refs[-7:-4]
    scratch, sems = refs[-4:-1], refs[-1]
    total = tree_sum([square[...] for square in squares])
    factors = [lax.rsqrt(total[k, 0:1, 0:1] / entries[k] + NORM_EPS) for k in range(2)]
    copies = []
    for n, pieces in enumerate(plan):
        axis, kind = ("batch", 0) if n == 0 else ("proto", 1)
        size = scratch[n].shape[1]
        for m, piece in enumerate(pieces):
            which = jnp.bitwise_xor(lax.axis_index(axis), m)
            rows = pl.ds(pl.multiple_of(which * size, size), size)
            scratch[n][m] = piece_ref(ins, *piece)[:size, :] * factors[kind]
            sem = sems.at[len(copies)]
            copies.append(pltpu.make_async_copy(scratch[n].at[m], outs[n].at[rows], sem))
            copies[-1].start()
    for copy in copies:
        copy.wait()


def finish(entries, squares, groups, sizes):
    arrays, plan = distinct(groups)
    feats = arrays[0].shape[-1]
    scratch = [
        pltpu.VMEM((len(group), size, feats), jnp.float32) for group, size in zip(groups, sizes)
    ]
    outs = tuple(
        jax.ShapeDtypeStruct((len(group) * size, feats), jnp.float32)
        for group, size in zip(groups, sizes)
    )
    count = sum(len(group) for group in groups)
    return pl.pallas_call(
        functools.partial(finish_kernel, entries, plan, len(squares)),
        out_shape=outs,
        in_specs=[vmem_spec()] * (len(squares) + len(arrays)),
        out_specs=(pl.BlockSpec(memory_space=pltpu.HBM),) * len(outs),
        scratch_shapes=scratch + [pltpu.SemaphoreType.DMA((count,))],
        compiler_params=params(12),
        name="finish",
    )(*squares, *arrays)


def swap(own, axis, mask):
    return lax.ppermute(own, axis, [(i, i ^ mask) for i in range(lax.axis_size(axis))])


def bits_of(axis):
    count = lax.axis_size(axis)
    bits = count.bit_length() - 1
    if count != 1 << bits:
        raise ValueError("axis size")
    return bits


def far_first(own, axis, step, count):
    parts = {m: swap(own, axis, m * step) for m in reversed(range(1, count))}
    return [parts[m] for m in range(1, count)]


def proto_parts(own):
    return [own] + far_first(own, "proto", 1, lax.axis_size("proto"))


def batch_parts(own):
    pair = own + swap(own, "batch", 1)
    return [pair] + far_first(pair, "batch", 2, lax.axis_size("batch") // 2)


def scatter_sums(groups):
    stage, terms = 0, [None] * len(groups)
    state = list(groups)
    while any(term is None for term in terms):
        live = [n for n in range(len(state)) if terms[n] is None]
        recvs = {}
        for n in live:
            axis, order, send, keep = state[n]
            recvs[n] = swap(send, axis, 1 << order[stage])
        going = []
        for n in live:
            axis, order, send, keep = state[n]
            if stage + 1 == len(order):
                terms[n] = (keep, recvs[n])
            else:
                going.append(n)
        if going:
            arrays = [x for n in going for x in (state[n][3], recvs[n])]
            split = split_add(arrays, [(2 * i, 2 * i + 1, None) for i in range(len(going))])
            for n, (send, keep) in zip(going, split):
                state[n] = (state[n][0], state[n][1], send, keep)
        stage += 1
    return [x for term in terms for x in term]


def forward_kernel(near_ref, far_ref, x_ref, y_ref, pack_ref, slow_ref, fast_ref):
    pack_ref[0] = near_ref[...]
    pack_ref[1] = far_ref[...]
    slow_ref[...] = y_ref[0]
    fast_ref[...] = x_ref[1]


def forwards(near, far, x, y):
    view = jax.ShapeDtypeStruct(x.shape[1:], x.dtype)
    return pl.pallas_call(
        forward_kernel,
        out_shape=(jax.ShapeDtypeStruct((2,) + near.shape, near.dtype), view, view),
        in_specs=[vmem_spec()] * 4,
        out_specs=(vmem_spec(),) * 3,
        compiler_params=params(10),
        name="forwards",
    )(near, far, x, y)


def copy_kernel(x_ref, *refs):
    refs[-1][...] = x_ref[...]


def copy_after(x, arrived):
    return pl.pallas_call(
        copy_kernel,
        out_shape=jax.ShapeDtypeStruct(x.shape, x.dtype),
        in_specs=[vmem_spec()] + [pl.BlockSpec(memory_space=pl.ANY)] * len(arrived),
        out_specs=vmem_spec(),
        compiler_params=params(8),
        name="copy_after",
    )(x, *arrived)


def gather_pairs(proto, embed):
    y, x = swap(embed, "proto", 2), swap(embed, "proto", 1)
    far, near = swap(proto, "batch", 4), swap(proto, "batch", 2)
    core = swap(proto, "batch", 1)
    pack, slow, fast = forwards(near, far, x, y)
    slow, fast = swap(slow, "proto", 1), swap(fast, "proto", 2)
    corner = swap(far, "batch", 2)
    core_pack = swap(pack, "batch", 1)
    core_corner = swap(copy_after(corner, [slow, fast]), "batch", 1)
    whole = [proto, core, near, (core_pack, 0), far, (core_pack, 1), corner, core_corner]
    protos = [piece if isinstance(piece, tuple) else (piece, None) for piece in whole]
    return protos, [[(embed, v), (x, v), (y, v), (last, None)] for v, last in enumerate((slow, fast))]


def gather_batch(own):
    bits = list(reversed(range(lax.axis_size("batch").bit_length() - 1)))
    pieces = {0: own}
    first = {bit: swap(own, "batch", 1 << bit) for bit in bits}
    for bit in bits:
        for m in list(pieces):
            pieces[m | 1 << bit] = first[bit] if m == 0 else swap(pieces[m], "batch", 1 << bit)
    return [(pieces[m], None) for m in range(len(pieces))]


def gather_views(own, orders):
    first = {bit: swap(own, "proto", 1 << bit) for bit in sorted(orders[0])}
    groups = []
    for v, order in enumerate(orders):
        pieces = {0: (own, v)}
        for bit in order:
            for m in list(pieces):
                if m == 0:
                    pieces[1 << bit] = (first[bit], v)
                else:
                    array, view = pieces[m]
                    piece = array if view is None else array[view]
                    pieces[m | 1 << bit] = (swap(piece, "proto", 1 << bit), None)
        groups.append([pieces[m] for m in range(len(pieces))])
    return groups


def body(slow_embed, fast_embed, prototypes):
    clip_dev, feat_width = slow_embed.shape
    proto_dev = prototypes.shape[0]
    batch_count = lax.axis_size("batch")
    proto_count = lax.axis_size("proto")
    clips_all = clip_dev * batch_count
    protos_all = proto_dev * proto_count
    proto_entries = float(protos_all * feat_width)
    embed_entries = float(2 * clips_all * feat_width)
    batch_bits, proto_bits = bits_of("batch"), bits_of("proto")
    me_batch, me_proto = lax.axis_index("batch"), lax.axis_index("proto")

    t, col, den, unit_bt, proto_b = scores(slow_embed, fast_embed, prototypes)
    for iteration in range(ITERS):
        rows, r = row_pass(t, den, batch_parts(col), protos_all, iteration == 0)
        row_parts = proto_parts(rows)
        if iteration == 0:
            den_parts = row_parts
        if iteration + 1 < ITERS:
            col = col_pass(t, row_parts, clips_all)

    near = tuple(range(batch_bits - 1))
    batch_orders = (near, tuple(reversed(near)))
    proto_orders = (tuple(range(proto_bits)), tuple(reversed(range(proto_bits))))
    send, g = send_gradients(t, r, unit_bt, row_parts, den_parts, batch_orders)
    shares = embed_gradients(g, proto_b, proto_orders)
    keep = keep_gradients(g, unit_bt, shares[0], batch_orders)

    proto_rows = proto_dev // batch_count
    clip_rows = clip_dev // proto_count
    raws = [lax.dynamic_slice_in_dim(prototypes, me_batch * proto_rows, proto_rows, 0)]
    for x in (slow_embed, fast_embed):
        raws.append(lax.dynamic_slice_in_dim(x, me_proto * clip_rows, clip_rows, 0))
    recv = swap(send, "batch", 1)
    halves = split_add([keep, recv], [(0, 1, h) for h in range(2)])
    groups = []
    for h in range(2):
        order = tuple(bit + 1 for bit in batch_orders[h])
        groups.append(("batch", order) + tuple(halves[h]))
    for v in range(2):
        groups.append(("proto", proto_orders[v], shares[2 * v], shares[2 * v + 1]))
    terms = scatter_sums(groups)
    grad_proto, grad_embed = project_shares(raws, terms)
    if batch_bits == 3 and proto_bits == 2:
        proto_pieces, view_pieces = gather_pairs(grad_proto, grad_embed)
    else:
        proto_pieces = gather_batch(grad_proto)
        view_pieces = gather_views(grad_embed, (proto_orders[1], proto_orders[0]))
    squares = proto_parts(sum_squares(proto_pieces, proto_rows))
    sizes = (proto_rows, clip_rows, clip_rows)
    groups = [proto_pieces] + view_pieces
    return finish((proto_entries, embed_entries), squares, groups, sizes)


def solution(mesh):
    placed = (P("batch", None), P("batch", None), P("proto", None))
    return jax.shard_map(
        body,
        mesh=mesh,
        in_specs=placed,
        out_specs=(P("proto", None), P("batch", None), P("batch", None)),
        check_vma=False,
    )
```

```python
import functools

import jax
import jax.numpy as jnp
from jax import lax
from jax.experimental import pallas as pl
from jax.experimental.pallas import tpu as pltpu
from jax.sharding import PartitionSpec as P

ITERS = 3


CODE_EPS = 0.05
TEMPER = 0.1
NORM_EPS = 1e-06
LANES = 128
MIB = 1024 * 1024


def vmem_spec():
    return pl.BlockSpec(memory_space=pltpu.VMEM)


def params(limit):
    return pltpu.CompilerParams(vmem_limit_bytes=limit * MIB)


def to_columns(line):
    return jnp.broadcast_to(line, (LANES, LANES)).T


def to_line(partial):
    return jnp.sum(partial.T, axis=0, keepdims=True)


def lane_sum(block):
    total = block[:, :LANES]
    for j in range(1, block.shape[1] // LANES):
        total = total + block[:, j * LANES : (j + 1) * LANES]
    return total


def row_fold(block):
    return jnp.sum(block.reshape(block.shape[0] // 8, 8, block.shape[1]), axis=0)


def sum_of(refs, first=0, size=None):
    size = refs[0].shape[0] if size is None else size
    total = refs[0][first : first + size, :]
    for ref in refs[1:]:
        total = total + ref[first : first + size, :]
    return total


LOG2E = 1.4426950408889634


def score_kernel(slow, fast, protos, t_ref, col_ref, den_ref, ubt_ref, cb_ref, raw_s, w_s, ub_s, den_s, sems):
    clips, feats = slow.shape
    count = protos.shape[0]
    loads = []
    for v, src in enumerate((slow, fast)):
        loads.append(pltpu.make_async_copy(src, raw_s.at[v], sems.at[v]))
    loads.append(pltpu.make_async_copy(protos, w_s, sems.at[2]))
    for load in loads:
        load.start()
    for v in range(2):
        loads[v].wait()
        for first in range(0, clips, 256):
            rows = pl.ds(first, 256)
            x = raw_s[v, rows, :].astype(jnp.float32)
            length = jnp.sqrt(jnp.sum(x * x, axis=-1, keepdims=True) + 1e-12)
            u = x / length
            ub_s[v, rows, :] = u.astype(jnp.bfloat16)
            ubt_ref[:, v * clips + first : v * clips + first + 256] = u.T.astype(jnp.bfloat16)
    den_s[...] = jnp.zeros_like(den_s)
    loads[2].wait()

    def chunk(j, _):
        first = pl.multiple_of(j * 256, 256)
        w = w_s[pl.ds(first, 256), :]
        length = jnp.sqrt(jnp.sum(w * w, axis=-1, keepdims=True) + 1e-12)
        c = w / length
        cb_ref[pl.ds(first, 256), :] = c.astype(jnp.bfloat16)
        weights = c.T.astype(jnp.bfloat16)
        for v in range(2):
            cols = jnp.zeros((8, 256), jnp.float32)
            for r in range(0, clips, 512):
                s = jnp.dot(
                    ub_s[v, r : r + 512, :], weights, preferred_element_type=jnp.float32
                )
                for q in range(0, 512, 64):
                    rows = pl.ds(r + q, 64)
                    t = jnp.exp2(s[q : q + 64] * (LOG2E / TEMPER))
                    t_ref[v, rows, pl.ds(first, 256)] = t
                    cols = cols + row_fold(t * t)
                    den_s[v, rows, :] += lane_sum(t)
            line = jnp.sum(cols, axis=0, keepdims=True)
            for h in range(2):
                col_ref[pl.ds(v * (count // LANES) + j * 2 + h, 1), :] = line[
                    :, h * LANES : (h + 1) * LANES
                ]
        return 0

    lax.fori_loop(0, count // 256, chunk, 0)
    groups = clips // LANES
    for v in range(2):
        for i in range(groups):
            den_ref[pl.ds(v * groups + i, 1), :] = to_line(den_s[v, i * LANES : (i + 1) * LANES, :])


def scores(slow, fast, protos):
    clips, feats = slow.shape
    count = protos.shape[0]
    return pl.pallas_call(
        score_kernel,
        out_shape=(
            pltpu.VMEM((2, clips, count), jnp.float32),
            jax.ShapeDtypeStruct((2 * count // LANES, LANES), jnp.float32),
            jax.ShapeDtypeStruct((2 * clips // LANES, LANES), jnp.float32),
            jax.ShapeDtypeStruct((feats, 2 * clips), jnp.bfloat16),
            jax.ShapeDtypeStruct((count, feats), jnp.bfloat16),
        ),
        in_specs=[pl.BlockSpec(memory_space=pltpu.HBM)] * 3,
        out_specs=(vmem_spec(),) * 5,
        scratch_shapes=[
            pltpu.VMEM((2, clips, feats), jnp.bfloat16),
            pltpu.VMEM((count, feats), jnp.float32),
            pltpu.VMEM((2, clips, feats), jnp.bfloat16),
            pltpu.VMEM((2, clips, LANES), jnp.float32),
            pltpu.SemaphoreType.DMA((3,)),
        ],
        compiler_params=params(24),
        name="scores",
    )(*[pltpu.with_memory_space_constraint(x, pltpu.HBM) for x in (slow, fast, protos)])


def row_kernel(protos_all, extra, t_ref, den_ref, *refs):
    col_parts, (row_ref, r_ref, acc_s) = refs[:-3], refs[-3:]
    clips, count = t_ref.shape[1:]
    groups, lines = clips // LANES, count // LANES
    r_ref[...] = 1.0 / (float(protos_all) * sum_of(col_parts))
    if extra:
        row_ref[2 * groups :, :] = den_ref[...]
    for v in range(2):

        def step(i, _, v=v):
            rows = pl.ds(pl.multiple_of(i * LANES, LANES), LANES)
            acc = jnp.zeros((LANES, LANES), jnp.float32)
            for j in range(lines):
                t = t_ref[v, rows, j * LANES : (j + 1) * LANES]
                acc = acc + t * t * r_ref[v * lines + j : v * lines + j + 1, :]
            acc_s[pl.ds(pl.multiple_of((v * groups + i) * LANES, LANES), LANES), :] = acc
            return 0

        lax.fori_loop(0, groups, step, 0)
    for line in range(2 * groups):
        row_ref[line : line + 1, :] = to_line(acc_s[line * LANES : (line + 1) * LANES, :])


def row_pass(t, den, col_parts, protos_all, extra):
    clips, count = t.shape[1:]
    lines = 2 * clips // LANES * (2 if extra else 1)
    return pl.pallas_call(
        functools.partial(row_kernel, protos_all, extra),
        out_shape=(
            jax.ShapeDtypeStruct((lines, LANES), jnp.float32),
            jax.ShapeDtypeStruct((2 * count // LANES, LANES), jnp.float32),
        ),
        in_specs=[vmem_spec()] * (2 + len(col_parts)),
        out_specs=(vmem_spec(),) * 2,
        scratch_shapes=[pltpu.VMEM((2 * clips, LANES), jnp.float32)],
        compiler_params=params(8),
        name="row_pass",
    )(pltpu.with_memory_space_constraint(t, pltpu.VMEM), den, *col_parts)


def col_kernel(clips_all, t_ref, *refs):
    row_parts, (col_ref, acc_s, s_s) = refs[:-3], refs[-3:]
    clips, count = t_ref.shape[1:]
    groups, lines = clips // LANES, count // LANES
    s_s[...] = 1.0 / (float(clips_all) * sum_of(row_parts, 0, 2 * groups))
    acc_s[...] = jnp.zeros_like(acc_s)
    for v in range(2):

        def step(i, _, v=v):
            rows = pl.ds(pl.multiple_of(i * LANES, LANES), LANES)
            scale = to_columns(s_s[pl.ds(v * groups + i, 1), :])
            for j in range(lines):
                span = slice(j * LANES, (j + 1) * LANES)
                t = t_ref[v, rows, span]
                acc_s[v, :, span] += row_fold(t * t * scale)
            return 0

        lax.fori_loop(0, groups, step, 0)
        for j in range(lines):
            col_ref[v * lines + j : v * lines + j + 1, :] = jnp.sum(
                acc_s[v, :, j * LANES : (j + 1) * LANES], axis=0, keepdims=True
            )


def col_pass(t, row_parts, clips_all):
    clips, count = t.shape[1:]
    return pl.pallas_call(
        functools.partial(col_kernel, clips_all),
        out_shape=jax.ShapeDtypeStruct((2 * count // LANES, LANES), jnp.float32),
        in_specs=[vmem_spec()] * (1 + len(row_parts)),
        out_specs=vmem_spec(),
        scratch_shapes=[
            pltpu.VMEM((2, 8, count), jnp.float32),
            pltpu.VMEM((2 * clips // LANES, LANES), jnp.float32),
        ],
        compiler_params=params(8),
        name="col_pass",
    )(pltpu.with_memory_space_constraint(t, pltpu.VMEM), *row_parts)


def piece_of(position, order):
    steps = len(order)
    return sum(((position >> (steps - 1 - j)) & 1) << bit for j, bit in enumerate(order))


def place_of(piece, order):
    steps = len(order)
    return sum(((piece >> bit) & 1) << (steps - 1 - j) for j, bit in enumerate(order))


def chunk_span(m, width):
    which = jnp.bitwise_xor(lax.axis_index("batch"), m)
    return which, pl.multiple_of(which * width, width)


def proto_grads(ubt, chunk, orders, i, out_ref):
    dct = jnp.dot(ubt, chunk, preferred_element_type=jnp.float32)
    half = dct.shape[0] // 2
    for h in range(2):
        out_ref[h, place_of(i, orders[h])] = dct[h * half : (h + 1) * half]


def send_kernel(orders, parts, t_ref, r_ref, ubt_ref, *refs):
    row_parts, den_parts = refs[:parts], refs[parts : 2 * parts]
    send_ref, g_ref, chunk_s, code_s, prob_s = refs[2 * parts :]
    clips, count = t_ref.shape[1:]
    groups, lines = clips // LANES, count // LANES
    pieces = 1 << len(orders[0])
    width = count // (2 * pieces)
    code = (1.0 / TEMPER) / sum_of(row_parts, 0, 2 * groups)
    prob = (1.0 / TEMPER) / sum_of(den_parts, 2 * groups, 2 * groups)
    for v in range(2):
        for i in range(groups):
            line = v * groups + i
            rows = slice(i * LANES, (i + 1) * LANES)
            code_s[v, rows, :] = to_columns(code[line : line + 1, :])
            prob_s[v, rows, :] = to_columns(prob[line : line + 1, :])

    def score_grads(m, keep_chunk):
        which, first = chunk_span(m, width)
        for i in range(0, clips, 32):
            rows = slice(i, i + 32)
            codes = [code_s[v, rows, :] for v in range(2)]
            probs = [prob_s[v, rows, :] for v in range(2)]
            for h in range(width // LANES):
                span = pl.ds(first + h * LANES, LANES)
                line = which * (width // LANES) + h
                t = [t_ref[v, rows, span] for v in range(2)]
                q = [
                    t[v] * t[v] * r_ref[pl.ds(v * lines + line, 1), :] * codes[v]
                    for v in range(2)
                ]
                for v in range(2):
                    g = (t[v] * probs[v] - q[1 - v]).astype(jnp.bfloat16)
                    own = slice(v * clips + i, v * clips + i + 32)
                    g_ref[own, span] = g
                    if keep_chunk:
                        chunk_s[own, h * LANES : (h + 1) * LANES] = g

    def pair(i, _):
        score_grads(2 * i + 1, True)
        score_grads(2 * i, False)
        proto_grads(ubt_ref[...], chunk_s[...], orders, i, send_ref)
        return 0

    lax.fori_loop(0, pieces, pair, 0)


def send_gradients(t, r, ubt, row_parts, den_parts, orders):
    clips, count = t.shape[1:]
    feats = ubt.shape[0]
    pieces = 1 << len(orders[0])
    width = count // (2 * pieces)
    return pl.pallas_call(
        functools.partial(send_kernel, orders, len(row_parts)),
        out_shape=(
            jax.ShapeDtypeStruct((2, pieces, feats // 2, width), jnp.float32),
            pltpu.VMEM((2 * clips, count), jnp.bfloat16),
        ),
        in_specs=[vmem_spec()] * (3 + 2 * len(row_parts)),
        out_specs=(vmem_spec(),) * 2,
        scratch_shapes=[
            pltpu.VMEM((2 * clips, width), jnp.bfloat16),
            pltpu.VMEM((2, clips, LANES), jnp.float32),
            pltpu.VMEM((2, clips, LANES), jnp.float32),
        ],
        compiler_params=params(14),
        cost_estimate=pl.CostEstimate(
            flops=2 * clips * count * feats, bytes_accessed=20 * MIB, transcendentals=0
        ),
        name="send_gradients",
    )(pltpu.with_memory_space_constraint(t, pltpu.VMEM), r, ubt, *row_parts, *den_parts)


def embed_grad_kernel(orders, g_ref, cb_ref, *outs):
    clips = g_ref.shape[0] // 2
    peers = 1 << len(orders[0])
    size = clips // peers
    for v in range(2):
        for place in range(peers):
            which = jnp.bitwise_xor(lax.axis_index("proto"), piece_of(place, orders[v]))
            rows = pl.ds(pl.multiple_of(v * clips + which * size, size), size)
            out_ref = outs[2 * v + (0 if place >= peers // 2 else 1)]
            out_ref[place % (peers // 2)] = jnp.dot(
                g_ref[rows, :], cb_ref[...], preferred_element_type=jnp.float32
            )


def embed_gradients(g, cb, orders):
    clips, count = g.shape[0] // 2, g.shape[1]
    feats = cb.shape[1]
    peers = 1 << len(orders[0])
    share = jax.ShapeDtypeStruct((peers // 2, clips // peers, feats), jnp.float32)
    return pl.pallas_call(
        functools.partial(embed_grad_kernel, orders),
        out_shape=(share,) * 4,
        in_specs=[vmem_spec()] * 2,
        out_specs=(vmem_spec(),) * 4,
        compiler_params=params(14),
        cost_estimate=pl.CostEstimate(
            flops=4 * clips * count * feats, bytes_accessed=11 * MIB, transcendentals=0
        ),
        name="embed_gradients",
    )(pltpu.with_memory_space_constraint(g, pltpu.VMEM), cb)


def keep_kernel(orders, g_ref, ubt_ref, after_ref, keep_ref):
    pieces = 1 << len(orders[0])
    width = g_ref.shape[1] // (2 * pieces)

    def step(i, _):
        _, first = chunk_span(2 * i, width)
        proto_grads(ubt_ref[...], g_ref[:, pl.ds(first, width)], orders, i, keep_ref)
        return 0

    lax.fori_loop(0, pieces, step, 0)


def keep_gradients(g, ubt, after, orders):
    count = g.shape[1]
    feats, clips = ubt.shape
    pieces = 1 << len(orders[0])
    return pl.pallas_call(
        functools.partial(keep_kernel, orders),
        out_shape=jax.ShapeDtypeStruct((2, pieces, feats // 2, count // (2 * pieces)), jnp.float32),
        in_specs=[vmem_spec()] * 2 + [pl.BlockSpec(memory_space=pl.ANY)],
        out_specs=vmem_spec(),
        compiler_params=params(14),
        cost_estimate=pl.CostEstimate(
            flops=clips * count * feats, bytes_accessed=6 * MIB, transcendentals=0
        ),
        name="keep_gradients",
    )(pltpu.with_memory_space_constraint(g, pltpu.VMEM), ubt, after)


def split_add_kernel(plan, inputs, *refs):
    ins, outs = refs[:inputs], refs[inputs:]
    for n, (keep_place, recv_place, part) in enumerate(plan):
        keep, recv = ins[keep_place], ins[recv_place]
        if part is not None:
            keep, recv = keep.at[part], recv.at[part]
        send_out, keep_out = outs[2 * n : 2 * n + 2]
        half = keep_out.shape[0]
        keep_out[...] = keep[:half] + recv[:half]
        send_out[...] = keep[half:] + recv[half:]


def split_add(arrays, plan):
    halves = []
    for place, _, part in plan:
        shape = arrays[place].shape if part is None else arrays[place].shape[1:]
        halves += [jax.ShapeDtypeStruct((shape[0] // 2,) + shape[1:], jnp.float32)] * 2
    outs = pl.pallas_call(
        functools.partial(split_add_kernel, plan, len(arrays)),
        out_shape=tuple(halves),
        in_specs=[vmem_spec()] * len(arrays),
        out_specs=(vmem_spec(),) * len(halves),
        compiler_params=params(12),
        name="split_add",
    )(*arrays)
    return [(outs[2 * n], outs[2 * n + 1]) for n in range(len(plan))]


def project(raw, grad):
    x = raw.astype(jnp.float32)
    length = jnp.sqrt(jnp.sum(x * x, axis=-1, keepdims=True) + 1e-12)
    unit = x / length
    along = jnp.sum(unit * grad, axis=-1, keepdims=True)
    return (grad - unit * along) / length


EXTRA = 8


def share_kernel(proto_raw, slow_raw, fast_raw, *refs):
    terms, (proto_out, embed_out) = refs[:-2], refs[-2:]
    count = proto_raw.shape[0]
    squares = [jnp.zeros((8, LANES), jnp.float32)] * 2
    halves = [terms[2 * h][0] + terms[2 * h + 1][0] for h in range(2)]
    grad = project(proto_raw[...], jnp.concatenate(halves, axis=0).T)
    proto_out[:count, :] = grad
    squares[0] = row_fold(lane_sum(grad * grad))
    for v, raw in enumerate((slow_raw, fast_raw)):
        grad = project(raw[...], terms[4 + 2 * v][0] + terms[5 + 2 * v][0])
        embed_out[v] = grad
        squares[1] = squares[1] + row_fold(lane_sum(grad * grad))
    for kind in range(2):
        total = jnp.sum(jnp.sum(squares[kind], axis=0, keepdims=True), axis=1, keepdims=True)
        proto_out[count:, kind * LANES : (kind + 1) * LANES] = jnp.broadcast_to(total, (EXTRA, LANES))


def project_shares(raws, terms):
    rows, feats = raws[1].shape
    count = raws[0].shape[0]
    return pl.pallas_call(
        share_kernel,
        out_shape=(
            jax.ShapeDtypeStruct((count + EXTRA, feats), jnp.float32),
            jax.ShapeDtypeStruct((2, rows, feats), jnp.float32),
        ),
        in_specs=[vmem_spec()] * (len(raws) + len(terms)),
        out_specs=(vmem_spec(),) * 2,
        compiler_params=params(10),
        name="project_shares",
    )(*raws, *terms)


def tree_sum(terms):
    while len(terms) > 1:
        terms = [terms[i] + terms[i + 1] for i in range(0, len(terms), 2)]
    return terms[0]


def distinct(groups):
    arrays, plan = [], []
    for group in groups:
        places = []
        for array, part in group:
            place = next((i for i, known in enumerate(arrays) if known is array), None)
            if place is None:
                place = len(arrays)
                arrays.append(array)
            places.append((place, part))
        plan.append(places)
    return arrays, plan


def piece_ref(ins, place, part):
    return ins[place] if part is None else ins[place].at[part]


def squares_kernel(plan, rows, *refs):
    ins, out_ref = refs[:-1], refs[-1]
    total = tree_sum([piece_ref(ins, *piece)[rows:, :] for piece in plan])
    for kind in range(2):
        out_ref[kind] = total[:, kind * LANES : (kind + 1) * LANES]


def sum_squares(pieces, rows):
    arrays, plan = distinct([pieces])
    return pl.pallas_call(
        functools.partial(squares_kernel, plan[0], rows),
        out_shape=jax.ShapeDtypeStruct((2, 8, LANES), jnp.float32),
        in_specs=[vmem_spec()] * len(arrays),
        out_specs=vmem_spec(),
        compiler_params=params(8),
        cost_estimate=pl.CostEstimate(flops=8, bytes_accessed=8, transcendentals=0),
        name="sum_squares",
    )(*arrays)


def finish_kernel(entries, plan, count, *refs):
    squares, ins, outs = refs[:count], refs[count:-7], refs[-7:-4]
    scratch, sems = refs[-4:-1], refs[-1]
    total = tree_sum([square[...] for square in squares])
    factors = [lax.rsqrt(total[k, 0:1, 0:1] / entries[k] + NORM_EPS) for k in range(2)]
    copies = []
    for n, pieces in enumerate(plan):
        axis, kind = ("batch", 0) if n == 0 else ("proto", 1)
        size = scratch[n].shape[1]
        for m, piece in enumerate(pieces):
            which = jnp.bitwise_xor(lax.axis_index(axis), m)
            rows = pl.ds(pl.multiple_of(which * size, size), size)
            scratch[n][m] = piece_ref(ins, *piece)[:size, :] * factors[kind]
            sem = sems.at[len(copies)]
            copies.append(pltpu.make_async_copy(scratch[n].at[m], outs[n].at[rows], sem))
            copies[-1].start()
    for copy in copies:
        copy.wait()


def finish(entries, squares, groups, sizes):
    arrays, plan = distinct(groups)
    feats = arrays[0].shape[-1]
    scratch = [
        pltpu.VMEM((len(group), size, feats), jnp.float32) for group, size in zip(groups, sizes)
    ]
    outs = tuple(
        jax.ShapeDtypeStruct((len(group) * size, feats), jnp.float32)
        for group, size in zip(groups, sizes)
    )
    count = sum(len(group) for group in groups)
    return pl.pallas_call(
        functools.partial(finish_kernel, entries, plan, len(squares)),
        out_shape=outs,
        in_specs=[vmem_spec()] * (len(squares) + len(arrays)),
        out_specs=(pl.BlockSpec(memory_space=pltpu.HBM),) * len(outs),
        scratch_shapes=scratch + [pltpu.SemaphoreType.DMA((count,))],
        compiler_params=params(12),
        name="finish",
    )(*squares, *arrays)


def swap(own, axis, mask):
    return lax.ppermute(own, axis, [(i, i ^ mask) for i in range(lax.axis_size(axis))])


def bits_of(axis):
    count = lax.axis_size(axis)
    bits = count.bit_length() - 1
    if count != 1 << bits:
        raise ValueError("axis size")
    return bits


def far_first(own, axis, step, count):
    return [swap(own, axis, m * step) for m in reversed(range(1, count))]


def proto_parts(own):
    return far_first(own, "proto", 1, lax.axis_size("proto")) + [own]


def batch_parts(own):
    pair = own + swap(own, "batch", 1)
    return far_first(pair, "batch", 2, lax.axis_size("batch") // 2) + [pair]


def scatter_sums(groups):
    stage, terms = 0, [None] * len(groups)
    state = list(groups)
    while any(term is None for term in terms):
        live = [n for n in range(len(state)) if terms[n] is None]
        recvs = {}
        for n in live:
            axis, order, send, keep = state[n]
            recvs[n] = swap(send, axis, 1 << order[stage])
        going = []
        for n in live:
            axis, order, send, keep = state[n]
            if stage + 1 == len(order):
                terms[n] = (keep, recvs[n])
            else:
                going.append(n)
        if going:
            arrays = [x for n in going for x in (state[n][3], recvs[n])]
            split = split_add(arrays, [(2 * i, 2 * i + 1, None) for i in range(len(going))])
            for n, (send, keep) in zip(going, split):
                state[n] = (state[n][0], state[n][1], send, keep)
        stage += 1
    return [x for term in terms for x in term]


def forward_kernel(near_ref, far_ref, x_ref, y_ref, pack_ref, slow_ref, fast_ref):
    pack_ref[0] = near_ref[...]
    pack_ref[1] = far_ref[...]
    slow_ref[...] = y_ref[0]
    fast_ref[...] = x_ref[1]


def forwards(near, far, x, y):
    view = jax.ShapeDtypeStruct(x.shape[1:], x.dtype)
    return pl.pallas_call(
        forward_kernel,
        out_shape=(jax.ShapeDtypeStruct((2,) + near.shape, near.dtype), view, view),
        in_specs=[vmem_spec()] * 4,
        out_specs=(vmem_spec(),) * 3,
        compiler_params=params(10),
        name="forwards",
    )(near, far, x, y)


def copy_kernel(x_ref, *refs):
    refs[-1][...] = x_ref[...]


def copy_after(x, arrived):
    return pl.pallas_call(
        copy_kernel,
        out_shape=jax.ShapeDtypeStruct(x.shape, x.dtype),
        in_specs=[vmem_spec()] + [pl.BlockSpec(memory_space=pl.ANY)] * len(arrived),
        out_specs=vmem_spec(),
        compiler_params=params(8),
        name="copy_after",
    )(x, *arrived)


def gather_pairs(proto, embed):
    y, x = swap(embed, "proto", 2), swap(embed, "proto", 1)
    far, near = swap(proto, "batch", 4), swap(proto, "batch", 2)
    core = swap(proto, "batch", 1)
    pack, slow, fast = forwards(near, far, x, y)
    slow, fast = swap(slow, "proto", 1), swap(fast, "proto", 2)
    corner = swap(far, "batch", 2)
    core_pack = swap(pack, "batch", 1)
    core_corner = swap(copy_after(corner, [slow, fast]), "batch", 1)
    whole = [proto, core, near, (core_pack, 0), far, (core_pack, 1), corner, core_corner]
    protos = [piece if isinstance(piece, tuple) else (piece, None) for piece in whole]
    return protos, [[(embed, v), (x, v), (y, v), (last, None)] for v, last in enumerate((slow, fast))]


def gather_batch(own):
    bits = list(reversed(range(lax.axis_size("batch").bit_length() - 1)))
    pieces = {0: own}
    first = {bit: swap(own, "batch", 1 << bit) for bit in bits}
    for bit in bits:
        for m in list(pieces):
            pieces[m | 1 << bit] = first[bit] if m == 0 else swap(pieces[m], "batch", 1 << bit)
    return [(pieces[m], None) for m in range(len(pieces))]


def gather_views(own, orders):
    first = {bit: swap(own, "proto", 1 << bit) for bit in sorted(orders[0])}
    groups = []
    for v, order in enumerate(orders):
        pieces = {0: (own, v)}
        for bit in order:
            for m in list(pieces):
                if m == 0:
                    pieces[1 << bit] = (first[bit], v)
                else:
                    array, view = pieces[m]
                    piece = array if view is None else array[view]
                    pieces[m | 1 << bit] = (swap(piece, "proto", 1 << bit), None)
        groups.append([pieces[m] for m in range(len(pieces))])
    return groups


def body(slow_embed, fast_embed, prototypes):
    clip_dev, feat_width = slow_embed.shape
    proto_dev = prototypes.shape[0]
    batch_count = lax.axis_size("batch")
    proto_count = lax.axis_size("proto")
    clips_all = clip_dev * batch_count
    protos_all = proto_dev * proto_count
    proto_entries = float(protos_all * feat_width)
    embed_entries = float(2 * clips_all * feat_width)
    batch_bits, proto_bits = bits_of("batch"), bits_of("proto")
    me_batch, me_proto = lax.axis_index("batch"), lax.axis_index("proto")

    t, col, den, unit_bt, proto_b = scores(slow_embed, fast_embed, prototypes)
    for iteration in range(ITERS):
        rows, r = row_pass(t, den, batch_parts(col), protos_all, iteration == 0)
        row_parts = proto_parts(rows)
        if iteration == 0:
            den_parts = row_parts
        if iteration + 1 < ITERS:
            col = col_pass(t, row_parts, clips_all)

    near = tuple(range(batch_bits - 1))
    batch_orders = (near, tuple(reversed(near)))
    proto_orders = (tuple(range(proto_bits)), tuple(reversed(range(proto_bits))))
    send, g = send_gradients(t, r, unit_bt, row_parts, den_parts, batch_orders)
    shares = embed_gradients(g, proto_b, proto_orders)
    keep = keep_gradients(g, unit_bt, shares[0], batch_orders)

    proto_rows = proto_dev // batch_count
    clip_rows = clip_dev // proto_count
    raws = [lax.dynamic_slice_in_dim(prototypes, me_batch * proto_rows, proto_rows, 0)]
    for x in (slow_embed, fast_embed):
        raws.append(lax.dynamic_slice_in_dim(x, me_proto * clip_rows, clip_rows, 0))
    recv = swap(send, "batch", 1)
    halves = split_add([keep, recv], [(0, 1, h) for h in range(2)])
    groups = []
    for h in range(2):
        order = tuple(bit + 1 for bit in batch_orders[h])
        groups.append(("batch", order) + tuple(halves[h]))
    for v in range(2):
        groups.append(("proto", proto_orders[v], shares[2 * v], shares[2 * v + 1]))
    terms = scatter_sums(groups)
    grad_proto, grad_embed = project_shares(raws, terms)
    if batch_bits == 3 and proto_bits == 2:
        proto_pieces, view_pieces = gather_pairs(grad_proto, grad_embed)
    else:
        proto_pieces = gather_batch(grad_proto)
        view_pieces = gather_views(grad_embed, (proto_orders[1], proto_orders[0]))
    square = sum_squares(proto_pieces[::2], proto_rows)
    squares = proto_parts(square + swap(square, "batch", 1))
    sizes = (proto_rows, clip_rows, clip_rows)
    groups = [proto_pieces] + view_pieces
    return finish((proto_entries, embed_entries), squares, groups, sizes)


def solution(mesh):
    placed = (P("batch", None), P("batch", None), P("proto", None))
    return jax.shard_map(
        body,
        mesh=mesh,
        in_specs=placed,
        out_specs=(P("proto", None), P("batch", None), P("batch", None)),
        check_vma=False,
    )
```

```python
import functools

import jax
import jax.numpy as jnp
from jax import lax
from jax.experimental import pallas as pl
from jax.experimental.pallas import tpu as pltpu
from jax.sharding import PartitionSpec as P

ITERS = 3


CODE_EPS = 0.05
TEMPER = 0.1
NORM_EPS = 1e-06
LANES = 128
MIB = 1024 * 1024


def vmem_spec():
    return pl.BlockSpec(memory_space=pltpu.VMEM)


def params(limit):
    return pltpu.CompilerParams(vmem_limit_bytes=limit * MIB)


def to_columns(line):
    return jnp.broadcast_to(line, (LANES, LANES)).T


def to_line(partial):
    return jnp.sum(partial.T, axis=0, keepdims=True)


def lane_sum(block):
    total = block[:, :LANES]
    for j in range(1, block.shape[1] // LANES):
        total = total + block[:, j * LANES : (j + 1) * LANES]
    return total


def row_fold(block):
    return jnp.sum(block.reshape(block.shape[0] // 8, 8, block.shape[1]), axis=0)


def sum_of(refs, first=0, size=None):
    size = refs[0].shape[0] if size is None else size
    total = refs[0][first : first + size, :]
    for ref in refs[1:]:
        total = total + ref[first : first + size, :]
    return total


LOG2E = 1.4426950408889634


def score_kernel(slow, fast, protos, t_ref, col_ref, den_ref, ub_ref, cb_ref, raw_s, w_s, den_s, sems):
    clips, feats = slow.shape
    count = protos.shape[0]
    loads = []
    for v, src in enumerate((slow, fast)):
        loads.append(pltpu.make_async_copy(src, raw_s.at[v], sems.at[v]))
    loads.append(pltpu.make_async_copy(protos, w_s, sems.at[2]))
    for load in loads:
        load.start()
    for v in range(2):
        loads[v].wait()
        for first in range(0, clips, 256):
            rows = pl.ds(first, 256)
            x = raw_s[v, rows, :].astype(jnp.float32)
            length = jnp.sqrt(jnp.sum(x * x, axis=-1, keepdims=True) + 1e-12)
            ub_ref[v, rows, :] = (x / length).astype(jnp.bfloat16)
    den_s[...] = jnp.zeros_like(den_s)
    loads[2].wait()

    def chunk(j, _):
        first = pl.multiple_of(j * 256, 256)
        w = w_s[pl.ds(first, 256), :]
        length = jnp.sqrt(jnp.sum(w * w, axis=-1, keepdims=True) + 1e-12)
        c = w / length
        cb_ref[pl.ds(first, 256), :] = c.astype(jnp.bfloat16)
        weights = c.T.astype(jnp.bfloat16)
        for v in range(2):
            cols = jnp.zeros((8, 256), jnp.float32)
            for r in range(0, clips, 512):
                s = jnp.dot(
                    ub_ref[v, r : r + 512, :], weights, preferred_element_type=jnp.float32
                )
                for q in range(0, 512, 64):
                    rows = pl.ds(r + q, 64)
                    t = jnp.exp2(s[q : q + 64] * (LOG2E / TEMPER))
                    t_ref[v, rows, pl.ds(first, 256)] = t
                    cols = cols + row_fold(t * t)
                    den_s[v, rows, :] += lane_sum(t)
            line = jnp.sum(cols, axis=0, keepdims=True)
            for h in range(2):
                col_ref[pl.ds(v * (count // LANES) + j * 2 + h, 1), :] = line[
                    :, h * LANES : (h + 1) * LANES
                ]
        return 0

    lax.fori_loop(0, count // 256, chunk, 0)
    groups = clips // LANES
    for v in range(2):
        for i in range(groups):
            den_ref[pl.ds(v * groups + i, 1), :] = to_line(den_s[v, i * LANES : (i + 1) * LANES, :])


def scores(slow, fast, protos):
    clips, feats = slow.shape
    count = protos.shape[0]
    return pl.pallas_call(
        score_kernel,
        out_shape=(
            pltpu.VMEM((2, clips, count), jnp.float32),
            jax.ShapeDtypeStruct((2 * count // LANES, LANES), jnp.float32),
            jax.ShapeDtypeStruct((2 * clips // LANES, LANES), jnp.float32),
            jax.ShapeDtypeStruct((2, clips, feats), jnp.bfloat16),
            jax.ShapeDtypeStruct((count, feats), jnp.bfloat16),
        ),
        in_specs=[pl.BlockSpec(memory_space=pltpu.HBM)] * 3,
        out_specs=(vmem_spec(),) * 5,
        scratch_shapes=[
            pltpu.VMEM((2, clips, feats), jnp.bfloat16),
            pltpu.VMEM((count, feats), jnp.float32),
            pltpu.VMEM((2, clips, LANES), jnp.float32),
            pltpu.SemaphoreType.DMA((3,)),
        ],
        compiler_params=params(24),
        name="scores",
    )(*[pltpu.with_memory_space_constraint(x, pltpu.HBM) for x in (slow, fast, protos)])


def turn_kernel(ub_ref, ubt_ref):
    clips = ub_ref.shape[1]
    for v in range(2):
        for first in range(0, clips, 256):
            u = ub_ref[v, first : first + 256, :].astype(jnp.float32)
            ubt_ref[:, v * clips + first : v * clips + first + 256] = u.T.astype(jnp.bfloat16)


def turned(ub):
    clips, feats = ub.shape[1:]
    return pl.pallas_call(
        turn_kernel,
        out_shape=jax.ShapeDtypeStruct((feats, 2 * clips), ub.dtype),
        in_specs=[vmem_spec()],
        out_specs=vmem_spec(),
        compiler_params=params(8),
        cost_estimate=pl.CostEstimate(
            flops=2 * clips * feats, bytes_accessed=4 * MIB, transcendentals=0
        ),
        name="turned",
    )(ub)


def row_kernel(protos_all, extra, t_ref, den_ref, *refs):
    col_parts, (row_ref, r_ref, acc_s) = refs[:-3], refs[-3:]
    clips, count = t_ref.shape[1:]
    groups, lines = clips // LANES, count // LANES
    r_ref[...] = 1.0 / (float(protos_all) * sum_of(col_parts))
    if extra:
        row_ref[2 * groups :, :] = den_ref[...]
    for v in range(2):

        def step(i, _, v=v):
            rows = pl.ds(pl.multiple_of(i * LANES, LANES), LANES)
            acc = jnp.zeros((LANES, LANES), jnp.float32)
            for j in range(lines):
                t = t_ref[v, rows, j * LANES : (j + 1) * LANES]
                acc = acc + t * t * r_ref[v * lines + j : v * lines + j + 1, :]
            acc_s[pl.ds(pl.multiple_of((v * groups + i) * LANES, LANES), LANES), :] = acc
            return 0

        lax.fori_loop(0, groups, step, 0)
    for line in range(2 * groups):
        row_ref[line : line + 1, :] = to_line(acc_s[line * LANES : (line + 1) * LANES, :])


def row_pass(t, den, col_parts, protos_all, extra):
    clips, count = t.shape[1:]
    lines = 2 * clips // LANES * (2 if extra else 1)
    return pl.pallas_call(
        functools.partial(row_kernel, protos_all, extra),
        out_shape=(
            jax.ShapeDtypeStruct((lines, LANES), jnp.float32),
            jax.ShapeDtypeStruct((2 * count // LANES, LANES), jnp.float32),
        ),
        in_specs=[vmem_spec()] * (2 + len(col_parts)),
        out_specs=(vmem_spec(),) * 2,
        scratch_shapes=[pltpu.VMEM((2 * clips, LANES), jnp.float32)],
        compiler_params=params(8),
        name="row_pass",
    )(pltpu.with_memory_space_constraint(t, pltpu.VMEM), den, *col_parts)


def col_kernel(clips_all, t_ref, *refs):
    row_parts, (col_ref, acc_s, s_s) = refs[:-3], refs[-3:]
    clips, count = t_ref.shape[1:]
    groups, lines = clips // LANES, count // LANES
    s_s[...] = 1.0 / (float(clips_all) * sum_of(row_parts, 0, 2 * groups))
    acc_s[...] = jnp.zeros_like(acc_s)
    for v in range(2):

        def step(i, _, v=v):
            rows = pl.ds(pl.multiple_of(i * LANES, LANES), LANES)
            scale = to_columns(s_s[pl.ds(v * groups + i, 1), :])
            for j in range(lines):
                span = slice(j * LANES, (j + 1) * LANES)
                t = t_ref[v, rows, span]
                acc_s[v, :, span] += row_fold(t * t * scale)
            return 0

        lax.fori_loop(0, groups, step, 0)
        for j in range(lines):
            col_ref[v * lines + j : v * lines + j + 1, :] = jnp.sum(
                acc_s[v, :, j * LANES : (j + 1) * LANES], axis=0, keepdims=True
            )


def col_pass(t, row_parts, clips_all):
    clips, count = t.shape[1:]
    return pl.pallas_call(
        functools.partial(col_kernel, clips_all),
        out_shape=jax.ShapeDtypeStruct((2 * count // LANES, LANES), jnp.float32),
        in_specs=[vmem_spec()] * (1 + len(row_parts)),
        out_specs=vmem_spec(),
        scratch_shapes=[
            pltpu.VMEM((2, 8, count), jnp.float32),
            pltpu.VMEM((2 * clips // LANES, LANES), jnp.float32),
        ],
        compiler_params=params(8),
        name="col_pass",
    )(pltpu.with_memory_space_constraint(t, pltpu.VMEM), *row_parts)


def piece_of(position, order):
    steps = len(order)
    return sum(((position >> (steps - 1 - j)) & 1) << bit for j, bit in enumerate(order))


def place_of(piece, order):
    steps = len(order)
    return sum(((piece >> bit) & 1) << (steps - 1 - j) for j, bit in enumerate(order))


def chunk_span(m, width):
    which = jnp.bitwise_xor(lax.axis_index("batch"), m)
    return which, pl.multiple_of(which * width, width)


def proto_grads(ubt, chunk, orders, i, out_ref):
    dct = jnp.dot(ubt, chunk, preferred_element_type=jnp.float32)
    half = dct.shape[0] // 2
    for h in range(2):
        out_ref[h, place_of(i, orders[h])] = dct[h * half : (h + 1) * half]


def send_kernel(orders, parts, t_ref, r_ref, ubt_ref, *refs):
    row_parts, den_parts = refs[:parts], refs[parts : 2 * parts]
    send_ref, g_ref, chunk_s, code_s, prob_s = refs[2 * parts :]
    clips, count = t_ref.shape[1:]
    groups, lines = clips // LANES, count // LANES
    pieces = 1 << len(orders[0])
    width = count // (2 * pieces)
    code = (1.0 / TEMPER) / sum_of(row_parts, 0, 2 * groups)
    prob = (1.0 / TEMPER) / sum_of(den_parts, 2 * groups, 2 * groups)
    for v in range(2):
        for i in range(groups):
            line = v * groups + i
            rows = slice(i * LANES, (i + 1) * LANES)
            code_s[v, rows, :] = to_columns(code[line : line + 1, :])
            prob_s[v, rows, :] = to_columns(prob[line : line + 1, :])

    def score_grads(m, keep_chunk):
        which, first = chunk_span(m, width)
        for i in range(0, clips, 32):
            rows = slice(i, i + 32)
            codes = [code_s[v, rows, :] for v in range(2)]
            probs = [prob_s[v, rows, :] for v in range(2)]
            for h in range(width // LANES):
                span = pl.ds(first + h * LANES, LANES)
                line = which * (width // LANES) + h
                t = [t_ref[v, rows, span] for v in range(2)]
                q = [
                    t[v] * t[v] * r_ref[pl.ds(v * lines + line, 1), :] * codes[v]
                    for v in range(2)
                ]
                for v in range(2):
                    g = (t[v] * probs[v] - q[1 - v]).astype(jnp.bfloat16)
                    own = slice(v * clips + i, v * clips + i + 32)
                    g_ref[own, span] = g
                    if keep_chunk:
                        chunk_s[own, h * LANES : (h + 1) * LANES] = g

    def pair(i, _):
        score_grads(2 * i + 1, True)
        score_grads(2 * i, False)
        proto_grads(ubt_ref[...], chunk_s[...], orders, i, send_ref)
        return 0

    lax.fori_loop(0, pieces, pair, 0)


def send_gradients(t, r, ubt, row_parts, den_parts, orders):
    clips, count = t.shape[1:]
    feats = ubt.shape[0]
    pieces = 1 << len(orders[0])
    width = count // (2 * pieces)
    return pl.pallas_call(
        functools.partial(send_kernel, orders, len(row_parts)),
        out_shape=(
            jax.ShapeDtypeStruct((2, pieces, feats // 2, width), jnp.float32),
            pltpu.VMEM((2 * clips, count), jnp.bfloat16),
        ),
        in_specs=[vmem_spec()] * (3 + 2 * len(row_parts)),
        out_specs=(vmem_spec(),) * 2,
        scratch_shapes=[
            pltpu.VMEM((2 * clips, width), jnp.bfloat16),
            pltpu.VMEM((2, clips, LANES), jnp.float32),
            pltpu.VMEM((2, clips, LANES), jnp.float32),
        ],
        compiler_params=params(14),
        cost_estimate=pl.CostEstimate(
            flops=2 * clips * count * feats, bytes_accessed=20 * MIB, transcendentals=0
        ),
        name="send_gradients",
    )(pltpu.with_memory_space_constraint(t, pltpu.VMEM), r, ubt, *row_parts, *den_parts)


def embed_grad_kernel(orders, g_ref, cb_ref, *outs):
    clips = g_ref.shape[0] // 2
    peers = 1 << len(orders[0])
    size = clips // peers
    for v in range(2):
        for place in range(peers):
            which = jnp.bitwise_xor(lax.axis_index("proto"), piece_of(place, orders[v]))
            rows = pl.ds(pl.multiple_of(v * clips + which * size, size), size)
            out_ref = outs[2 * v + (0 if place >= peers // 2 else 1)]
            out_ref[place % (peers // 2)] = jnp.dot(
                g_ref[rows, :], cb_ref[...], preferred_element_type=jnp.float32
            )


def embed_gradients(g, cb, orders):
    clips, count = g.shape[0] // 2, g.shape[1]
    feats = cb.shape[1]
    peers = 1 << len(orders[0])
    share = jax.ShapeDtypeStruct((peers // 2, clips // peers, feats), jnp.float32)
    return pl.pallas_call(
        functools.partial(embed_grad_kernel, orders),
        out_shape=(share,) * 4,
        in_specs=[vmem_spec()] * 2,
        out_specs=(vmem_spec(),) * 4,
        compiler_params=params(14),
        cost_estimate=pl.CostEstimate(
            flops=4 * clips * count * feats, bytes_accessed=11 * MIB, transcendentals=0
        ),
        name="embed_gradients",
    )(pltpu.with_memory_space_constraint(g, pltpu.VMEM), cb)


def keep_kernel(orders, g_ref, ubt_ref, after_ref, keep_ref):
    pieces = 1 << len(orders[0])
    width = g_ref.shape[1] // (2 * pieces)

    def step(i, _):
        _, first = chunk_span(2 * i, width)
        proto_grads(ubt_ref[...], g_ref[:, pl.ds(first, width)], orders, i, keep_ref)
        return 0

    lax.fori_loop(0, pieces, step, 0)


def keep_gradients(g, ubt, after, orders):
    count = g.shape[1]
    feats, clips = ubt.shape
    pieces = 1 << len(orders[0])
    return pl.pallas_call(
        functools.partial(keep_kernel, orders),
        out_shape=jax.ShapeDtypeStruct((2, pieces, feats // 2, count // (2 * pieces)), jnp.float32),
        in_specs=[vmem_spec()] * 2 + [pl.BlockSpec(memory_space=pl.ANY)],
        out_specs=vmem_spec(),
        compiler_params=params(14),
        cost_estimate=pl.CostEstimate(
            flops=clips * count * feats, bytes_accessed=6 * MIB, transcendentals=0
        ),
        name="keep_gradients",
    )(pltpu.with_memory_space_constraint(g, pltpu.VMEM), ubt, after)


def split_add_kernel(plan, inputs, *refs):
    ins, outs = refs[:inputs], refs[inputs:]
    for n, (keep_place, recv_place, part) in enumerate(plan):
        keep, recv = ins[keep_place], ins[recv_place]
        if part is not None:
            keep, recv = keep.at[part], recv.at[part]
        send_out, keep_out = outs[2 * n : 2 * n + 2]
        half = keep_out.shape[0]
        keep_out[...] = keep[:half] + recv[:half]
        send_out[...] = keep[half:] + recv[half:]


def split_add(arrays, plan):
    halves = []
    for place, _, part in plan:
        shape = arrays[place].shape if part is None else arrays[place].shape[1:]
        halves += [jax.ShapeDtypeStruct((shape[0] // 2,) + shape[1:], jnp.float32)] * 2
    outs = pl.pallas_call(
        functools.partial(split_add_kernel, plan, len(arrays)),
        out_shape=tuple(halves),
        in_specs=[vmem_spec()] * len(arrays),
        out_specs=(vmem_spec(),) * len(halves),
        compiler_params=params(12),
        name="split_add",
    )(*arrays)
    return [(outs[2 * n], outs[2 * n + 1]) for n in range(len(plan))]


def project(raw, grad):
    x = raw.astype(jnp.float32)
    length = jnp.sqrt(jnp.sum(x * x, axis=-1, keepdims=True) + 1e-12)
    unit = x / length
    along = jnp.sum(unit * grad, axis=-1, keepdims=True)
    return (grad - unit * along) / length


EXTRA = 8


def share_kernel(proto_raw, slow_raw, fast_raw, *refs):
    terms, (proto_out, embed_out) = refs[:-2], refs[-2:]
    count = proto_raw.shape[0]
    squares = [jnp.zeros((8, LANES), jnp.float32)] * 2
    halves = [terms[2 * h][0] + terms[2 * h + 1][0] for h in range(2)]
    grad = project(proto_raw[...], jnp.concatenate(halves, axis=0).T)
    proto_out[:count, :] = grad
    squares[0] = row_fold(lane_sum(grad * grad))
    for v, raw in enumerate((slow_raw, fast_raw)):
        grad = project(raw[...], terms[4 + 2 * v][0] + terms[5 + 2 * v][0])
        embed_out[v] = grad
        squares[1] = squares[1] + row_fold(lane_sum(grad * grad))
    for kind in range(2):
        total = jnp.sum(jnp.sum(squares[kind], axis=0, keepdims=True), axis=1, keepdims=True)
        proto_out[count:, kind * LANES : (kind + 1) * LANES] = jnp.broadcast_to(total, (EXTRA, LANES))


def project_shares(raws, terms):
    rows, feats = raws[1].shape
    count = raws[0].shape[0]
    return pl.pallas_call(
        share_kernel,
        out_shape=(
            jax.ShapeDtypeStruct((count + EXTRA, feats), jnp.float32),
            jax.ShapeDtypeStruct((2, rows, feats), jnp.float32),
        ),
        in_specs=[vmem_spec()] * (len(raws) + len(terms)),
        out_specs=(vmem_spec(),) * 2,
        compiler_params=params(10),
        name="project_shares",
    )(*raws, *terms)


def tree_sum(terms):
    while len(terms) > 1:
        terms = [terms[i] + terms[i + 1] for i in range(0, len(terms), 2)]
    return terms[0]


def distinct(groups):
    arrays, plan = [], []
    for group in groups:
        places = []
        for array, part in group:
            place = next((i for i, known in enumerate(arrays) if known is array), None)
            if place is None:
                place = len(arrays)
                arrays.append(array)
            places.append((place, part))
        plan.append(places)
    return arrays, plan


def piece_ref(ins, place, part):
    return ins[place] if part is None else ins[place].at[part]


def squares_kernel(plan, rows, *refs):
    ins, out_ref = refs[:-1], refs[-1]
    total = tree_sum([piece_ref(ins, *piece)[rows:, :] for piece in plan])
    for kind in range(2):
        out_ref[kind] = total[:, kind * LANES : (kind + 1) * LANES]


def sum_squares(pieces, rows):
    arrays, plan = distinct([pieces])
    return pl.pallas_call(
        functools.partial(squares_kernel, plan[0], rows),
        out_shape=jax.ShapeDtypeStruct((2, 8, LANES), jnp.float32),
        in_specs=[vmem_spec()] * len(arrays),
        out_specs=vmem_spec(),
        compiler_params=params(8),
        cost_estimate=pl.CostEstimate(flops=8, bytes_accessed=8, transcendentals=0),
        name="sum_squares",
    )(*arrays)


def finish_kernel(entries, plan, count, *refs):
    squares, ins, outs = refs[:count], refs[count:-7], refs[-7:-4]
    scratch, sems = refs[-4:-1], refs[-1]
    total = tree_sum([square[...] for square in squares])
    factors = [lax.rsqrt(total[k, 0:1, 0:1] / entries[k] + NORM_EPS) for k in range(2)]
    copies = []
    for n, pieces in enumerate(plan):
        axis, kind = ("batch", 0) if n == 0 else ("proto", 1)
        size = scratch[n].shape[1]
        for m, piece in enumerate(pieces):
            which = jnp.bitwise_xor(lax.axis_index(axis), m)
            rows = pl.ds(pl.multiple_of(which * size, size), size)
            scratch[n][m] = piece_ref(ins, *piece)[:size, :] * factors[kind]
            sem = sems.at[len(copies)]
            copies.append(pltpu.make_async_copy(scratch[n].at[m], outs[n].at[rows], sem))
            copies[-1].start()
    for copy in copies:
        copy.wait()


def finish(entries, squares, groups, sizes):
    arrays, plan = distinct(groups)
    feats = arrays[0].shape[-1]
    scratch = [
        pltpu.VMEM((len(group), size, feats), jnp.float32) for group, size in zip(groups, sizes)
    ]
    outs = tuple(
        jax.ShapeDtypeStruct((len(group) * size, feats), jnp.float32)
        for group, size in zip(groups, sizes)
    )
    count = sum(len(group) for group in groups)
    return pl.pallas_call(
        functools.partial(finish_kernel, entries, plan, len(squares)),
        out_shape=outs,
        in_specs=[vmem_spec()] * (len(squares) + len(arrays)),
        out_specs=(pl.BlockSpec(memory_space=pltpu.HBM),) * len(outs),
        scratch_shapes=scratch + [pltpu.SemaphoreType.DMA((count,))],
        compiler_params=params(12),
        name="finish",
    )(*squares, *arrays)


def swap(own, axis, mask):
    return lax.ppermute(own, axis, [(i, i ^ mask) for i in range(lax.axis_size(axis))])


def bits_of(axis):
    count = lax.axis_size(axis)
    bits = count.bit_length() - 1
    if count != 1 << bits:
        raise ValueError("axis size")
    return bits


def far_first(own, axis, step, count):
    return [swap(own, axis, m * step) for m in reversed(range(1, count))]


def proto_parts(own):
    return far_first(own, "proto", 1, lax.axis_size("proto")) + [own]


def batch_parts(own):
    pair = own + swap(own, "batch", 1)
    return far_first(pair, "batch", 2, lax.axis_size("batch") // 2) + [pair]


def scatter_sums(groups):
    stage, terms = 0, [None] * len(groups)
    state = list(groups)
    while any(term is None for term in terms):
        live = [n for n in range(len(state)) if terms[n] is None]
        recvs = {}
        for n in live:
            axis, order, send, keep = state[n]
            recvs[n] = swap(send, axis, 1 << order[stage])
        going = []
        for n in live:
            axis, order, send, keep = state[n]
            if stage + 1 == len(order):
                terms[n] = (keep, recvs[n])
            else:
                going.append(n)
        if going:
            arrays = [x for n in going for x in (state[n][3], recvs[n])]
            split = split_add(arrays, [(2 * i, 2 * i + 1, None) for i in range(len(going))])
            for n, (send, keep) in zip(going, split):
                state[n] = (state[n][0], state[n][1], send, keep)
        stage += 1
    return [x for term in terms for x in term]


def gather_batch(own):
    bits = list(reversed(range(lax.axis_size("batch").bit_length() - 1)))
    pieces = {0: own}
    first = {bit: swap(own, "batch", 1 << bit) for bit in bits}
    for bit in bits:
        for m in list(pieces):
            pieces[m | 1 << bit] = first[bit] if m == 0 else swap(pieces[m], "batch", 1 << bit)
    return [(pieces[m], None) for m in range(len(pieces))]


def gather_views(own, orders):
    first = {bit: swap(own, "proto", 1 << bit) for bit in sorted(orders[0])}
    groups = []
    for v, order in enumerate(orders):
        pieces = {0: (own, v)}
        for bit in order:
            for m in list(pieces):
                if m == 0:
                    pieces[1 << bit] = (first[bit], v)
                else:
                    array, view = pieces[m]
                    piece = array if view is None else array[view]
                    pieces[m | 1 << bit] = (swap(piece, "proto", 1 << bit), None)
        groups.append([pieces[m] for m in range(len(pieces))])
    return groups


def body(slow_embed, fast_embed, prototypes):
    clip_dev, feat_width = slow_embed.shape
    proto_dev = prototypes.shape[0]
    batch_count = lax.axis_size("batch")
    proto_count = lax.axis_size("proto")
    clips_all = clip_dev * batch_count
    protos_all = proto_dev * proto_count
    proto_entries = float(protos_all * feat_width)
    embed_entries = float(2 * clips_all * feat_width)
    batch_bits, proto_bits = bits_of("batch"), bits_of("proto")
    me_batch, me_proto = lax.axis_index("batch"), lax.axis_index("proto")

    t, col, den, unit_b, proto_b = scores(slow_embed, fast_embed, prototypes)
    unit_bt = turned(unit_b)
    for iteration in range(ITERS):
        rows, r = row_pass(t, den, batch_parts(col), protos_all, iteration == 0)
        row_parts = proto_parts(rows)
        if iteration == 0:
            den_parts = row_parts
        if iteration + 1 < ITERS:
            col = col_pass(t, row_parts, clips_all)

    near = tuple(range(batch_bits - 1))
    batch_orders = (near, tuple(reversed(near)))
    proto_orders = (tuple(range(proto_bits)), tuple(reversed(range(proto_bits))))
    send, g = send_gradients(t, r, unit_bt, row_parts, den_parts, batch_orders)
    shares = embed_gradients(g, proto_b, proto_orders)
    keep = keep_gradients(g, unit_bt, shares[0], batch_orders)

    proto_rows = proto_dev // batch_count
    clip_rows = clip_dev // proto_count
    raws = [lax.dynamic_slice_in_dim(prototypes, me_batch * proto_rows, proto_rows, 0)]
    for x in (slow_embed, fast_embed):
        raws.append(lax.dynamic_slice_in_dim(x, me_proto * clip_rows, clip_rows, 0))
    recv = swap(send, "batch", 1)
    halves = split_add([keep, recv], [(0, 1, h) for h in range(2)])
    groups = []
    for h in range(2):
        order = tuple(bit + 1 for bit in batch_orders[h])
        groups.append(("batch", order) + tuple(halves[h]))
    for v in range(2):
        groups.append(("proto", proto_orders[v], shares[2 * v], shares[2 * v + 1]))
    terms = scatter_sums(groups)
    grad_proto, grad_embed = project_shares(raws, terms)
    proto_pieces = gather_batch(grad_proto)
    view_pieces = gather_views(grad_embed, (proto_orders[1], proto_orders[0]))
    squares = proto_parts(sum_squares(proto_pieces, proto_rows))
    sizes = (proto_rows, clip_rows, clip_rows)
    groups = [proto_pieces] + view_pieces
    return finish((proto_entries, embed_entries), squares, groups, sizes)


def solution(mesh):
    placed = (P("batch", None), P("batch", None), P("proto", None))
    return jax.shard_map(
        body,
        mesh=mesh,
        in_specs=placed,
        out_specs=(P("proto", None), P("batch", None), P("batch", None)),
        check_vma=False,
    )
```

```python
import functools

import jax
import jax.numpy as jnp
from jax import lax
from jax.experimental import pallas as pl
from jax.experimental.pallas import tpu as pltpu
from jax.sharding import PartitionSpec as P

ITERS = 3


CODE_EPS = 0.05
TEMPER = 0.1
NORM_EPS = 1e-06
LANES = 128
MIB = 1024 * 1024


def vmem_spec():
    return pl.BlockSpec(memory_space=pltpu.VMEM)


def params(limit):
    return pltpu.CompilerParams(vmem_limit_bytes=limit * MIB)


def to_columns(line):
    return jnp.broadcast_to(line, (LANES, LANES)).T


def to_line(partial):
    return jnp.sum(partial.T, axis=0, keepdims=True)


def lane_sum(block):
    total = block[:, :LANES]
    for j in range(1, block.shape[1] // LANES):
        total = total + block[:, j * LANES : (j + 1) * LANES]
    return total


def row_fold(block):
    return jnp.sum(block.reshape(block.shape[0] // 8, 8, block.shape[1]), axis=0)


def sum_of(refs, first=0, size=None):
    size = refs[0].shape[0] if size is None else size
    total = refs[0][first : first + size, :]
    for ref in refs[1:]:
        total = total + ref[first : first + size, :]
    return total


LOG2E = 1.4426950408889634


def score_kernel(slow, fast, protos, t_ref, col_ref, den_ref, ub_ref, cb_ref, raw_s, w_s, den_s, sems):
    clips, feats = slow.shape
    count = protos.shape[0]
    loads = []
    for v, src in enumerate((slow, fast)):
        loads.append(pltpu.make_async_copy(src, raw_s.at[v], sems.at[v]))
    loads.append(pltpu.make_async_copy(protos, w_s, sems.at[2]))
    for load in loads:
        load.start()
    for v in range(2):
        loads[v].wait()
        for first in range(0, clips, 256):
            rows = pl.ds(first, 256)
            x = raw_s[v, rows, :].astype(jnp.float32)
            length = jnp.sqrt(jnp.sum(x * x, axis=-1, keepdims=True) + 1e-12)
            ub_ref[v, rows, :] = (x / length).astype(jnp.bfloat16)
    den_s[...] = jnp.zeros_like(den_s)
    loads[2].wait()

    def chunk(j, _):
        first = pl.multiple_of(j * 256, 256)
        w = w_s[pl.ds(first, 256), :]
        length = jnp.sqrt(jnp.sum(w * w, axis=-1, keepdims=True) + 1e-12)
        c = w / length
        cb_ref[pl.ds(first, 256), :] = c.astype(jnp.bfloat16)
        weights = c.T.astype(jnp.bfloat16)
        for v in range(2):
            cols = jnp.zeros((8, 256), jnp.float32)
            for r in range(0, clips, 512):
                s = jnp.dot(
                    ub_ref[v, r : r + 512, :], weights, preferred_element_type=jnp.float32
                )
                for q in range(0, 512, 64):
                    rows = pl.ds(r + q, 64)
                    t = jnp.exp2(s[q : q + 64] * (LOG2E / TEMPER))
                    t_ref[v, rows, pl.ds(first, 256)] = t
                    cols = cols + row_fold(t * t)
                    den_s[v, rows, :] += lane_sum(t)
            line = jnp.sum(cols, axis=0, keepdims=True)
            for h in range(2):
                col_ref[pl.ds(v * (count // LANES) + j * 2 + h, 1), :] = line[
                    :, h * LANES : (h + 1) * LANES
                ]
        return 0

    lax.fori_loop(0, count // 256, chunk, 0)
    groups = clips // LANES
    for v in range(2):
        for i in range(groups):
            den_ref[pl.ds(v * groups + i, 1), :] = to_line(den_s[v, i * LANES : (i + 1) * LANES, :])


def scores(slow, fast, protos):
    clips, feats = slow.shape
    count = protos.shape[0]
    return pl.pallas_call(
        score_kernel,
        out_shape=(
            pltpu.VMEM((2, clips, count), jnp.float32),
            jax.ShapeDtypeStruct((2 * count // LANES, LANES), jnp.float32),
            jax.ShapeDtypeStruct((2 * clips // LANES, LANES), jnp.float32),
            jax.ShapeDtypeStruct((2, clips, feats), jnp.bfloat16),
            jax.ShapeDtypeStruct((count, feats), jnp.bfloat16),
        ),
        in_specs=[pl.BlockSpec(memory_space=pltpu.HBM)] * 3,
        out_specs=(vmem_spec(),) * 5,
        scratch_shapes=[
            pltpu.VMEM((2, clips, feats), jnp.bfloat16),
            pltpu.VMEM((count, feats), jnp.float32),
            pltpu.VMEM((2, clips, LANES), jnp.float32),
            pltpu.SemaphoreType.DMA((3,)),
        ],
        compiler_params=params(24),
        name="scores",
    )(*[pltpu.with_memory_space_constraint(x, pltpu.HBM) for x in (slow, fast, protos)])


def turn_kernel(ub_ref, ubt_ref):
    clips = ub_ref.shape[1]
    for v in range(2):
        for first in range(0, clips, 256):
            u = ub_ref[v, first : first + 256, :].astype(jnp.float32)
            ubt_ref[:, v * clips + first : v * clips + first + 256] = u.T.astype(jnp.bfloat16)


def turned(ub):
    clips, feats = ub.shape[1:]
    return pl.pallas_call(
        turn_kernel,
        out_shape=jax.ShapeDtypeStruct((feats, 2 * clips), ub.dtype),
        in_specs=[vmem_spec()],
        out_specs=vmem_spec(),
        compiler_params=params(8),
        cost_estimate=pl.CostEstimate(
            flops=2 * clips * feats, bytes_accessed=4 * MIB, transcendentals=0
        ),
        name="turned",
    )(ub)


def row_kernel(protos_all, extra, t_ref, den_ref, *refs):
    col_parts, (row_ref, r_ref, acc_s) = refs[:-3], refs[-3:]
    clips, count = t_ref.shape[1:]
    groups, lines = clips // LANES, count // LANES
    r_ref[...] = 1.0 / (float(protos_all) * sum_of(col_parts))
    if extra:
        row_ref[2 * groups :, :] = den_ref[...]
    for v in range(2):

        def step(i, _, v=v):
            rows = pl.ds(pl.multiple_of(i * LANES, LANES), LANES)
            acc = jnp.zeros((LANES, LANES), jnp.float32)
            for j in range(lines):
                t = t_ref[v, rows, j * LANES : (j + 1) * LANES]
                acc = acc + t * t * r_ref[v * lines + j : v * lines + j + 1, :]
            acc_s[pl.ds(pl.multiple_of((v * groups + i) * LANES, LANES), LANES), :] = acc
            return 0

        lax.fori_loop(0, groups, step, 0)
    for line in range(2 * groups):
        row_ref[line : line + 1, :] = to_line(acc_s[line * LANES : (line + 1) * LANES, :])


def row_pass(t, den, col_parts, protos_all, extra):
    clips, count = t.shape[1:]
    lines = 2 * clips // LANES * (2 if extra else 1)
    return pl.pallas_call(
        functools.partial(row_kernel, protos_all, extra),
        out_shape=(
            jax.ShapeDtypeStruct((lines, LANES), jnp.float32),
            jax.ShapeDtypeStruct((2 * count // LANES, LANES), jnp.float32),
        ),
        in_specs=[vmem_spec()] * (2 + len(col_parts)),
        out_specs=(vmem_spec(),) * 2,
        scratch_shapes=[pltpu.VMEM((2 * clips, LANES), jnp.float32)],
        compiler_params=params(8),
        name="row_pass",
    )(pltpu.with_memory_space_constraint(t, pltpu.VMEM), den, *col_parts)


def col_kernel(clips_all, t_ref, *refs):
    row_parts, (col_ref, acc_s, s_s) = refs[:-3], refs[-3:]
    clips, count = t_ref.shape[1:]
    groups, lines = clips // LANES, count // LANES
    s_s[...] = 1.0 / (float(clips_all) * sum_of(row_parts, 0, 2 * groups))
    acc_s[...] = jnp.zeros_like(acc_s)
    for v in range(2):

        def step(i, _, v=v):
            rows = pl.ds(pl.multiple_of(i * LANES, LANES), LANES)
            scale = to_columns(s_s[pl.ds(v * groups + i, 1), :])
            for j in range(lines):
                span = slice(j * LANES, (j + 1) * LANES)
                t = t_ref[v, rows, span]
                acc_s[v, :, span] += row_fold(t * t * scale)
            return 0

        lax.fori_loop(0, groups, step, 0)
        for j in range(lines):
            col_ref[v * lines + j : v * lines + j + 1, :] = jnp.sum(
                acc_s[v, :, j * LANES : (j + 1) * LANES], axis=0, keepdims=True
            )


def col_pass(t, row_parts, clips_all):
    clips, count = t.shape[1:]
    return pl.pallas_call(
        functools.partial(col_kernel, clips_all),
        out_shape=jax.ShapeDtypeStruct((2 * count // LANES, LANES), jnp.float32),
        in_specs=[vmem_spec()] * (1 + len(row_parts)),
        out_specs=vmem_spec(),
        scratch_shapes=[
            pltpu.VMEM((2, 8, count), jnp.float32),
            pltpu.VMEM((2 * clips // LANES, LANES), jnp.float32),
        ],
        compiler_params=params(8),
        name="col_pass",
    )(pltpu.with_memory_space_constraint(t, pltpu.VMEM), *row_parts)


def piece_of(position, order):
    steps = len(order)
    return sum(((position >> (steps - 1 - j)) & 1) << bit for j, bit in enumerate(order))


def place_of(piece, order):
    steps = len(order)
    return sum(((piece >> bit) & 1) << (steps - 1 - j) for j, bit in enumerate(order))


def chunk_span(m, width):
    which = jnp.bitwise_xor(lax.axis_index("batch"), m)
    return which, pl.multiple_of(which * width, width)


def proto_grads(ubt, chunk, orders, i, out_ref):
    dct = jnp.dot(ubt, chunk, preferred_element_type=jnp.float32)
    half = dct.shape[0] // 2
    for h in range(2):
        out_ref[h, place_of(i, orders[h])] = dct[h * half : (h + 1) * half]


def send_kernel(orders, parts, t_ref, r_ref, ubt_ref, *refs):
    row_parts, den_parts = refs[:parts], refs[parts : 2 * parts]
    send_ref, g_ref, chunk_s, code_s, prob_s = refs[2 * parts :]
    clips, count = t_ref.shape[1:]
    groups, lines = clips // LANES, count // LANES
    pieces = 1 << len(orders[0])
    width = count // (2 * pieces)
    code = (1.0 / TEMPER) / sum_of(row_parts, 0, 2 * groups)
    prob = (1.0 / TEMPER) / sum_of(den_parts, 2 * groups, 2 * groups)
    for v in range(2):
        for i in range(groups):
            line = v * groups + i
            rows = slice(i * LANES, (i + 1) * LANES)
            code_s[v, rows, :] = to_columns(code[line : line + 1, :])
            prob_s[v, rows, :] = to_columns(prob[line : line + 1, :])

    def score_grads(m, keep_chunk):
        which, first = chunk_span(m, width)
        for i in range(0, clips, 32):
            rows = slice(i, i + 32)
            codes = [code_s[v, rows, :] for v in range(2)]
            probs = [prob_s[v, rows, :] for v in range(2)]
            for h in range(width // LANES):
                span = pl.ds(first + h * LANES, LANES)
                line = which * (width // LANES) + h
                t = [t_ref[v, rows, span] for v in range(2)]
                q = [
                    t[v] * t[v] * r_ref[pl.ds(v * lines + line, 1), :] * codes[v]
                    for v in range(2)
                ]
                for v in range(2):
                    g = (t[v] * probs[v] - q[1 - v]).astype(jnp.bfloat16)
                    own = slice(v * clips + i, v * clips + i + 32)
                    g_ref[own, span] = g
                    if keep_chunk:
                        chunk_s[own, h * LANES : (h + 1) * LANES] = g

    def pair(i, _):
        score_grads(2 * i + 1, True)
        score_grads(2 * i, False)
        proto_grads(ubt_ref[...], chunk_s[...], orders, i, send_ref)
        return 0

    lax.fori_loop(0, pieces, pair, 0)


def send_gradients(t, r, ubt, row_parts, den_parts, orders):
    clips, count = t.shape[1:]
    feats = ubt.shape[0]
    pieces = 1 << len(orders[0])
    width = count // (2 * pieces)
    return pl.pallas_call(
        functools.partial(send_kernel, orders, len(row_parts)),
        out_shape=(
            jax.ShapeDtypeStruct((2, pieces, feats // 2, width), jnp.float32),
            pltpu.VMEM((2 * clips, count), jnp.bfloat16),
        ),
        in_specs=[vmem_spec()] * (3 + 2 * len(row_parts)),
        out_specs=(vmem_spec(),) * 2,
        scratch_shapes=[
            pltpu.VMEM((2 * clips, width), jnp.bfloat16),
            pltpu.VMEM((2, clips, LANES), jnp.float32),
            pltpu.VMEM((2, clips, LANES), jnp.float32),
        ],
        compiler_params=params(14),
        cost_estimate=pl.CostEstimate(
            flops=2 * clips * count * feats, bytes_accessed=20 * MIB, transcendentals=0
        ),
        name="send_gradients",
    )(pltpu.with_memory_space_constraint(t, pltpu.VMEM), r, ubt, *row_parts, *den_parts)


def embed_grad_kernel(orders, g_ref, cb_ref, *outs):
    clips = g_ref.shape[0] // 2
    peers = 1 << len(orders[0])
    size = clips // peers
    for v in range(2):
        for place in range(peers):
            which = jnp.bitwise_xor(lax.axis_index("proto"), piece_of(place, orders[v]))
            rows = pl.ds(pl.multiple_of(v * clips + which * size, size), size)
            out_ref = outs[2 * v + (0 if place >= peers // 2 else 1)]
            out_ref[place % (peers // 2)] = jnp.dot(
                g_ref[rows, :], cb_ref[...], preferred_element_type=jnp.float32
            )


def embed_gradients(g, cb, orders):
    clips, count = g.shape[0] // 2, g.shape[1]
    feats = cb.shape[1]
    peers = 1 << len(orders[0])
    share = jax.ShapeDtypeStruct((peers // 2, clips // peers, feats), jnp.float32)
    return pl.pallas_call(
        functools.partial(embed_grad_kernel, orders),
        out_shape=(share,) * 4,
        in_specs=[vmem_spec()] * 2,
        out_specs=(vmem_spec(),) * 4,
        compiler_params=params(14),
        cost_estimate=pl.CostEstimate(
            flops=4 * clips * count * feats, bytes_accessed=11 * MIB, transcendentals=0
        ),
        name="embed_gradients",
    )(pltpu.with_memory_space_constraint(g, pltpu.VMEM), cb)


def keep_kernel(orders, g_ref, ubt_ref, after_ref, keep_ref):
    pieces = 1 << len(orders[0])
    width = g_ref.shape[1] // (2 * pieces)

    def step(i, _):
        _, first = chunk_span(2 * i, width)
        proto_grads(ubt_ref[...], g_ref[:, pl.ds(first, width)], orders, i, keep_ref)
        return 0

    lax.fori_loop(0, pieces, step, 0)


def keep_gradients(g, ubt, after, orders):
    count = g.shape[1]
    feats, clips = ubt.shape
    pieces = 1 << len(orders[0])
    return pl.pallas_call(
        functools.partial(keep_kernel, orders),
        out_shape=jax.ShapeDtypeStruct((2, pieces, feats // 2, count // (2 * pieces)), jnp.float32),
        in_specs=[vmem_spec()] * 2 + [pl.BlockSpec(memory_space=pl.ANY)],
        out_specs=vmem_spec(),
        compiler_params=params(14),
        cost_estimate=pl.CostEstimate(
            flops=clips * count * feats, bytes_accessed=6 * MIB, transcendentals=0
        ),
        name="keep_gradients",
    )(pltpu.with_memory_space_constraint(g, pltpu.VMEM), ubt, after)


def split_add_kernel(plan, inputs, *refs):
    ins, outs = refs[:inputs], refs[inputs:]
    for n, (keep_place, recv_place, part) in enumerate(plan):
        keep, recv = ins[keep_place], ins[recv_place]
        if part is not None:
            keep, recv = keep.at[part], recv.at[part]
        send_out, keep_out = outs[2 * n : 2 * n + 2]
        half = keep_out.shape[0]
        keep_out[...] = keep[:half] + recv[:half]
        send_out[...] = keep[half:] + recv[half:]


def split_add(arrays, plan):
    halves = []
    for place, _, part in plan:
        shape = arrays[place].shape if part is None else arrays[place].shape[1:]
        halves += [jax.ShapeDtypeStruct((shape[0] // 2,) + shape[1:], jnp.float32)] * 2
    outs = pl.pallas_call(
        functools.partial(split_add_kernel, plan, len(arrays)),
        out_shape=tuple(halves),
        in_specs=[vmem_spec()] * len(arrays),
        out_specs=(vmem_spec(),) * len(halves),
        compiler_params=params(12),
        name="split_add",
    )(*arrays)
    return [(outs[2 * n], outs[2 * n + 1]) for n in range(len(plan))]


def project(raw, grad):
    x = raw.astype(jnp.float32)
    length = jnp.sqrt(jnp.sum(x * x, axis=-1, keepdims=True) + 1e-12)
    unit = x / length
    along = jnp.sum(unit * grad, axis=-1, keepdims=True)
    return (grad - unit * along) / length


EXTRA = 8


def share_kernel(proto_raw, slow_raw, fast_raw, *refs):
    terms, (proto_out, embed_out) = refs[:-2], refs[-2:]
    count = proto_raw.shape[0]
    squares = [jnp.zeros((8, LANES), jnp.float32)] * 2
    halves = [terms[2 * h][0] + terms[2 * h + 1][0] for h in range(2)]
    grad = project(proto_raw[...], jnp.concatenate(halves, axis=0).T)
    proto_out[:count, :] = grad
    squares[0] = row_fold(lane_sum(grad * grad))
    for v, raw in enumerate((slow_raw, fast_raw)):
        grad = project(raw[...], terms[4 + 2 * v][0] + terms[5 + 2 * v][0])
        embed_out[v] = grad
        squares[1] = squares[1] + row_fold(lane_sum(grad * grad))
    for kind in range(2):
        total = jnp.sum(jnp.sum(squares[kind], axis=0, keepdims=True), axis=1, keepdims=True)
        proto_out[count:, kind * LANES : (kind + 1) * LANES] = jnp.broadcast_to(total, (EXTRA, LANES))


def project_shares(raws, terms):
    rows, feats = raws[1].shape
    count = raws[0].shape[0]
    return pl.pallas_call(
        share_kernel,
        out_shape=(
            jax.ShapeDtypeStruct((count + EXTRA, feats), jnp.float32),
            jax.ShapeDtypeStruct((2, rows, feats), jnp.float32),
        ),
        in_specs=[vmem_spec()] * (len(raws) + len(terms)),
        out_specs=(vmem_spec(),) * 2,
        compiler_params=params(10),
        name="project_shares",
    )(*raws, *terms)


def tree_sum(terms):
    while len(terms) > 1:
        terms = [terms[i] + terms[i + 1] for i in range(0, len(terms), 2)]
    return terms[0]


def distinct(groups):
    arrays, plan = [], []
    for group in groups:
        places = []
        for array, part in group:
            place = next((i for i, known in enumerate(arrays) if known is array), None)
            if place is None:
                place = len(arrays)
                arrays.append(array)
            places.append((place, part))
        plan.append(places)
    return arrays, plan


def piece_ref(ins, place, part):
    return ins[place] if part is None else ins[place].at[part]


def squares_kernel(plan, rows, *refs):
    ins, out_ref = refs[:-1], refs[-1]
    total = tree_sum([piece_ref(ins, *piece)[rows:, :] for piece in plan])
    for kind in range(2):
        out_ref[kind] = total[:, kind * LANES : (kind + 1) * LANES]


def sum_squares(pieces, rows):
    arrays, plan = distinct([pieces])
    return pl.pallas_call(
        functools.partial(squares_kernel, plan[0], rows),
        out_shape=jax.ShapeDtypeStruct((2, 8, LANES), jnp.float32),
        in_specs=[vmem_spec()] * len(arrays),
        out_specs=vmem_spec(),
        compiler_params=params(8),
        cost_estimate=pl.CostEstimate(flops=8, bytes_accessed=8, transcendentals=0),
        name="sum_squares",
    )(*arrays)


def finish_kernel(entries, plan, count, *refs):
    squares, ins, outs = refs[:count], refs[count:-7], refs[-7:-4]
    scratch, sems = refs[-4:-1], refs[-1]
    total = tree_sum([square[...] for square in squares])
    factors = [lax.rsqrt(total[k, 0:1, 0:1] / entries[k] + NORM_EPS) for k in range(2)]
    copies = []
    for n, pieces in enumerate(plan):
        axis, kind = ("batch", 0) if n == 0 else ("proto", 1)
        size = scratch[n].shape[1]
        for m, piece in enumerate(pieces):
            which = jnp.bitwise_xor(lax.axis_index(axis), m)
            rows = pl.ds(pl.multiple_of(which * size, size), size)
            scratch[n][m] = piece_ref(ins, *piece)[:size, :] * factors[kind]
            sem = sems.at[len(copies)]
            copies.append(pltpu.make_async_copy(scratch[n].at[m], outs[n].at[rows], sem))
            copies[-1].start()
    for copy in copies:
        copy.wait()


def finish(entries, squares, groups, sizes):
    arrays, plan = distinct(groups)
    feats = arrays[0].shape[-1]
    scratch = [
        pltpu.VMEM((len(group), size, feats), jnp.float32) for group, size in zip(groups, sizes)
    ]
    outs = tuple(
        jax.ShapeDtypeStruct((len(group) * size, feats), jnp.float32)
        for group, size in zip(groups, sizes)
    )
    count = sum(len(group) for group in groups)
    return pl.pallas_call(
        functools.partial(finish_kernel, entries, plan, len(squares)),
        out_shape=outs,
        in_specs=[vmem_spec()] * (len(squares) + len(arrays)),
        out_specs=(pl.BlockSpec(memory_space=pltpu.HBM),) * len(outs),
        scratch_shapes=scratch + [pltpu.SemaphoreType.DMA((count,))],
        compiler_params=params(12),
        name="finish",
    )(*squares, *arrays)


def swap(own, axis, mask):
    return lax.ppermute(own, axis, [(i, i ^ mask) for i in range(lax.axis_size(axis))])


def bits_of(axis):
    count = lax.axis_size(axis)
    bits = count.bit_length() - 1
    if count != 1 << bits:
        raise ValueError("axis size")
    return bits


def far_first(own, axis, step, count):
    return [swap(own, axis, m * step) for m in reversed(range(1, count))]


def proto_parts(own):
    return far_first(own, "proto", 1, lax.axis_size("proto")) + [own]


def batch_parts(own, turn):
    pair = own + swap(own, "batch", 1)
    parts = far_first(pair, "batch", 2, lax.axis_size("batch") // 2)
    return parts[turn:] + parts[:turn] + [pair]


def scatter_sums(groups):
    stage, terms = 0, [None] * len(groups)
    state = list(groups)
    while any(term is None for term in terms):
        live = [n for n in range(len(state)) if terms[n] is None]
        recvs = {}
        for n in live:
            axis, order, send, keep = state[n]
            recvs[n] = swap(send, axis, 1 << order[stage])
        going = []
        for n in live:
            axis, order, send, keep = state[n]
            if stage + 1 == len(order):
                terms[n] = (keep, recvs[n])
            else:
                going.append(n)
        if going:
            arrays = [x for n in going for x in (state[n][3], recvs[n])]
            split = split_add(arrays, [(2 * i, 2 * i + 1, None) for i in range(len(going))])
            for n, (send, keep) in zip(going, split):
                state[n] = (state[n][0], state[n][1], send, keep)
        stage += 1
    return [x for term in terms for x in term]


def gather_batch(own):
    bits = list(reversed(range(lax.axis_size("batch").bit_length() - 1)))
    pieces = {0: own}
    first = {bit: swap(own, "batch", 1 << bit) for bit in bits}
    for bit in bits:
        for m in list(pieces):
            pieces[m | 1 << bit] = first[bit] if m == 0 else swap(pieces[m], "batch", 1 << bit)
    return [(pieces[m], None) for m in range(len(pieces))]


def gather_views(own, orders):
    first = {bit: swap(own, "proto", 1 << bit) for bit in sorted(orders[0])}
    groups = []
    for v, order in enumerate(orders):
        pieces = {0: (own, v)}
        for bit in order:
            for m in list(pieces):
                if m == 0:
                    pieces[1 << bit] = (first[bit], v)
                else:
                    array, view = pieces[m]
                    piece = array if view is None else array[view]
                    pieces[m | 1 << bit] = (swap(piece, "proto", 1 << bit), None)
        groups.append([pieces[m] for m in range(len(pieces))])
    return groups


def body(slow_embed, fast_embed, prototypes):
    clip_dev, feat_width = slow_embed.shape
    proto_dev = prototypes.shape[0]
    batch_count = lax.axis_size("batch")
    proto_count = lax.axis_size("proto")
    clips_all = clip_dev * batch_count
    protos_all = proto_dev * proto_count
    proto_entries = float(protos_all * feat_width)
    embed_entries = float(2 * clips_all * feat_width)
    batch_bits, proto_bits = bits_of("batch"), bits_of("proto")
    me_batch, me_proto = lax.axis_index("batch"), lax.axis_index("proto")

    t, col, den, unit_b, proto_b = scores(slow_embed, fast_embed, prototypes)
    unit_bt = turned(unit_b)
    for iteration in range(ITERS):
        rows, r = row_pass(t, den, batch_parts(col, iteration % 2), protos_all, iteration == 0)
        row_parts = proto_parts(rows)
        if iteration == 0:
            den_parts = row_parts
        if iteration + 1 < ITERS:
            col = col_pass(t, row_parts, clips_all)

    near = tuple(range(batch_bits - 1))
    batch_orders = (near, tuple(reversed(near)))
    proto_orders = (tuple(range(proto_bits)), tuple(reversed(range(proto_bits))))
    send, g = send_gradients(t, r, unit_bt, row_parts, den_parts, batch_orders)
    shares = embed_gradients(g, proto_b, proto_orders)
    keep = keep_gradients(g, unit_bt, shares[0], batch_orders)

    proto_rows = proto_dev // batch_count
    clip_rows = clip_dev // proto_count
    raws = [lax.dynamic_slice_in_dim(prototypes, me_batch * proto_rows, proto_rows, 0)]
    for x in (slow_embed, fast_embed):
        raws.append(lax.dynamic_slice_in_dim(x, me_proto * clip_rows, clip_rows, 0))
    recv = swap(send, "batch", 1)
    halves = split_add([keep, recv], [(0, 1, h) for h in range(2)])
    z_groups, proto_groups = [], []
    for h in reversed(range(2)):
        order = tuple(bit + 1 for bit in batch_orders[h])
        z_groups.append(("batch", order) + tuple(halves[h]))
    for v in range(2):
        proto_groups.append(("proto", proto_orders[v], shares[2 * v], shares[2 * v + 1]))
    far_terms = scatter_sums(z_groups)
    terms = far_terms[2:] + far_terms[:2] + scatter_sums(proto_groups)
    grad_proto, grad_embed = project_shares(raws, terms)
    proto_pieces = gather_batch(grad_proto)
    view_pieces = gather_views(grad_embed, (proto_orders[1], proto_orders[0]))
    squares = proto_parts(sum_squares(proto_pieces, proto_rows))
    sizes = (proto_rows, clip_rows, clip_rows)
    groups = [proto_pieces] + view_pieces
    return finish((proto_entries, embed_entries), squares, groups, sizes)


def solution(mesh):
    placed = (P("batch", None), P("batch", None), P("proto", None))
    return jax.shard_map(
        body,
        mesh=mesh,
        in_specs=placed,
        out_specs=(P("proto", None), P("batch", None), P("batch", None)),
        check_vma=False,
    )
```

```python
import functools

import jax
import jax.numpy as jnp
from jax import lax
from jax.experimental import pallas as pl
from jax.experimental.pallas import tpu as pltpu
from jax.sharding import PartitionSpec as P

ITERS = 3


CODE_EPS = 0.05
TEMPER = 0.1
NORM_EPS = 1e-06
LANES = 128
MIB = 1024 * 1024


def vmem_spec():
    return pl.BlockSpec(memory_space=pltpu.VMEM)


def params(limit):
    return pltpu.CompilerParams(vmem_limit_bytes=limit * MIB)


def to_columns(line):
    return jnp.broadcast_to(line, (LANES, LANES)).T


def to_line(partial):
    return jnp.sum(partial.T, axis=0, keepdims=True)


def lane_sum(block):
    total = block[:, :LANES]
    for j in range(1, block.shape[1] // LANES):
        total = total + block[:, j * LANES : (j + 1) * LANES]
    return total


def row_fold(block):
    return jnp.sum(block.reshape(block.shape[0] // 8, 8, block.shape[1]), axis=0)


def sum_of(refs, first=0, size=None):
    size = refs[0].shape[0] if size is None else size
    total = refs[0][first : first + size, :]
    for ref in refs[1:]:
        total = total + ref[first : first + size, :]
    return total


LOG2E = 1.4426950408889634


def score_kernel(slow, fast, protos, t_ref, col_ref, den_ref, ub_ref, cb_ref, raw_s, w_s, ct_s, den_s, sems):
    clips, feats = slow.shape
    count = protos.shape[0]
    loads = []
    for v, src in enumerate((slow, fast)):
        loads.append(pltpu.make_async_copy(src, raw_s.at[v], sems.at[v]))
    loads.append(pltpu.make_async_copy(protos, w_s, sems.at[2]))
    for load in loads:
        load.start()
    for v in range(2):
        loads[v].wait()
        for first in range(0, clips, 256):
            rows = pl.ds(first, 256)
            x = raw_s[v, rows, :].astype(jnp.float32)
            length = jnp.sqrt(jnp.sum(x * x, axis=-1, keepdims=True) + 1e-12)
            ub_ref[v, rows, :] = (x / length).astype(jnp.bfloat16)
    den_s[...] = jnp.zeros_like(den_s)
    loads[2].wait()
    for first in range(0, count, 256):
        w = w_s[first : first + 256, :]
        length = jnp.sqrt(jnp.sum(w * w, axis=-1, keepdims=True) + 1e-12)
        c = w / length
        cb_ref[first : first + 256, :] = c.astype(jnp.bfloat16)
        ct_s[:, first : first + 256] = c.T.astype(jnp.bfloat16)

    def chunk(j, _):
        first = pl.multiple_of(j * 256, 256)
        weights = ct_s[:, pl.ds(first, 256)]
        for v in range(2):
            cols = jnp.zeros((8, 256), jnp.float32)
            for r in range(0, clips, 512):
                s = jnp.dot(
                    ub_ref[v, r : r + 512, :], weights, preferred_element_type=jnp.float32
                )
                for q in range(0, 512, 64):
                    rows = pl.ds(r + q, 64)
                    t = jnp.exp2(s[q : q + 64] * (LOG2E / TEMPER))
                    t_ref[v, rows, pl.ds(first, 256)] = t
                    cols = cols + row_fold(t * t)
                    den_s[v, rows, :] += lane_sum(t)
            line = jnp.sum(cols, axis=0, keepdims=True)
            for h in range(2):
                col_ref[pl.ds(v * (count // LANES) + j * 2 + h, 1), :] = line[
                    :, h * LANES : (h + 1) * LANES
                ]
        return 0

    lax.fori_loop(0, count // 256, chunk, 0)
    groups = clips // LANES
    for v in range(2):
        for i in range(groups):
            den_ref[pl.ds(v * groups + i, 1), :] = to_line(den_s[v, i * LANES : (i + 1) * LANES, :])


def scores(slow, fast, protos):
    clips, feats = slow.shape
    count = protos.shape[0]
    return pl.pallas_call(
        score_kernel,
        out_shape=(
            pltpu.VMEM((2, clips, count), jnp.float32),
            jax.ShapeDtypeStruct((2 * count // LANES, LANES), jnp.float32),
            jax.ShapeDtypeStruct((2 * clips // LANES, LANES), jnp.float32),
            jax.ShapeDtypeStruct((2, clips, feats), jnp.bfloat16),
            jax.ShapeDtypeStruct((count, feats), jnp.bfloat16),
        ),
        in_specs=[pl.BlockSpec(memory_space=pltpu.HBM)] * 3,
        out_specs=(vmem_spec(),) * 5,
        scratch_shapes=[
            pltpu.VMEM((2, clips, feats), jnp.bfloat16),
            pltpu.VMEM((count, feats), jnp.float32),
            pltpu.VMEM((feats, count), jnp.bfloat16),
            pltpu.VMEM((2, clips, LANES), jnp.float32),
            pltpu.SemaphoreType.DMA((3,)),
        ],
        compiler_params=params(24),
        name="scores",
    )(*[pltpu.with_memory_space_constraint(x, pltpu.HBM) for x in (slow, fast, protos)])


def turn_kernel(ub_ref, ubt_ref):
    clips = ub_ref.shape[1]
    for v in range(2):
        for first in range(0, clips, 256):
            u = ub_ref[v, first : first + 256, :].astype(jnp.float32)
            ubt_ref[:, v * clips + first : v * clips + first + 256] = u.T.astype(jnp.bfloat16)


def turned(ub):
    clips, feats = ub.shape[1:]
    return pl.pallas_call(
        turn_kernel,
        out_shape=jax.ShapeDtypeStruct((feats, 2 * clips), ub.dtype),
        in_specs=[vmem_spec()],
        out_specs=vmem_spec(),
        compiler_params=params(8),
        cost_estimate=pl.CostEstimate(
            flops=2 * clips * feats, bytes_accessed=4 * MIB, transcendentals=0
        ),
        name="turned",
    )(ub)


def row_kernel(protos_all, extra, t_ref, den_ref, *refs):
    col_parts, (row_ref, r_ref, acc_s) = refs[:-3], refs[-3:]
    clips, count = t_ref.shape[1:]
    groups, lines = clips // LANES, count // LANES
    r_ref[...] = 1.0 / (float(protos_all) * sum_of(col_parts))
    if extra:
        row_ref[2 * groups :, :] = den_ref[...]
    for v in range(2):

        def step(i, _, v=v):
            rows = pl.ds(pl.multiple_of(i * LANES, LANES), LANES)
            acc = jnp.zeros((LANES, LANES), jnp.float32)
            for j in range(lines):
                t = t_ref[v, rows, j * LANES : (j + 1) * LANES]
                acc = acc + t * t * r_ref[v * lines + j : v * lines + j + 1, :]
            acc_s[pl.ds(pl.multiple_of((v * groups + i) * LANES, LANES), LANES), :] = acc
            return 0

        lax.fori_loop(0, groups, step, 0)
    for line in range(2 * groups):
        row_ref[line : line + 1, :] = to_line(acc_s[line * LANES : (line + 1) * LANES, :])


def row_pass(t, den, col_parts, protos_all, extra):
    clips, count = t.shape[1:]
    lines = 2 * clips // LANES * (2 if extra else 1)
    return pl.pallas_call(
        functools.partial(row_kernel, protos_all, extra),
        out_shape=(
            jax.ShapeDtypeStruct((lines, LANES), jnp.float32),
            jax.ShapeDtypeStruct((2 * count // LANES, LANES), jnp.float32),
        ),
        in_specs=[vmem_spec()] * (2 + len(col_parts)),
        out_specs=(vmem_spec(),) * 2,
        scratch_shapes=[pltpu.VMEM((2 * clips, LANES), jnp.float32)],
        compiler_params=params(8),
        name="row_pass",
    )(pltpu.with_memory_space_constraint(t, pltpu.VMEM), den, *col_parts)


def col_kernel(clips_all, t_ref, *refs):
    row_parts, (col_ref, acc_s, s_s) = refs[:-3], refs[-3:]
    clips, count = t_ref.shape[1:]
    groups, lines = clips // LANES, count // LANES
    scale = 1.0 / (float(clips_all) * sum_of(row_parts, 0, 2 * groups))
    for line in range(2 * groups):
        s_s[line * LANES : (line + 1) * LANES, :] = to_columns(scale[line : line + 1, :])
    acc_s[...] = jnp.zeros_like(acc_s)
    for v in range(2):

        def step(i, _, v=v):
            rows = pl.ds(pl.multiple_of(i * LANES, LANES), LANES)
            scale = s_s[pl.ds(pl.multiple_of((v * groups + i) * LANES, LANES), LANES), :]
            for j in range(lines):
                span = slice(j * LANES, (j + 1) * LANES)
                t = t_ref[v, rows, span]
                acc_s[v, :, span] += row_fold(t * t * scale)
            return 0

        lax.fori_loop(0, groups, step, 0)
        for j in range(lines):
            col_ref[v * lines + j : v * lines + j + 1, :] = jnp.sum(
                acc_s[v, :, j * LANES : (j + 1) * LANES], axis=0, keepdims=True
            )


def col_pass(t, row_parts, clips_all):
    clips, count = t.shape[1:]
    return pl.pallas_call(
        functools.partial(col_kernel, clips_all),
        out_shape=jax.ShapeDtypeStruct((2 * count // LANES, LANES), jnp.float32),
        in_specs=[vmem_spec()] * (1 + len(row_parts)),
        out_specs=vmem_spec(),
        scratch_shapes=[
            pltpu.VMEM((2, 8, count), jnp.float32),
            pltpu.VMEM((2 * clips, LANES), jnp.float32),
        ],
        compiler_params=params(8),
        name="col_pass",
    )(pltpu.with_memory_space_constraint(t, pltpu.VMEM), *row_parts)


def piece_of(position, order):
    steps = len(order)
    return sum(((position >> (steps - 1 - j)) & 1) << bit for j, bit in enumerate(order))


def place_of(piece, order):
    steps = len(order)
    return sum(((piece >> bit) & 1) << (steps - 1 - j) for j, bit in enumerate(order))


def chunk_span(m, width):
    which = jnp.bitwise_xor(lax.axis_index("batch"), m)
    return which, pl.multiple_of(which * width, width)


def proto_grads(ubt, chunk, orders, i, out_ref):
    dct = jnp.dot(ubt, chunk, preferred_element_type=jnp.float32)
    half = dct.shape[0] // 2
    for h in range(2):
        out_ref[h, place_of(i, orders[h])] = dct[h * half : (h + 1) * half]


def prob_kernel(*refs):
    den_parts, prob_ref = refs[:-1], refs[-1]
    lines = den_parts[0].shape[0] // 2
    prob = (1.0 / TEMPER) / sum_of(den_parts, lines, lines)
    for line in range(lines):
        prob_ref[line * LANES : (line + 1) * LANES, :] = to_columns(prob[line : line + 1, :])


def prob_columns(den_parts):
    lines = den_parts[0].shape[0] // 2
    return pl.pallas_call(
        prob_kernel,
        out_shape=jax.ShapeDtypeStruct((lines * LANES, LANES), jnp.float32),
        in_specs=[vmem_spec()] * len(den_parts),
        out_specs=vmem_spec(),
        compiler_params=params(8),
        cost_estimate=pl.CostEstimate(
            flops=lines * LANES * LANES, bytes_accessed=2 * MIB, transcendentals=0
        ),
        name="prob_columns",
    )(*den_parts)


def send_kernel(orders, parts, t_ref, r_ref, ubt_ref, prob_s, *refs):
    row_parts = refs[:parts]
    send_ref, g_ref, chunk_s, code_s = refs[parts:]
    clips, count = t_ref.shape[1:]
    groups, lines = clips // LANES, count // LANES
    pieces = 1 << len(orders[0])
    width = count // (2 * pieces)
    code = (1.0 / TEMPER) / sum_of(row_parts, 0, 2 * groups)
    for line in range(2 * groups):
        code_s[line * LANES : (line + 1) * LANES, :] = to_columns(code[line : line + 1, :])

    def score_grads(m, keep_chunk):
        which, first = chunk_span(m, width)
        for i in range(0, clips, 32):
            rows = slice(i, i + 32)
            codes = [code_s[v * clips + i : v * clips + i + 32, :] for v in range(2)]
            probs = [prob_s[v * clips + i : v * clips + i + 32, :] for v in range(2)]
            for h in range(width // LANES):
                span = pl.ds(first + h * LANES, LANES)
                line = which * (width // LANES) + h
                t = [t_ref[v, rows, span] for v in range(2)]
                q = [
                    t[v] * t[v] * r_ref[pl.ds(v * lines + line, 1), :] * codes[v]
                    for v in range(2)
                ]
                for v in range(2):
                    g = (t[v] * probs[v] - q[1 - v]).astype(jnp.bfloat16)
                    own = slice(v * clips + i, v * clips + i + 32)
                    g_ref[own, span] = g
                    if keep_chunk:
                        chunk_s[own, h * LANES : (h + 1) * LANES] = g

    def pair(i, _):
        score_grads(2 * i + 1, True)
        score_grads(2 * i, False)
        proto_grads(ubt_ref[...], chunk_s[...], orders, i, send_ref)
        return 0

    lax.fori_loop(0, pieces, pair, 0)


def send_gradients(t, r, ubt, prob, row_parts, orders):
    clips, count = t.shape[1:]
    feats = ubt.shape[0]
    pieces = 1 << len(orders[0])
    width = count // (2 * pieces)
    return pl.pallas_call(
        functools.partial(send_kernel, orders, len(row_parts)),
        out_shape=(
            jax.ShapeDtypeStruct((2, pieces, feats // 2, width), jnp.float32),
            pltpu.VMEM((2 * clips, count), jnp.bfloat16),
        ),
        in_specs=[vmem_spec()] * (4 + len(row_parts)),
        out_specs=(vmem_spec(),) * 2,
        scratch_shapes=[
            pltpu.VMEM((2 * clips, width), jnp.bfloat16),
            pltpu.VMEM((2 * clips, LANES), jnp.float32),
        ],
        compiler_params=params(14),
        cost_estimate=pl.CostEstimate(
            flops=2 * clips * count * feats, bytes_accessed=20 * MIB, transcendentals=0
        ),
        name="send_gradients",
    )(pltpu.with_memory_space_constraint(t, pltpu.VMEM), r, ubt, prob, *row_parts)


def embed_grad_kernel(orders, g_ref, cb_ref, *outs):
    clips = g_ref.shape[0] // 2
    peers = 1 << len(orders[0])
    size = clips // peers
    for v in range(2):
        for place in range(peers):
            which = jnp.bitwise_xor(lax.axis_index("proto"), piece_of(place, orders[v]))
            rows = pl.ds(pl.multiple_of(v * clips + which * size, size), size)
            out_ref = outs[2 * v + (0 if place >= peers // 2 else 1)]
            out_ref[place % (peers // 2)] = jnp.dot(
                g_ref[rows, :], cb_ref[...], preferred_element_type=jnp.float32
            )


def embed_gradients(g, cb, orders):
    clips, count = g.shape[0] // 2, g.shape[1]
    feats = cb.shape[1]
    peers = 1 << len(orders[0])
    share = jax.ShapeDtypeStruct((peers // 2, clips // peers, feats), jnp.float32)
    return pl.pallas_call(
        functools.partial(embed_grad_kernel, orders),
        out_shape=(share,) * 4,
        in_specs=[vmem_spec()] * 2,
        out_specs=(vmem_spec(),) * 4,
        compiler_params=params(14),
        cost_estimate=pl.CostEstimate(
            flops=4 * clips * count * feats, bytes_accessed=11 * MIB, transcendentals=0
        ),
        name="embed_gradients",
    )(pltpu.with_memory_space_constraint(g, pltpu.VMEM), cb)


def keep_kernel(orders, g_ref, ubt_ref, after_ref, keep_ref):
    pieces = 1 << len(orders[0])
    width = g_ref.shape[1] // (2 * pieces)

    def step(i, _):
        _, first = chunk_span(2 * i, width)
        proto_grads(ubt_ref[...], g_ref[:, pl.ds(first, width)], orders, i, keep_ref)
        return 0

    lax.fori_loop(0, pieces, step, 0)


def keep_gradients(g, ubt, after, orders):
    count = g.shape[1]
    feats, clips = ubt.shape
    pieces = 1 << len(orders[0])
    return pl.pallas_call(
        functools.partial(keep_kernel, orders),
        out_shape=jax.ShapeDtypeStruct((2, pieces, feats // 2, count // (2 * pieces)), jnp.float32),
        in_specs=[vmem_spec()] * 2 + [pl.BlockSpec(memory_space=pl.ANY)],
        out_specs=vmem_spec(),
        compiler_params=params(14),
        cost_estimate=pl.CostEstimate(
            flops=clips * count * feats, bytes_accessed=6 * MIB, transcendentals=0
        ),
        name="keep_gradients",
    )(pltpu.with_memory_space_constraint(g, pltpu.VMEM), ubt, after)


def split_add_kernel(plan, inputs, *refs):
    ins, outs = refs[:inputs], refs[inputs:]
    for n, (keep_place, recv_place, part) in enumerate(plan):
        keep, recv = ins[keep_place], ins[recv_place]
        if part is not None:
            keep, recv = keep.at[part], recv.at[part]
        send_out, keep_out = outs[2 * n : 2 * n + 2]
        half = keep_out.shape[0]
        keep_out[...] = keep[:half] + recv[:half]
        send_out[...] = keep[half:] + recv[half:]


def split_add(arrays, plan):
    halves = []
    for place, _, part in plan:
        shape = arrays[place].shape if part is None else arrays[place].shape[1:]
        halves += [jax.ShapeDtypeStruct((shape[0] // 2,) + shape[1:], jnp.float32)] * 2
    outs = pl.pallas_call(
        functools.partial(split_add_kernel, plan, len(arrays)),
        out_shape=tuple(halves),
        in_specs=[vmem_spec()] * len(arrays),
        out_specs=(vmem_spec(),) * len(halves),
        compiler_params=params(12),
        name="split_add",
    )(*arrays)
    return [(outs[2 * n], outs[2 * n + 1]) for n in range(len(plan))]


def project(raw, grad):
    x = raw.astype(jnp.float32)
    length = jnp.sqrt(jnp.sum(x * x, axis=-1, keepdims=True) + 1e-12)
    unit = x / length
    along = jnp.sum(unit * grad, axis=-1, keepdims=True)
    return (grad - unit * along) / length


EXTRA = 8


def share_kernel(proto_raw, slow_raw, fast_raw, *refs):
    terms, (proto_out, embed_out) = refs[:-2], refs[-2:]
    count = proto_raw.shape[0]
    squares = [jnp.zeros((8, LANES), jnp.float32)] * 2
    halves = [terms[2 * h][0] + terms[2 * h + 1][0] for h in range(2)]
    grad = project(proto_raw[...], jnp.concatenate(halves, axis=0).T)
    proto_out[:count, :] = grad
    squares[0] = row_fold(lane_sum(grad * grad))
    for v, raw in enumerate((slow_raw, fast_raw)):
        grad = project(raw[...], terms[4 + 2 * v][0] + terms[5 + 2 * v][0])
        embed_out[v] = grad
        squares[1] = squares[1] + row_fold(lane_sum(grad * grad))
    for kind in range(2):
        total = jnp.sum(jnp.sum(squares[kind], axis=0, keepdims=True), axis=1, keepdims=True)
        proto_out[count:, kind * LANES : (kind + 1) * LANES] = jnp.broadcast_to(total, (EXTRA, LANES))


def project_shares(raws, terms):
    rows, feats = raws[1].shape
    count = raws[0].shape[0]
    return pl.pallas_call(
        share_kernel,
        out_shape=(
            jax.ShapeDtypeStruct((count + EXTRA, feats), jnp.float32),
            jax.ShapeDtypeStruct((2, rows, feats), jnp.float32),
        ),
        in_specs=[vmem_spec()] * (len(raws) + len(terms)),
        out_specs=(vmem_spec(),) * 2,
        compiler_params=params(10),
        name="project_shares",
    )(*raws, *terms)


def tree_sum(terms):
    while len(terms) > 1:
        terms = [terms[i] + terms[i + 1] for i in range(0, len(terms), 2)]
    return terms[0]


def distinct(groups):
    arrays, plan = [], []
    for group in groups:
        places = []
        for array, part in group:
            place = next((i for i, known in enumerate(arrays) if known is array), None)
            if place is None:
                place = len(arrays)
                arrays.append(array)
            places.append((place, part))
        plan.append(places)
    return arrays, plan


def piece_ref(ins, place, part):
    return ins[place] if part is None else ins[place].at[part]


def squares_kernel(plan, rows, *refs):
    ins, out_ref = refs[:-1], refs[-1]
    total = tree_sum([piece_ref(ins, *piece)[rows:, :] for piece in plan])
    for kind in range(2):
        out_ref[kind] = total[:, kind * LANES : (kind + 1) * LANES]


def sum_squares(pieces, rows):
    arrays, plan = distinct([pieces])
    return pl.pallas_call(
        functools.partial(squares_kernel, plan[0], rows),
        out_shape=jax.ShapeDtypeStruct((2, 8, LANES), jnp.float32),
        in_specs=[vmem_spec()] * len(arrays),
        out_specs=vmem_spec(),
        compiler_params=params(8),
        cost_estimate=pl.CostEstimate(flops=8, bytes_accessed=8, transcendentals=0),
        name="sum_squares",
    )(*arrays)


def finish_kernel(entries, plan, count, *refs):
    squares, ins, outs = refs[:count], refs[count:-7], refs[-7:-4]
    scratch, sems = refs[-4:-1], refs[-1]
    total = tree_sum([square[...] for square in squares])
    factors = [lax.rsqrt(total[k, 0:1, 0:1] / entries[k] + NORM_EPS) for k in range(2)]
    copies = []
    for n, pieces in enumerate(plan):
        axis, kind = ("batch", 0) if n == 0 else ("proto", 1)
        size = scratch[n].shape[1]
        for m, piece in enumerate(pieces):
            which = jnp.bitwise_xor(lax.axis_index(axis), m)
            rows = pl.ds(pl.multiple_of(which * size, size), size)
            scratch[n][m] = piece_ref(ins, *piece)[:size, :] * factors[kind]
            sem = sems.at[len(copies)]
            copies.append(pltpu.make_async_copy(scratch[n].at[m], outs[n].at[rows], sem))
            copies[-1].start()
    for copy in copies:
        copy.wait()


def finish(entries, squares, groups, sizes):
    arrays, plan = distinct(groups)
    feats = arrays[0].shape[-1]
    scratch = [
        pltpu.VMEM((len(group), size, feats), jnp.float32) for group, size in zip(groups, sizes)
    ]
    outs = tuple(
        jax.ShapeDtypeStruct((len(group) * size, feats), jnp.float32)
        for group, size in zip(groups, sizes)
    )
    count = sum(len(group) for group in groups)
    return pl.pallas_call(
        functools.partial(finish_kernel, entries, plan, len(squares)),
        out_shape=outs,
        in_specs=[vmem_spec()] * (len(squares) + len(arrays)),
        out_specs=(pl.BlockSpec(memory_space=pltpu.HBM),) * len(outs),
        scratch_shapes=scratch + [pltpu.SemaphoreType.DMA((count,))],
        compiler_params=params(12),
        name="finish",
    )(*squares, *arrays)


def swap(own, axis, mask):
    return lax.ppermute(own, axis, [(i, i ^ mask) for i in range(lax.axis_size(axis))])


def bits_of(axis):
    count = lax.axis_size(axis)
    bits = count.bit_length() - 1
    if count != 1 << bits:
        raise ValueError("axis size")
    return bits


def far_first(own, axis, step, count):
    return [swap(own, axis, m * step) for m in reversed(range(1, count))]


def proto_parts(own):
    return far_first(own, "proto", 1, lax.axis_size("proto")) + [own]


def batch_parts(own, turn):
    pair = own + swap(own, "batch", 1)
    parts = far_first(pair, "batch", 2, lax.axis_size("batch") // 2)
    return parts[turn:] + parts[:turn] + [pair]


def scatter_sums(groups):
    stage, terms = 0, [None] * len(groups)
    state = list(groups)
    while any(term is None for term in terms):
        live = [n for n in range(len(state)) if terms[n] is None]
        recvs = {}
        for n in live:
            axis, order, send, keep = state[n]
            recvs[n] = swap(send, axis, 1 << order[stage])
        going = []
        for n in live:
            axis, order, send, keep = state[n]
            if stage + 1 == len(order):
                terms[n] = (keep, recvs[n])
            else:
                going.append(n)
        if going:
            arrays = [x for n in going for x in (state[n][3], recvs[n])]
            split = split_add(arrays, [(2 * i, 2 * i + 1, None) for i in range(len(going))])
            for n, (send, keep) in zip(going, split):
                state[n] = (state[n][0], state[n][1], send, keep)
        stage += 1
    return [x for term in terms for x in term]


def gather_batch(own):
    bits = list(reversed(range(lax.axis_size("batch").bit_length() - 1)))
    pieces = {0: own}
    first = {bit: swap(own, "batch", 1 << bit) for bit in bits}
    for bit in bits:
        for m in list(pieces):
            pieces[m | 1 << bit] = first[bit] if m == 0 else swap(pieces[m], "batch", 1 << bit)
    return [(pieces[m], None) for m in range(len(pieces))]


def gather_views(own, orders):
    first = {bit: swap(own, "proto", 1 << bit) for bit in sorted(orders[0])}
    groups = []
    for v, order in enumerate(orders):
        pieces = {0: (own, v)}
        for bit in order:
            for m in list(pieces):
                if m == 0:
                    pieces[1 << bit] = (first[bit], v)
                else:
                    array, view = pieces[m]
                    piece = array if view is None else array[view]
                    pieces[m | 1 << bit] = (swap(piece, "proto", 1 << bit), None)
        groups.append([pieces[m] for m in range(len(pieces))])
    return groups


def body(slow_embed, fast_embed, prototypes):
    clip_dev, feat_width = slow_embed.shape
    proto_dev = prototypes.shape[0]
    batch_count = lax.axis_size("batch")
    proto_count = lax.axis_size("proto")
    clips_all = clip_dev * batch_count
    protos_all = proto_dev * proto_count
    proto_entries = float(protos_all * feat_width)
    embed_entries = float(2 * clips_all * feat_width)
    batch_bits, proto_bits = bits_of("batch"), bits_of("proto")
    me_batch, me_proto = lax.axis_index("batch"), lax.axis_index("proto")

    t, col, den, unit_b, proto_b = scores(slow_embed, fast_embed, prototypes)
    unit_bt = turned(unit_b)
    for iteration in range(ITERS):
        rows, r = row_pass(t, den, batch_parts(col, iteration % 2), protos_all, iteration == 0)
        row_parts = proto_parts(rows)
        if iteration == 0:
            prob = prob_columns(row_parts)
        if iteration + 1 < ITERS:
            col = col_pass(t, row_parts, clips_all)

    near = tuple(range(batch_bits - 1))
    batch_orders = (near, tuple(reversed(near)))
    proto_orders = (tuple(range(proto_bits)), tuple(reversed(range(proto_bits))))
    send, g = send_gradients(t, r, unit_bt, prob, row_parts, batch_orders)
    shares = embed_gradients(g, proto_b, proto_orders)
    keep = keep_gradients(g, unit_bt, shares[0], batch_orders)

    proto_rows = proto_dev // batch_count
    clip_rows = clip_dev // proto_count
    raws = [lax.dynamic_slice_in_dim(prototypes, me_batch * proto_rows, proto_rows, 0)]
    for x in (slow_embed, fast_embed):
        raws.append(lax.dynamic_slice_in_dim(x, me_proto * clip_rows, clip_rows, 0))
    recv = swap(send, "batch", 1)
    halves = split_add([keep, recv], [(0, 1, h) for h in range(2)])
    z_groups, proto_groups = [], []
    for h in reversed(range(2)):
        order = tuple(bit + 1 for bit in batch_orders[h])
        z_groups.append(("batch", order) + tuple(halves[h]))
    for v in range(2):
        proto_groups.append(("proto", proto_orders[v], shares[2 * v], shares[2 * v + 1]))
    far_terms = scatter_sums(z_groups)
    terms = far_terms[2:] + far_terms[:2] + scatter_sums(proto_groups)
    grad_proto, grad_embed = project_shares(raws, terms)
    proto_pieces = gather_batch(grad_proto)
    view_pieces = gather_views(grad_embed, (proto_orders[1], proto_orders[0]))
    squares = proto_parts(sum_squares(proto_pieces, proto_rows))
    sizes = (proto_rows, clip_rows, clip_rows)
    groups = [proto_pieces] + view_pieces
    return finish((proto_entries, embed_entries), squares, groups, sizes)


def solution(mesh):
    placed = (P("batch", None), P("batch", None), P("proto", None))
    return jax.shard_map(
        body,
        mesh=mesh,
        in_specs=placed,
        out_specs=(P("proto", None), P("batch", None), P("batch", None)),
        check_vma=False,
    )
```

```python
import functools

import jax
import jax.numpy as jnp
from jax import lax
from jax.experimental import pallas as pl
from jax.experimental.pallas import tpu as pltpu
from jax.sharding import PartitionSpec as P

ITERS = 3


CODE_EPS = 0.05
TEMPER = 0.1
NORM_EPS = 1e-06
LANES = 128
MIB = 1024 * 1024


def vmem_spec():
    return pl.BlockSpec(memory_space=pltpu.VMEM)


def params(limit):
    return pltpu.CompilerParams(vmem_limit_bytes=limit * MIB)


def to_columns(line):
    return jnp.broadcast_to(line, (LANES, LANES)).T


def to_line(partial):
    return jnp.sum(partial.T, axis=0, keepdims=True)


def lane_sum(block):
    total = block[:, :LANES]
    for j in range(1, block.shape[1] // LANES):
        total = total + block[:, j * LANES : (j + 1) * LANES]
    return total


def row_fold(block):
    return jnp.sum(block.reshape(block.shape[0] // 8, 8, block.shape[1]), axis=0)


def sum_of(refs, first=0, size=None):
    size = refs[0].shape[0] if size is None else size
    total = refs[0][first : first + size, :]
    for ref in refs[1:]:
        total = total + ref[first : first + size, :]
    return total


LOG2E = 1.4426950408889634


def score_kernel(slow, fast, protos, t_ref, col_ref, ub_ref, cb_ref, raw_s, w_s, ct_s, sems):
    clips, feats = slow.shape
    count = protos.shape[0]
    loads = []
    for v, src in enumerate((slow, fast)):
        loads.append(pltpu.make_async_copy(src, raw_s.at[v], sems.at[v]))
    loads.append(pltpu.make_async_copy(protos, w_s, sems.at[2]))
    for load in loads:
        load.start()
    for v in range(2):
        loads[v].wait()
        for first in range(0, clips, 256):
            rows = pl.ds(first, 256)
            x = raw_s[v, rows, :].astype(jnp.float32)
            length = jnp.sqrt(jnp.sum(x * x, axis=-1, keepdims=True) + 1e-12)
            ub_ref[v, rows, :] = (x / length).astype(jnp.bfloat16)
    loads[2].wait()
    for first in range(0, count, 256):
        w = w_s[first : first + 256, :]
        length = jnp.sqrt(jnp.sum(w * w, axis=-1, keepdims=True) + 1e-12)
        c = w / length
        cb_ref[first : first + 256, :] = c.astype(jnp.bfloat16)
        ct_s[:, first : first + 256] = c.T.astype(jnp.bfloat16)

    def chunk(j, _):
        first = pl.multiple_of(j * 256, 256)
        weights = ct_s[:, pl.ds(first, 256)]
        for v in range(2):
            cols = jnp.zeros((8, 256), jnp.float32)
            for r in range(0, clips, 512):
                s = jnp.dot(
                    ub_ref[v, r : r + 512, :], weights, preferred_element_type=jnp.float32
                )
                for q in range(0, 512, 64):
                    rows = pl.ds(r + q, 64)
                    t = jnp.exp2(s[q : q + 64] * (LOG2E / TEMPER))
                    t_ref[v, rows, pl.ds(first, 256)] = t
                    cols = cols + row_fold(t * t)
            line = jnp.sum(cols, axis=0, keepdims=True)
            for h in range(2):
                col_ref[pl.ds(v * (count // LANES) + j * 2 + h, 1), :] = line[
                    :, h * LANES : (h + 1) * LANES
                ]
        return 0

    lax.fori_loop(0, count // 256, chunk, 0)


def scores(slow, fast, protos):
    clips, feats = slow.shape
    count = protos.shape[0]
    return pl.pallas_call(
        score_kernel,
        out_shape=(
            pltpu.VMEM((2, clips, count), jnp.float32),
            jax.ShapeDtypeStruct((2 * count // LANES, LANES), jnp.float32),
            jax.ShapeDtypeStruct((2, clips, feats), jnp.bfloat16),
            jax.ShapeDtypeStruct((count, feats), jnp.bfloat16),
        ),
        in_specs=[pl.BlockSpec(memory_space=pltpu.HBM)] * 3,
        out_specs=(vmem_spec(),) * 4,
        scratch_shapes=[
            pltpu.VMEM((2, clips, feats), jnp.bfloat16),
            pltpu.VMEM((count, feats), jnp.float32),
            pltpu.VMEM((feats, count), jnp.bfloat16),
            pltpu.SemaphoreType.DMA((3,)),
        ],
        compiler_params=params(24),
        name="scores",
    )(*[pltpu.with_memory_space_constraint(x, pltpu.HBM) for x in (slow, fast, protos)])


def turn_kernel(ub_ref, ubt_ref):
    clips = ub_ref.shape[1]
    for v in range(2):
        for first in range(0, clips, 256):
            u = ub_ref[v, first : first + 256, :].astype(jnp.float32)
            ubt_ref[:, v * clips + first : v * clips + first + 256] = u.T.astype(jnp.bfloat16)


def turned(ub):
    clips, feats = ub.shape[1:]
    return pl.pallas_call(
        turn_kernel,
        out_shape=jax.ShapeDtypeStruct((feats, 2 * clips), ub.dtype),
        in_specs=[vmem_spec()],
        out_specs=vmem_spec(),
        compiler_params=params(8),
        cost_estimate=pl.CostEstimate(
            flops=2 * clips * feats, bytes_accessed=4 * MIB, transcendentals=0
        ),
        name="turned",
    )(ub)


def row_kernel(protos_all, extra, t_ref, *refs):
    col_parts, (row_ref, r_ref, acc_s) = refs[:-3], refs[-3:]
    clips, count = t_ref.shape[1:]
    groups, lines = clips // LANES, count // LANES
    r_ref[...] = 1.0 / (float(protos_all) * sum_of(col_parts))
    for v in range(2):

        def step(i, _, v=v):
            rows = pl.ds(pl.multiple_of(i * LANES, LANES), LANES)
            acc = jnp.zeros((LANES, LANES), jnp.float32)
            den = jnp.zeros((LANES, LANES), jnp.float32)
            for j in range(lines):
                t = t_ref[v, rows, j * LANES : (j + 1) * LANES]
                acc = acc + t * t * r_ref[v * lines + j : v * lines + j + 1, :]
                if extra:
                    den = den + t
            first = pl.multiple_of((v * groups + i) * LANES, LANES)
            acc_s[pl.ds(first, LANES), :] = acc
            if extra:
                acc_s[pl.ds(2 * clips + first, LANES), :] = den
            return 0

        lax.fori_loop(0, groups, step, 0)
    for line in range(row_ref.shape[0]):
        row_ref[line : line + 1, :] = to_line(acc_s[line * LANES : (line + 1) * LANES, :])


def row_pass(t, col_parts, protos_all, extra):
    clips, count = t.shape[1:]
    lines = 2 * clips // LANES * (2 if extra else 1)
    return pl.pallas_call(
        functools.partial(row_kernel, protos_all, extra),
        out_shape=(
            jax.ShapeDtypeStruct((lines, LANES), jnp.float32),
            jax.ShapeDtypeStruct((2 * count // LANES, LANES), jnp.float32),
        ),
        in_specs=[vmem_spec()] * (1 + len(col_parts)),
        out_specs=(vmem_spec(),) * 2,
        scratch_shapes=[pltpu.VMEM((lines * LANES, LANES), jnp.float32)],
        compiler_params=params(8),
        name="row_pass",
    )(pltpu.with_memory_space_constraint(t, pltpu.VMEM), *col_parts)


def col_kernel(clips_all, t_ref, *refs):
    row_parts, (col_ref, acc_s, s_s) = refs[:-3], refs[-3:]
    clips, count = t_ref.shape[1:]
    groups, lines = clips // LANES, count // LANES
    scale = 1.0 / (float(clips_all) * sum_of(row_parts, 0, 2 * groups))
    for line in range(2 * groups):
        s_s[line * LANES : (line + 1) * LANES, :] = to_columns(scale[line : line + 1, :])
    acc_s[...] = jnp.zeros_like(acc_s)
    for v in range(2):

        def step(i, _, v=v):
            rows = pl.ds(pl.multiple_of(i * LANES, LANES), LANES)
            scale = s_s[pl.ds(pl.multiple_of((v * groups + i) * LANES, LANES), LANES), :]
            for j in range(lines):
                span = slice(j * LANES, (j + 1) * LANES)
                t = t_ref[v, rows, span]
                acc_s[v, :, span] += row_fold(t * t * scale)
            return 0

        lax.fori_loop(0, groups, step, 0)
        for j in range(lines):
            col_ref[v * lines + j : v * lines + j + 1, :] = jnp.sum(
                acc_s[v, :, j * LANES : (j + 1) * LANES], axis=0, keepdims=True
            )


def col_pass(t, row_parts, clips_all):
    clips, count = t.shape[1:]
    return pl.pallas_call(
        functools.partial(col_kernel, clips_all),
        out_shape=jax.ShapeDtypeStruct((2 * count // LANES, LANES), jnp.float32),
        in_specs=[vmem_spec()] * (1 + len(row_parts)),
        out_specs=vmem_spec(),
        scratch_shapes=[
            pltpu.VMEM((2, 8, count), jnp.float32),
            pltpu.VMEM((2 * clips, LANES), jnp.float32),
        ],
        compiler_params=params(8),
        name="col_pass",
    )(pltpu.with_memory_space_constraint(t, pltpu.VMEM), *row_parts)


def piece_of(position, order):
    steps = len(order)
    return sum(((position >> (steps - 1 - j)) & 1) << bit for j, bit in enumerate(order))


def place_of(piece, order):
    steps = len(order)
    return sum(((piece >> bit) & 1) << (steps - 1 - j) for j, bit in enumerate(order))


def chunk_span(m, width):
    which = jnp.bitwise_xor(lax.axis_index("batch"), m)
    return which, pl.multiple_of(which * width, width)


def proto_grads(ubt, chunk, orders, i, out_ref):
    dct = jnp.dot(ubt, chunk, preferred_element_type=jnp.float32)
    half = dct.shape[0] // 2
    for h in range(2):
        out_ref[h, place_of(i, orders[h])] = dct[h * half : (h + 1) * half]


def prob_kernel(*refs):
    den_parts, prob_ref = refs[:-1], refs[-1]
    lines = den_parts[0].shape[0] // 2
    prob = (1.0 / TEMPER) / sum_of(den_parts, lines, lines)
    for line in range(lines):
        prob_ref[line * LANES : (line + 1) * LANES, :] = to_columns(prob[line : line + 1, :])


def prob_columns(den_parts):
    lines = den_parts[0].shape[0] // 2
    return pl.pallas_call(
        prob_kernel,
        out_shape=jax.ShapeDtypeStruct((lines * LANES, LANES), jnp.float32),
        in_specs=[vmem_spec()] * len(den_parts),
        out_specs=vmem_spec(),
        compiler_params=params(8),
        cost_estimate=pl.CostEstimate(
            flops=lines * LANES * LANES, bytes_accessed=2 * MIB, transcendentals=0
        ),
        name="prob_columns",
    )(*den_parts)


def send_kernel(orders, parts, t_ref, r_ref, ubt_ref, prob_s, *refs):
    row_parts = refs[:parts]
    send_ref, g_ref, first_s, second_s, code_s = refs[parts:]
    clips, count = t_ref.shape[1:]
    groups, lines = clips // LANES, count // LANES
    pieces = 1 << len(orders[0])
    width = count // (2 * pieces)
    code = (1.0 / TEMPER) / sum_of(row_parts, 0, 2 * groups)
    for line in range(2 * groups):
        code_s[line * LANES : (line + 1) * LANES, :] = to_columns(code[line : line + 1, :])

    def score_grads(i, chunk_s):
        places = [chunk_span(2 * i + core, width) for core in range(2)]
        for row in range(0, clips, 32):
            codes = [code_s[v * clips + row : v * clips + row + 32, :] for v in range(2)]
            probs = [prob_s[v * clips + row : v * clips + row + 32, :] for v in range(2)]
            for core, (which, first) in enumerate(places):
                for h in range(width // LANES):
                    span = pl.ds(first + h * LANES, LANES)
                    line = which * (width // LANES) + h
                    t = [t_ref[v, row : row + 32, span] for v in range(2)]
                    q = [
                        t[v] * t[v] * r_ref[pl.ds(v * lines + line, 1), :] * codes[v]
                        for v in range(2)
                    ]
                    for v in range(2):
                        g = (t[v] * probs[v] - q[1 - v]).astype(jnp.bfloat16)
                        own = slice(v * clips + row, v * clips + row + 32)
                        g_ref[own, span] = g
                        if core == 1:
                            chunk_s[own, h * LANES : (h + 1) * LANES] = g

    def two_pairs(k, _):
        score_grads(2 * k, first_s)
        score_grads(2 * k + 1, second_s)
        proto_grads(ubt_ref[...], first_s[...], orders, 2 * k, send_ref)
        proto_grads(ubt_ref[...], second_s[...], orders, 2 * k + 1, send_ref)
        return 0

    lax.fori_loop(0, pieces // 2, two_pairs, 0)


def send_gradients(t, r, ubt, prob, row_parts, orders):
    clips, count = t.shape[1:]
    feats = ubt.shape[0]
    pieces = 1 << len(orders[0])
    width = count // (2 * pieces)
    return pl.pallas_call(
        functools.partial(send_kernel, orders, len(row_parts)),
        out_shape=(
            jax.ShapeDtypeStruct((2, pieces, feats // 2, width), jnp.float32),
            pltpu.VMEM((2 * clips, count), jnp.bfloat16),
        ),
        in_specs=[vmem_spec()] * (4 + len(row_parts)),
        out_specs=(vmem_spec(),) * 2,
        scratch_shapes=[
            pltpu.VMEM((2 * clips, width), jnp.bfloat16),
            pltpu.VMEM((2 * clips, width), jnp.bfloat16),
            pltpu.VMEM((2 * clips, LANES), jnp.float32),
        ],
        compiler_params=params(14),
        cost_estimate=pl.CostEstimate(
            flops=2 * clips * count * feats, bytes_accessed=20 * MIB, transcendentals=0
        ),
        name="send_gradients",
    )(pltpu.with_memory_space_constraint(t, pltpu.VMEM), r, ubt, prob, *row_parts)


def embed_grad_kernel(orders, g_ref, cb_ref, *outs):
    clips = g_ref.shape[0] // 2
    peers = 1 << len(orders[0])
    size = clips // peers
    for v in range(2):
        for place in range(peers):
            which = jnp.bitwise_xor(lax.axis_index("proto"), piece_of(place, orders[v]))
            rows = pl.ds(pl.multiple_of(v * clips + which * size, size), size)
            out_ref = outs[2 * v + (0 if place >= peers // 2 else 1)]
            out_ref[place % (peers // 2)] = jnp.dot(
                g_ref[rows, :], cb_ref[...], preferred_element_type=jnp.float32
            )


def embed_gradients(g, cb, orders):
    clips, count = g.shape[0] // 2, g.shape[1]
    feats = cb.shape[1]
    peers = 1 << len(orders[0])
    share = jax.ShapeDtypeStruct((peers // 2, clips // peers, feats), jnp.float32)
    return pl.pallas_call(
        functools.partial(embed_grad_kernel, orders),
        out_shape=(share,) * 4,
        in_specs=[vmem_spec()] * 2,
        out_specs=(vmem_spec(),) * 4,
        compiler_params=params(14),
        cost_estimate=pl.CostEstimate(
            flops=4 * clips * count * feats, bytes_accessed=11 * MIB, transcendentals=0
        ),
        name="embed_gradients",
    )(pltpu.with_memory_space_constraint(g, pltpu.VMEM), cb)


def keep_kernel(orders, g_ref, ubt_ref, after_ref, keep_ref):
    pieces = 1 << len(orders[0])
    width = g_ref.shape[1] // (2 * pieces)

    def step(i, _):
        _, first = chunk_span(2 * i, width)
        proto_grads(ubt_ref[...], g_ref[:, pl.ds(first, width)], orders, i, keep_ref)
        return 0

    lax.fori_loop(0, pieces, step, 0)


def keep_gradients(g, ubt, after, orders):
    count = g.shape[1]
    feats, clips = ubt.shape
    pieces = 1 << len(orders[0])
    return pl.pallas_call(
        functools.partial(keep_kernel, orders),
        out_shape=jax.ShapeDtypeStruct((2, pieces, feats // 2, count // (2 * pieces)), jnp.float32),
        in_specs=[vmem_spec()] * 2 + [pl.BlockSpec(memory_space=pl.ANY)],
        out_specs=vmem_spec(),
        compiler_params=params(14),
        cost_estimate=pl.CostEstimate(
            flops=clips * count * feats, bytes_accessed=6 * MIB, transcendentals=0
        ),
        name="keep_gradients",
    )(pltpu.with_memory_space_constraint(g, pltpu.VMEM), ubt, after)


def split_add_kernel(plan, inputs, *refs):
    ins, outs = refs[:inputs], refs[inputs:]
    for n, (keep_place, recv_place, part) in enumerate(plan):
        keep, recv = ins[keep_place], ins[recv_place]
        if part is not None:
            keep, recv = keep.at[part], recv.at[part]
        send_out, keep_out = outs[2 * n : 2 * n + 2]
        half = keep_out.shape[0]
        keep_out[...] = keep[:half] + recv[:half]
        send_out[...] = keep[half:] + recv[half:]


def split_add(arrays, plan):
    halves = []
    for place, _, part in plan:
        shape = arrays[place].shape if part is None else arrays[place].shape[1:]
        halves += [jax.ShapeDtypeStruct((shape[0] // 2,) + shape[1:], jnp.float32)] * 2
    outs = pl.pallas_call(
        functools.partial(split_add_kernel, plan, len(arrays)),
        out_shape=tuple(halves),
        in_specs=[vmem_spec()] * len(arrays),
        out_specs=(vmem_spec(),) * len(halves),
        compiler_params=params(12),
        name="split_add",
    )(*arrays)
    return [(outs[2 * n], outs[2 * n + 1]) for n in range(len(plan))]


def project(raw, grad):
    x = raw.astype(jnp.float32)
    length = jnp.sqrt(jnp.sum(x * x, axis=-1, keepdims=True) + 1e-12)
    unit = x / length
    along = jnp.sum(unit * grad, axis=-1, keepdims=True)
    return (grad - unit * along) / length


EXTRA = 8


def share_kernel(proto_raw, slow_raw, fast_raw, *refs):
    terms, (proto_out, embed_out) = refs[:-2], refs[-2:]
    count = proto_raw.shape[0]
    squares = [jnp.zeros((8, LANES), jnp.float32)] * 2
    halves = [terms[2 * h][0] + terms[2 * h + 1][0] for h in range(2)]
    grad = project(proto_raw[...], jnp.concatenate(halves, axis=0).T)
    proto_out[:count, :] = grad
    squares[0] = row_fold(lane_sum(grad * grad))
    for v, raw in enumerate((slow_raw, fast_raw)):
        grad = project(raw[...], terms[4 + 2 * v][0] + terms[5 + 2 * v][0])
        embed_out[v] = grad
        squares[1] = squares[1] + row_fold(lane_sum(grad * grad))
    for kind in range(2):
        total = jnp.sum(jnp.sum(squares[kind], axis=0, keepdims=True), axis=1, keepdims=True)
        proto_out[count:, kind * LANES : (kind + 1) * LANES] = jnp.broadcast_to(total, (EXTRA, LANES))


def project_shares(raws, terms):
    rows, feats = raws[1].shape
    count = raws[0].shape[0]
    return pl.pallas_call(
        share_kernel,
        out_shape=(
            jax.ShapeDtypeStruct((count + EXTRA, feats), jnp.float32),
            jax.ShapeDtypeStruct((2, rows, feats), jnp.float32),
        ),
        in_specs=[vmem_spec()] * (len(raws) + len(terms)),
        out_specs=(vmem_spec(),) * 2,
        compiler_params=params(10),
        name="project_shares",
    )(*raws, *terms)


def tree_sum(terms):
    while len(terms) > 1:
        terms = [terms[i] + terms[i + 1] for i in range(0, len(terms), 2)]
    return terms[0]


def distinct(groups):
    arrays, plan = [], []
    for group in groups:
        places = []
        for array, part in group:
            place = next((i for i, known in enumerate(arrays) if known is array), None)
            if place is None:
                place = len(arrays)
                arrays.append(array)
            places.append((place, part))
        plan.append(places)
    return arrays, plan


def piece_ref(ins, place, part):
    return ins[place] if part is None else ins[place].at[part]


def squares_kernel(plan, rows, *refs):
    ins, out_ref = refs[:-1], refs[-1]
    total = tree_sum([piece_ref(ins, *piece)[rows:, :] for piece in plan])
    for kind in range(2):
        out_ref[kind] = total[:, kind * LANES : (kind + 1) * LANES]


def sum_squares(pieces, rows):
    arrays, plan = distinct([pieces])
    return pl.pallas_call(
        functools.partial(squares_kernel, plan[0], rows),
        out_shape=jax.ShapeDtypeStruct((2, 8, LANES), jnp.float32),
        in_specs=[vmem_spec()] * len(arrays),
        out_specs=vmem_spec(),
        compiler_params=params(8),
        cost_estimate=pl.CostEstimate(flops=8, bytes_accessed=8, transcendentals=0),
        name="sum_squares",
    )(*arrays)


def finish_kernel(entries, plan, count, *refs):
    squares, ins, outs = refs[:count], refs[count:-7], refs[-7:-4]
    scratch, sems = refs[-4:-1], refs[-1]
    total = tree_sum([square[...] for square in squares])
    factors = [lax.rsqrt(total[k, 0:1, 0:1] / entries[k] + NORM_EPS) for k in range(2)]
    copies = []
    for n, pieces in enumerate(plan):
        axis, kind = ("batch", 0) if n == 0 else ("proto", 1)
        size = scratch[n].shape[1]
        for m, piece in enumerate(pieces):
            which = jnp.bitwise_xor(lax.axis_index(axis), m)
            rows = pl.ds(pl.multiple_of(which * size, size), size)
            scratch[n][m] = piece_ref(ins, *piece)[:size, :] * factors[kind]
            sem = sems.at[len(copies)]
            copies.append(pltpu.make_async_copy(scratch[n].at[m], outs[n].at[rows], sem))
            copies[-1].start()
    for copy in copies:
        copy.wait()


def finish(entries, squares, groups, sizes):
    arrays, plan = distinct(groups)
    feats = arrays[0].shape[-1]
    scratch = [
        pltpu.VMEM((len(group), size, feats), jnp.float32) for group, size in zip(groups, sizes)
    ]
    outs = tuple(
        jax.ShapeDtypeStruct((len(group) * size, feats), jnp.float32)
        for group, size in zip(groups, sizes)
    )
    count = sum(len(group) for group in groups)
    return pl.pallas_call(
        functools.partial(finish_kernel, entries, plan, len(squares)),
        out_shape=outs,
        in_specs=[vmem_spec()] * (len(squares) + len(arrays)),
        out_specs=(pl.BlockSpec(memory_space=pltpu.HBM),) * len(outs),
        scratch_shapes=scratch + [pltpu.SemaphoreType.DMA((count,))],
        compiler_params=params(12),
        name="finish",
    )(*squares, *arrays)


def swap(own, axis, mask):
    return lax.ppermute(own, axis, [(i, i ^ mask) for i in range(lax.axis_size(axis))])


def bits_of(axis):
    count = lax.axis_size(axis)
    bits = count.bit_length() - 1
    if count != 1 << bits:
        raise ValueError("axis size")
    return bits


def far_first(own, axis, step, count):
    return [swap(own, axis, m * step) for m in reversed(range(1, count))]


def proto_parts(own):
    return far_first(own, "proto", 1, lax.axis_size("proto")) + [own]


def batch_parts(own, turn):
    pair = own + swap(own, "batch", 1)
    parts = far_first(pair, "batch", 2, lax.axis_size("batch") // 2)
    return parts[turn:] + parts[:turn] + [pair]


def scatter_sums(groups):
    stage, terms = 0, [None] * len(groups)
    state = list(groups)
    while any(term is None for term in terms):
        live = [n for n in range(len(state)) if terms[n] is None]
        recvs = {}
        for n in live:
            axis, order, send, keep = state[n]
            recvs[n] = swap(send, axis, 1 << order[stage])
        going = []
        for n in live:
            axis, order, send, keep = state[n]
            if stage + 1 == len(order):
                terms[n] = (keep, recvs[n])
            else:
                going.append(n)
        if going:
            arrays = [x for n in going for x in (state[n][3], recvs[n])]
            split = split_add(arrays, [(2 * i, 2 * i + 1, None) for i in range(len(going))])
            for n, (send, keep) in zip(going, split):
                state[n] = (state[n][0], state[n][1], send, keep)
        stage += 1
    return [x for term in terms for x in term]


def gather_batch(own):
    bits = list(reversed(range(lax.axis_size("batch").bit_length() - 1)))
    pieces = {0: own}
    first = {bit: swap(own, "batch", 1 << bit) for bit in bits}
    for bit in bits:
        for m in list(pieces):
            pieces[m | 1 << bit] = first[bit] if m == 0 else swap(pieces[m], "batch", 1 << bit)
    return [(pieces[m], None) for m in range(len(pieces))]


def gather_views(own, orders):
    first = {bit: swap(own, "proto", 1 << bit) for bit in sorted(orders[0])}
    groups = []
    for v, order in enumerate(orders):
        pieces = {0: (own, v)}
        for bit in order:
            for m in list(pieces):
                if m == 0:
                    pieces[1 << bit] = (first[bit], v)
                else:
                    array, view = pieces[m]
                    piece = array if view is None else array[view]
                    pieces[m | 1 << bit] = (swap(piece, "proto", 1 << bit), None)
        groups.append([pieces[m] for m in range(len(pieces))])
    return groups


def body(slow_embed, fast_embed, prototypes):
    clip_dev, feat_width = slow_embed.shape
    proto_dev = prototypes.shape[0]
    batch_count = lax.axis_size("batch")
    proto_count = lax.axis_size("proto")
    clips_all = clip_dev * batch_count
    protos_all = proto_dev * proto_count
    proto_entries = float(protos_all * feat_width)
    embed_entries = float(2 * clips_all * feat_width)
    batch_bits, proto_bits = bits_of("batch"), bits_of("proto")
    me_batch, me_proto = lax.axis_index("batch"), lax.axis_index("proto")

    t, col, unit_b, proto_b = scores(slow_embed, fast_embed, prototypes)
    unit_bt = turned(unit_b)
    for iteration in range(ITERS):
        rows, r = row_pass(
            t, batch_parts(col, iteration % 2), protos_all, iteration == 0
        )
        row_parts = proto_parts(rows)
        if iteration == 0:
            prob = prob_columns(row_parts)
        if iteration + 1 < ITERS:
            col = col_pass(t, row_parts, clips_all)

    near = tuple(range(batch_bits - 1))
    batch_orders = (near, tuple(reversed(near)))
    proto_orders = (tuple(range(proto_bits)), tuple(reversed(range(proto_bits))))
    send, g = send_gradients(t, r, unit_bt, prob, row_parts, batch_orders)
    shares = embed_gradients(g, proto_b, proto_orders)
    keep = keep_gradients(g, unit_bt, shares[0], batch_orders)

    proto_rows = proto_dev // batch_count
    clip_rows = clip_dev // proto_count
    raws = [lax.dynamic_slice_in_dim(prototypes, me_batch * proto_rows, proto_rows, 0)]
    for x in (slow_embed, fast_embed):
        raws.append(lax.dynamic_slice_in_dim(x, me_proto * clip_rows, clip_rows, 0))
    recv = swap(send, "batch", 1)
    halves = split_add([keep, recv], [(0, 1, h) for h in range(2)])
    z_groups, proto_groups = [], []
    for h in reversed(range(2)):
        order = tuple(bit + 1 for bit in batch_orders[h])
        z_groups.append(("batch", order) + tuple(halves[h]))
    for v in range(2):
        proto_groups.append(("proto", proto_orders[v], shares[2 * v], shares[2 * v + 1]))
    far_terms = scatter_sums(z_groups)
    terms = far_terms[2:] + far_terms[:2] + scatter_sums(proto_groups)
    grad_proto, grad_embed = project_shares(raws, terms)
    proto_pieces = gather_batch(grad_proto)
    view_pieces = gather_views(grad_embed, (proto_orders[1], proto_orders[0]))
    squares = proto_parts(sum_squares(proto_pieces, proto_rows))
    sizes = (proto_rows, clip_rows, clip_rows)
    groups = [proto_pieces] + view_pieces
    return finish((proto_entries, embed_entries), squares, groups, sizes)


def solution(mesh):
    placed = (P("batch", None), P("batch", None), P("proto", None))
    return jax.shard_map(
        body,
        mesh=mesh,
        in_specs=placed,
        out_specs=(P("proto", None), P("batch", None), P("batch", None)),
        check_vma=False,
    )
```

```python
import functools

import jax
import jax.numpy as jnp
from jax import lax
from jax.experimental import pallas as pl
from jax.experimental.pallas import tpu as pltpu
from jax.sharding import PartitionSpec as P

ITERS = 3


CODE_EPS = 0.05
TEMPER = 0.1
NORM_EPS = 1e-06
LANES = 128
MIB = 1024 * 1024


def vmem_spec():
    return pl.BlockSpec(memory_space=pltpu.VMEM)


def params(limit):
    return pltpu.CompilerParams(vmem_limit_bytes=limit * MIB)


def to_columns(line):
    return jnp.broadcast_to(line, (LANES, LANES)).T


def to_line(partial):
    return jnp.sum(partial.T, axis=0, keepdims=True)


def lane_sum(block):
    total = block[:, :LANES]
    for j in range(1, block.shape[1] // LANES):
        total = total + block[:, j * LANES : (j + 1) * LANES]
    return total


def row_fold(block):
    return jnp.sum(block.reshape(block.shape[0] // 8, 8, block.shape[1]), axis=0)


def sum_of(refs, first=0, size=None):
    size = refs[0].shape[0] if size is None else size
    total = refs[0][first : first + size, :]
    for ref in refs[1:]:
        total = total + ref[first : first + size, :]
    return total


LOG2E = 1.4426950408889634


def score_kernel(slow, fast, protos, e_ref, col_ref, den_ref, ub_ref, cb_ref, raw_s, w_s, ct_s, den_s, sems):
    clips, feats = slow.shape
    count = protos.shape[0]
    loads = []
    for v, src in enumerate((slow, fast)):
        loads.append(pltpu.make_async_copy(src, raw_s.at[v], sems.at[v]))
    loads.append(pltpu.make_async_copy(protos, w_s, sems.at[2]))
    for load in loads:
        load.start()
    for v in range(2):
        loads[v].wait()
        for first in range(0, clips, 256):
            rows = pl.ds(first, 256)
            x = raw_s[v, rows, :].astype(jnp.float32)
            length = jnp.sqrt(jnp.sum(x * x, axis=-1, keepdims=True) + 1e-12)
            ub_ref[v, rows, :] = (x / length).astype(jnp.bfloat16)
    den_s[...] = jnp.zeros_like(den_s)
    loads[2].wait()
    for first in range(0, count, 256):
        w = w_s[first : first + 256, :]
        length = jnp.sqrt(jnp.sum(w * w, axis=-1, keepdims=True) + 1e-12)
        c = w / length
        cb_ref[first : first + 256, :] = c.astype(jnp.bfloat16)
        ct_s[:, first : first + 256] = c.T.astype(jnp.bfloat16)

    def chunk(j, _):
        first = pl.multiple_of(j * 256, 256)
        weights = ct_s[:, pl.ds(first, 256)]
        for v in range(2):
            cols = jnp.zeros((8, 256), jnp.float32)
            for r in range(0, clips, 512):
                s = jnp.dot(
                    ub_ref[v, r : r + 512, :], weights, preferred_element_type=jnp.float32
                )
                for q in range(0, 512, 64):
                    rows = pl.ds(r + q, 64)
                    t = jnp.exp2(s[q : q + 64] * (LOG2E / TEMPER))
                    e = t * t
                    e_ref[v, rows, pl.ds(first, 256)] = e
                    cols = cols + row_fold(e)
                    den_s[v, rows, :] += lane_sum(t)
            line = jnp.sum(cols, axis=0, keepdims=True)
            for h in range(2):
                col_ref[pl.ds(v * (count // LANES) + j * 2 + h, 1), :] = line[
                    :, h * LANES : (h + 1) * LANES
                ]
        return 0

    lax.fori_loop(0, count // 256, chunk, 0)
    groups = clips // LANES
    for v in range(2):
        for i in range(groups):
            den_ref[pl.ds(v * groups + i, 1), :] = to_line(den_s[v, i * LANES : (i + 1) * LANES, :])


def scores(slow, fast, protos):
    clips, feats = slow.shape
    count = protos.shape[0]
    return pl.pallas_call(
        score_kernel,
        out_shape=(
            pltpu.VMEM((2, clips, count), jnp.float32),
            jax.ShapeDtypeStruct((2 * count // LANES, LANES), jnp.float32),
            jax.ShapeDtypeStruct((2 * clips // LANES, LANES), jnp.float32),
            jax.ShapeDtypeStruct((2, clips, feats), jnp.bfloat16),
            jax.ShapeDtypeStruct((count, feats), jnp.bfloat16),
        ),
        in_specs=[pl.BlockSpec(memory_space=pltpu.HBM)] * 3,
        out_specs=(vmem_spec(),) * 5,
        scratch_shapes=[
            pltpu.VMEM((2, clips, feats), jnp.bfloat16),
            pltpu.VMEM((count, feats), jnp.float32),
            pltpu.VMEM((feats, count), jnp.bfloat16),
            pltpu.VMEM((2, clips, LANES), jnp.float32),
            pltpu.SemaphoreType.DMA((3,)),
        ],
        compiler_params=params(24),
        name="scores",
    )(*[pltpu.with_memory_space_constraint(x, pltpu.HBM) for x in (slow, fast, protos)])


def turn_kernel(ub_ref, ubt_ref):
    clips = ub_ref.shape[1]
    for v in range(2):
        for first in range(0, clips, 256):
            u = ub_ref[v, first : first + 256, :].astype(jnp.float32)
            ubt_ref[:, v * clips + first : v * clips + first + 256] = u.T.astype(jnp.bfloat16)


def turned(ub):
    clips, feats = ub.shape[1:]
    return pl.pallas_call(
        turn_kernel,
        out_shape=jax.ShapeDtypeStruct((feats, 2 * clips), ub.dtype),
        in_specs=[vmem_spec()],
        out_specs=vmem_spec(),
        compiler_params=params(8),
        cost_estimate=pl.CostEstimate(
            flops=2 * clips * feats, bytes_accessed=4 * MIB, transcendentals=0
        ),
        name="turned",
    )(ub)


def row_kernel(protos_all, extra, e_ref, den_ref, *refs):
    col_parts, (row_ref, r_ref, acc_s) = refs[:-3], refs[-3:]
    clips, count = e_ref.shape[1:]
    groups, lines = clips // LANES, count // LANES
    r_ref[...] = 1.0 / (float(protos_all) * sum_of(col_parts))
    if extra:
        row_ref[2 * groups :, :] = den_ref[...]
    for v in range(2):

        def step(i, _, v=v):
            rows = pl.ds(pl.multiple_of(i * LANES, LANES), LANES)
            acc = jnp.zeros((LANES, LANES), jnp.float32)
            for j in range(lines):
                e = e_ref[v, rows, j * LANES : (j + 1) * LANES]
                acc = acc + e * r_ref[v * lines + j : v * lines + j + 1, :]
            acc_s[pl.ds(pl.multiple_of((v * groups + i) * LANES, LANES), LANES), :] = acc
            return 0

        lax.fori_loop(0, groups, step, 0)
    for line in range(2 * groups):
        row_ref[line : line + 1, :] = to_line(acc_s[line * LANES : (line + 1) * LANES, :])


def row_pass(e, den, col_parts, protos_all, extra):
    clips, count = e.shape[1:]
    lines = 2 * clips // LANES * (2 if extra else 1)
    return pl.pallas_call(
        functools.partial(row_kernel, protos_all, extra),
        out_shape=(
            jax.ShapeDtypeStruct((lines, LANES), jnp.float32),
            jax.ShapeDtypeStruct((2 * count // LANES, LANES), jnp.float32),
        ),
        in_specs=[vmem_spec()] * (2 + len(col_parts)),
        out_specs=(vmem_spec(),) * 2,
        scratch_shapes=[pltpu.VMEM((2 * clips, LANES), jnp.float32)],
        compiler_params=params(8),
        name="row_pass",
    )(pltpu.with_memory_space_constraint(e, pltpu.VMEM), den, *col_parts)


def col_kernel(clips_all, e_ref, *refs):
    row_parts, (col_ref, acc_s, s_s) = refs[:-3], refs[-3:]
    clips, count = e_ref.shape[1:]
    groups, lines = clips // LANES, count // LANES
    scale = 1.0 / (float(clips_all) * sum_of(row_parts, 0, 2 * groups))
    for line in range(2 * groups):
        s_s[line * LANES : (line + 1) * LANES, :] = to_columns(scale[line : line + 1, :])
    acc_s[...] = jnp.zeros_like(acc_s)
    for v in range(2):

        def step(i, _, v=v):
            rows = pl.ds(pl.multiple_of(i * LANES, LANES), LANES)
            scale = s_s[pl.ds(pl.multiple_of((v * groups + i) * LANES, LANES), LANES), :]
            for j in range(lines):
                span = slice(j * LANES, (j + 1) * LANES)
                acc_s[v, :, span] += row_fold(e_ref[v, rows, span] * scale)
            return 0

        lax.fori_loop(0, groups, step, 0)
        for j in range(lines):
            col_ref[v * lines + j : v * lines + j + 1, :] = jnp.sum(
                acc_s[v, :, j * LANES : (j + 1) * LANES], axis=0, keepdims=True
            )


def col_pass(e, row_parts, clips_all):
    clips, count = e.shape[1:]
    return pl.pallas_call(
        functools.partial(col_kernel, clips_all),
        out_shape=jax.ShapeDtypeStruct((2 * count // LANES, LANES), jnp.float32),
        in_specs=[vmem_spec()] * (1 + len(row_parts)),
        out_specs=vmem_spec(),
        scratch_shapes=[
            pltpu.VMEM((2, 8, count), jnp.float32),
            pltpu.VMEM((2 * clips, LANES), jnp.float32),
        ],
        compiler_params=params(8),
        name="col_pass",
    )(pltpu.with_memory_space_constraint(e, pltpu.VMEM), *row_parts)


def piece_of(position, order):
    steps = len(order)
    return sum(((position >> (steps - 1 - j)) & 1) << bit for j, bit in enumerate(order))


def place_of(piece, order):
    steps = len(order)
    return sum(((piece >> bit) & 1) << (steps - 1 - j) for j, bit in enumerate(order))


def chunk_span(m, width):
    which = jnp.bitwise_xor(lax.axis_index("batch"), m)
    return which, pl.multiple_of(which * width, width)


def proto_grads(ubt, chunk, orders, i, oue_ref):
    dct = jnp.dot(ubt, chunk, preferred_element_type=jnp.float32)
    half = dct.shape[0] // 2
    for h in range(2):
        oue_ref[h, place_of(i, orders[h])] = dct[h * half : (h + 1) * half]


def prob_kernel(*refs):
    den_parts, prob_ref = refs[:-1], refs[-1]
    lines = den_parts[0].shape[0] // 2
    prob = (1.0 / TEMPER) / sum_of(den_parts, lines, lines)
    for line in range(lines):
        prob_ref[line * LANES : (line + 1) * LANES, :] = to_columns(prob[line : line + 1, :])


def prob_columns(den_parts):
    lines = den_parts[0].shape[0] // 2
    return pl.pallas_call(
        prob_kernel,
        out_shape=jax.ShapeDtypeStruct((lines * LANES, LANES), jnp.float32),
        in_specs=[vmem_spec()] * len(den_parts),
        out_specs=vmem_spec(),
        compiler_params=params(8),
        cost_estimate=pl.CostEstimate(
            flops=lines * LANES * LANES, bytes_accessed=2 * MIB, transcendentals=0
        ),
        name="prob_columns",
    )(*den_parts)


def send_kernel(orders, parts, e_ref, r_ref, ubt_ref, prob_s, *refs):
    row_parts = refs[:parts]
    send_ref, g_ref, chunk_s, code_s = refs[parts:]
    clips, count = e_ref.shape[1:]
    groups, lines = clips // LANES, count // LANES
    pieces = 1 << len(orders[0])
    width = count // (2 * pieces)
    code = (1.0 / TEMPER) / sum_of(row_parts, 0, 2 * groups)
    for line in range(2 * groups):
        code_s[line * LANES : (line + 1) * LANES, :] = to_columns(code[line : line + 1, :])

    def score_grads(m, keep_chunk):
        which, first = chunk_span(m, width)
        for i in range(0, clips, 32):
            rows = slice(i, i + 32)
            codes = [code_s[v * clips + i : v * clips + i + 32, :] for v in range(2)]
            probs = [prob_s[v * clips + i : v * clips + i + 32, :] for v in range(2)]
            for h in range(width // LANES):
                span = pl.ds(first + h * LANES, LANES)
                line = which * (width // LANES) + h
                e = [e_ref[v, rows, span] for v in range(2)]
                t = [e[v] * lax.rsqrt(e[v]) for v in range(2)]
                q = [
                    e[v] * r_ref[pl.ds(v * lines + line, 1), :] * codes[v]
                    for v in range(2)
                ]
                for v in range(2):
                    g = (t[v] * probs[v] - q[1 - v]).astype(jnp.bfloat16)
                    own = slice(v * clips + i, v * clips + i + 32)
                    g_ref[own, span] = g
                    if keep_chunk:
                        chunk_s[own, h * LANES : (h + 1) * LANES] = g

    def pair(i, _):
        score_grads(2 * i + 1, True)
        score_grads(2 * i, False)
        proto_grads(ubt_ref[...], chunk_s[...], orders, i, send_ref)
        return 0

    lax.fori_loop(0, pieces, pair, 0)


def send_gradients(e, r, ubt, prob, row_parts, orders):
    clips, count = e.shape[1:]
    feats = ubt.shape[0]
    pieces = 1 << len(orders[0])
    width = count // (2 * pieces)
    return pl.pallas_call(
        functools.partial(send_kernel, orders, len(row_parts)),
        out_shape=(
            jax.ShapeDtypeStruct((2, pieces, feats // 2, width), jnp.float32),
            pltpu.VMEM((2 * clips, count), jnp.bfloat16),
        ),
        in_specs=[vmem_spec()] * (4 + len(row_parts)),
        out_specs=(vmem_spec(),) * 2,
        scratch_shapes=[
            pltpu.VMEM((2 * clips, width), jnp.bfloat16),
            pltpu.VMEM((2 * clips, LANES), jnp.float32),
        ],
        compiler_params=params(14),
        cost_estimate=pl.CostEstimate(
            flops=2 * clips * count * feats, bytes_accessed=20 * MIB, transcendentals=0
        ),
        name="send_gradients",
    )(pltpu.with_memory_space_constraint(e, pltpu.VMEM), r, ubt, prob, *row_parts)


def embed_grad_kernel(orders, g_ref, cb_ref, *outs):
    clips = g_ref.shape[0] // 2
    peers = 1 << len(orders[0])
    size = clips // peers
    for v in range(2):
        for place in range(peers):
            which = jnp.bitwise_xor(lax.axis_index("proto"), piece_of(place, orders[v]))
            rows = pl.ds(pl.multiple_of(v * clips + which * size, size), size)
            out_ref = outs[2 * v + (0 if place >= peers // 2 else 1)]
            out_ref[place % (peers // 2)] = jnp.dot(
                g_ref[rows, :], cb_ref[...], preferred_element_type=jnp.float32
            )


def embed_gradients(g, cb, orders):
    clips, count = g.shape[0] // 2, g.shape[1]
    feats = cb.shape[1]
    peers = 1 << len(orders[0])
    share = jax.ShapeDtypeStruct((peers // 2, clips // peers, feats), jnp.float32)
    return pl.pallas_call(
        functools.partial(embed_grad_kernel, orders),
        out_shape=(share,) * 4,
        in_specs=[vmem_spec()] * 2,
        out_specs=(vmem_spec(),) * 4,
        compiler_params=params(14),
        cost_estimate=pl.CostEstimate(
            flops=4 * clips * count * feats, bytes_accessed=11 * MIB, transcendentals=0
        ),
        name="embed_gradients",
    )(pltpu.with_memory_space_constraint(g, pltpu.VMEM), cb)


def keep_kernel(orders, g_ref, ubt_ref, after_ref, keep_ref):
    pieces = 1 << len(orders[0])
    width = g_ref.shape[1] // (2 * pieces)

    def step(i, _):
        _, first = chunk_span(2 * i, width)
        proto_grads(ubt_ref[...], g_ref[:, pl.ds(first, width)], orders, i, keep_ref)
        return 0

    lax.fori_loop(0, pieces, step, 0)


def keep_gradients(g, ubt, after, orders):
    count = g.shape[1]
    feats, clips = ubt.shape
    pieces = 1 << len(orders[0])
    return pl.pallas_call(
        functools.partial(keep_kernel, orders),
        out_shape=jax.ShapeDtypeStruct((2, pieces, feats // 2, count // (2 * pieces)), jnp.float32),
        in_specs=[vmem_spec()] * 2 + [pl.BlockSpec(memory_space=pl.ANY)],
        out_specs=vmem_spec(),
        compiler_params=params(14),
        cost_estimate=pl.CostEstimate(
            flops=clips * count * feats, bytes_accessed=6 * MIB, transcendentals=0
        ),
        name="keep_gradients",
    )(pltpu.with_memory_space_constraint(g, pltpu.VMEM), ubt, after)


def split_add_kernel(plan, inputs, *refs):
    ins, outs = refs[:inputs], refs[inputs:]
    for n, (keep_place, recv_place, part) in enumerate(plan):
        keep, recv = ins[keep_place], ins[recv_place]
        if part is not None:
            keep, recv = keep.at[part], recv.at[part]
        send_out, keep_out = outs[2 * n : 2 * n + 2]
        half = keep_out.shape[0]
        keep_out[...] = keep[:half] + recv[:half]
        send_out[...] = keep[half:] + recv[half:]


def split_add(arrays, plan):
    halves = []
    for place, _, part in plan:
        shape = arrays[place].shape if part is None else arrays[place].shape[1:]
        halves += [jax.ShapeDtypeStruct((shape[0] // 2,) + shape[1:], jnp.float32)] * 2
    outs = pl.pallas_call(
        functools.partial(split_add_kernel, plan, len(arrays)),
        out_shape=tuple(halves),
        in_specs=[vmem_spec()] * len(arrays),
        out_specs=(vmem_spec(),) * len(halves),
        compiler_params=params(12),
        name="split_add",
    )(*arrays)
    return [(outs[2 * n], outs[2 * n + 1]) for n in range(len(plan))]


def project(raw, grad):
    x = raw.astype(jnp.float32)
    length = jnp.sqrt(jnp.sum(x * x, axis=-1, keepdims=True) + 1e-12)
    unit = x / length
    along = jnp.sum(unit * grad, axis=-1, keepdims=True)
    return (grad - unit * along) / length


EXTRA = 8


def share_kernel(proto_raw, slow_raw, fast_raw, *refs):
    terms, (proto_out, embed_out) = refs[:-2], refs[-2:]
    count = proto_raw.shape[0]
    squares = [jnp.zeros((8, LANES), jnp.float32)] * 2
    halves = [terms[2 * h][0] + terms[2 * h + 1][0] for h in range(2)]
    grad = project(proto_raw[...], jnp.concatenate(halves, axis=0).T)
    proto_out[:count, :] = grad
    squares[0] = row_fold(lane_sum(grad * grad))
    for v, raw in enumerate((slow_raw, fast_raw)):
        grad = project(raw[...], terms[4 + 2 * v][0] + terms[5 + 2 * v][0])
        embed_out[v] = grad
        squares[1] = squares[1] + row_fold(lane_sum(grad * grad))
    for kind in range(2):
        total = jnp.sum(jnp.sum(squares[kind], axis=0, keepdims=True), axis=1, keepdims=True)
        proto_out[count:, kind * LANES : (kind + 1) * LANES] = jnp.broadcast_to(total, (EXTRA, LANES))


def project_shares(raws, terms):
    rows, feats = raws[1].shape
    count = raws[0].shape[0]
    return pl.pallas_call(
        share_kernel,
        out_shape=(
            jax.ShapeDtypeStruct((count + EXTRA, feats), jnp.float32),
            jax.ShapeDtypeStruct((2, rows, feats), jnp.float32),
        ),
        in_specs=[vmem_spec()] * (len(raws) + len(terms)),
        out_specs=(vmem_spec(),) * 2,
        compiler_params=params(10),
        name="project_shares",
    )(*raws, *terms)


def tree_sum(terms):
    while len(terms) > 1:
        terms = [terms[i] + terms[i + 1] for i in range(0, len(terms), 2)]
    return terms[0]


def distinct(groups):
    arrays, plan = [], []
    for group in groups:
        places = []
        for array, part in group:
            place = next((i for i, known in enumerate(arrays) if known is array), None)
            if place is None:
                place = len(arrays)
                arrays.append(array)
            places.append((place, part))
        plan.append(places)
    return arrays, plan


def piece_ref(ins, place, part):
    return ins[place] if part is None else ins[place].at[part]


def squares_kernel(plan, rows, *refs):
    ins, out_ref = refs[:-1], refs[-1]
    total = tree_sum([piece_ref(ins, *piece)[rows:, :] for piece in plan])
    for kind in range(2):
        out_ref[kind] = total[:, kind * LANES : (kind + 1) * LANES]


def sum_squares(pieces, rows):
    arrays, plan = distinct([pieces])
    return pl.pallas_call(
        functools.partial(squares_kernel, plan[0], rows),
        out_shape=jax.ShapeDtypeStruct((2, 8, LANES), jnp.float32),
        in_specs=[vmem_spec()] * len(arrays),
        out_specs=vmem_spec(),
        compiler_params=params(8),
        cost_estimate=pl.CostEstimate(flops=8, bytes_accessed=8, transcendentals=0),
        name="sum_squares",
    )(*arrays)


def finish_kernel(entries, plan, count, *refs):
    squares, ins, outs = refs[:count], refs[count:-7], refs[-7:-4]
    scratch, sems = refs[-4:-1], refs[-1]
    total = tree_sum([square[...] for square in squares])
    factors = [lax.rsqrt(total[k, 0:1, 0:1] / entries[k] + NORM_EPS) for k in range(2)]
    copies = []
    for n, pieces in enumerate(plan):
        axis, kind = ("batch", 0) if n == 0 else ("proto", 1)
        size = scratch[n].shape[1]
        for m, piece in enumerate(pieces):
            which = jnp.bitwise_xor(lax.axis_index(axis), m)
            rows = pl.ds(pl.multiple_of(which * size, size), size)
            scratch[n][m] = piece_ref(ins, *piece)[:size, :] * factors[kind]
            sem = sems.at[len(copies)]
            copies.append(pltpu.make_async_copy(scratch[n].at[m], outs[n].at[rows], sem))
            copies[-1].start()
    for copy in copies:
        copy.wait()


def finish(entries, squares, groups, sizes):
    arrays, plan = distinct(groups)
    feats = arrays[0].shape[-1]
    scratch = [
        pltpu.VMEM((len(group), size, feats), jnp.float32) for group, size in zip(groups, sizes)
    ]
    outs = tuple(
        jax.ShapeDtypeStruct((len(group) * size, feats), jnp.float32)
        for group, size in zip(groups, sizes)
    )
    count = sum(len(group) for group in groups)
    return pl.pallas_call(
        functools.partial(finish_kernel, entries, plan, len(squares)),
        out_shape=outs,
        in_specs=[vmem_spec()] * (len(squares) + len(arrays)),
        out_specs=(pl.BlockSpec(memory_space=pltpu.HBM),) * len(outs),
        scratch_shapes=scratch + [pltpu.SemaphoreType.DMA((count,))],
        compiler_params=params(12),
        name="finish",
    )(*squares, *arrays)


def swap(own, axis, mask):
    return lax.ppermute(own, axis, [(i, i ^ mask) for i in range(lax.axis_size(axis))])


def bits_of(axis):
    count = lax.axis_size(axis)
    bits = count.bit_length() - 1
    if count != 1 << bits:
        raise ValueError("axis size")
    return bits


def far_first(own, axis, step, count):
    return [swap(own, axis, m * step) for m in reversed(range(1, count))]


def proto_parts(own):
    return far_first(own, "proto", 1, lax.axis_size("proto")) + [own]


def batch_parts(own, turn):
    pair = own + swap(own, "batch", 1)
    parts = far_first(pair, "batch", 2, lax.axis_size("batch") // 2)
    return parts[turn:] + parts[:turn] + [pair]


def scatter_sums(groups):
    stage, terms = 0, [None] * len(groups)
    state = list(groups)
    while any(term is None for term in terms):
        live = [n for n in range(len(state)) if terms[n] is None]
        recvs = {}
        for n in live:
            axis, order, send, keep = state[n]
            recvs[n] = swap(send, axis, 1 << order[stage])
        going = []
        for n in live:
            axis, order, send, keep = state[n]
            if stage + 1 == len(order):
                terms[n] = (keep, recvs[n])
            else:
                going.append(n)
        if going:
            arrays = [x for n in going for x in (state[n][3], recvs[n])]
            split = split_add(arrays, [(2 * i, 2 * i + 1, None) for i in range(len(going))])
            for n, (send, keep) in zip(going, split):
                state[n] = (state[n][0], state[n][1], send, keep)
        stage += 1
    return [x for term in terms for x in term]


def gather_batch(own):
    bits = list(reversed(range(lax.axis_size("batch").bit_length() - 1)))
    pieces = {0: own}
    first = {bit: swap(own, "batch", 1 << bit) for bit in bits}
    for bit in bits:
        for m in list(pieces):
            pieces[m | 1 << bit] = first[bit] if m == 0 else swap(pieces[m], "batch", 1 << bit)
    return [(pieces[m], None) for m in range(len(pieces))]


def gather_views(own, orders):
    first = {bit: swap(own, "proto", 1 << bit) for bit in sorted(orders[0])}
    groups = []
    for v, order in enumerate(orders):
        pieces = {0: (own, v)}
        for bit in order:
            for m in list(pieces):
                if m == 0:
                    pieces[1 << bit] = (first[bit], v)
                else:
                    array, view = pieces[m]
                    piece = array if view is None else array[view]
                    pieces[m | 1 << bit] = (swap(piece, "proto", 1 << bit), None)
        groups.append([pieces[m] for m in range(len(pieces))])
    return groups


def body(slow_embed, fast_embed, prototypes):
    clip_dev, feat_width = slow_embed.shape
    proto_dev = prototypes.shape[0]
    batch_count = lax.axis_size("batch")
    proto_count = lax.axis_size("proto")
    clips_all = clip_dev * batch_count
    protos_all = proto_dev * proto_count
    proto_entries = float(protos_all * feat_width)
    embed_entries = float(2 * clips_all * feat_width)
    batch_bits, proto_bits = bits_of("batch"), bits_of("proto")
    me_batch, me_proto = lax.axis_index("batch"), lax.axis_index("proto")

    e, col, den, unit_b, proto_b = scores(slow_embed, fast_embed, prototypes)
    unit_bt = turned(unit_b)
    for iteration in range(ITERS):
        rows, r = row_pass(e, den, batch_parts(col, iteration % 2), protos_all, iteration == 0)
        row_parts = proto_parts(rows)
        if iteration == 0:
            prob = prob_columns(row_parts)
        if iteration + 1 < ITERS:
            col = col_pass(e, row_parts, clips_all)

    near = tuple(range(batch_bits - 1))
    batch_orders = (near, tuple(reversed(near)))
    proto_orders = (tuple(range(proto_bits)), tuple(reversed(range(proto_bits))))
    send, g = send_gradients(e, r, unit_bt, prob, row_parts, batch_orders)
    shares = embed_gradients(g, proto_b, proto_orders)
    keep = keep_gradients(g, unit_bt, shares[0], batch_orders)

    proto_rows = proto_dev // batch_count
    clip_rows = clip_dev // proto_count
    raws = [lax.dynamic_slice_in_dim(prototypes, me_batch * proto_rows, proto_rows, 0)]
    for x in (slow_embed, fast_embed):
        raws.append(lax.dynamic_slice_in_dim(x, me_proto * clip_rows, clip_rows, 0))
    recv = swap(send, "batch", 1)
    halves = split_add([keep, recv], [(0, 1, h) for h in range(2)])
    z_groups, proto_groups = [], []
    for h in reversed(range(2)):
        order = tuple(bit + 1 for bit in batch_orders[h])
        z_groups.append(("batch", order) + tuple(halves[h]))
    for v in range(2):
        proto_groups.append(("proto", proto_orders[v], shares[2 * v], shares[2 * v + 1]))
    far_terms = scatter_sums(z_groups)
    terms = far_terms[2:] + far_terms[:2] + scatter_sums(proto_groups)
    grad_proto, grad_embed = project_shares(raws, terms)
    proto_pieces = gather_batch(grad_proto)
    view_pieces = gather_views(grad_embed, (proto_orders[1], proto_orders[0]))
    squares = proto_parts(sum_squares(proto_pieces, proto_rows))
    sizes = (proto_rows, clip_rows, clip_rows)
    groups = [proto_pieces] + view_pieces
    return finish((proto_entries, embed_entries), squares, groups, sizes)


def solution(mesh):
    placed = (P("batch", None), P("batch", None), P("proto", None))
    return jax.shard_map(
        body,
        mesh=mesh,
        in_specs=placed,
        out_specs=(P("proto", None), P("batch", None), P("batch", None)),
        check_vma=False,
    )
```
